32 devices in a mesh: dp: 4 (over x, core), tensor: 8 (over z, y).
Axes of the slice: x: 2, y: 2, z: 4, core: 2. Of those that a mesh axis runs over, the one named last changes fastest.
Arguments:
- tokens: bfloat16 [8192, 2048], P(('dp', 'tensor')), may hold values from -6 to 6
- segments: int32 [8192], P('dp'), may hold values from 0 to 8, as said below
- attn_gain: float32 [2048], replicated, may hold values from 0.1 to 1.9
- ffn_gain: float32 [2048], replicated, may hold values from 0.1 to 1.9
- w_query: bfloat16 [2048, 2048], P(None, 'tensor'), may hold values from -0.1875 to 0.1875
- w_key: bfloat16 [2048, 2048], P(None, 'tensor'), may hold values from -0.1875 to 0.1875
- w_value: bfloat16 [2048, 2048], P(None, 'tensor'), may hold values from -0.125 to 0.125
- w_out: bfloat16 [2048, 2048], P('tensor'), may hold values from -0.75 to 0.75
- w_gate: bfloat16 [2048, 5504], P(None, 'tensor'), may hold values from -0.125 to 0.125
- w_up: bfloat16 [2048, 5504], P(None, 'tensor'), may hold values from -0.125 to 0.125
- w_down: bfloat16 [5504, 2048], P('tensor'), may hold values from -0.15625 to 0.15625
- cotangent: bfloat16 [8192, 2048], P(('dp', 'tensor')), may hold values from -6 to 6
Outputs:
- output: bfloat16 [8192, 2048], P(('dp', 'tensor'))
- input_grad: bfloat16 [8192, 2048], P(('dp', 'tensor'))
- grad_attn_gain: float32 [2048], replicated
- grad_ffn_gain: float32 [2048], replicated
- grad_w_query: float32 [2048, 2048], P(None, 'tensor')
- grad_w_key: float32 [2048, 2048], P(None, 'tensor')
- grad_w_value: float32 [2048, 2048], P(None, 'tensor')
- grad_w_out: float32 [2048, 2048], P('tensor')
- grad_w_gate: float32 [2048, 5504], P(None, 'tensor')
- grad_w_up: float32 [2048, 5504], P(None, 'tensor')
- grad_w_down: float32 [5504, 2048], P('tensor')
- doc_rms: float32 [3, 9], replicated
The draws below stay inside these ranges and needn't reach their ends.
Inputs may be any that keep to these rules, and one draw needn't show every extreme that they name: segments never fall, start at 0 and rise by one at each document start; each block of 2048 tokens holds exactly two document starts, the first at one of its tokens 2048 // 8 to 767, the second at one of its tokens 3 * 256 to 1791; in some block other than the last the second start lies at its token 1024 or earlier.
All inputs are finite; a program needn't handle non-finite values.
Results may differ from the reference program's by a relative error of at most 0.025.
Values may be sent and summed in bfloat16 or wider, within the bound.
No kernel may reach another device: no remote copies, remote signals or barrier semaphores. Data moves between devices by JAX's collectives and lax.ppermute only.
A program may use at most 192 MiB of HBM per device.

```python
import math
import jax
import jax.numpy as jnp
from jax import lax

D = 2048
HEADS = 16
HEAD_DIM = 128
FF = 5504
WINDOW = 1024
TOK_DEV = 2048
TOKENS = 8192
SEGS = 9


def draw_segments(key, part):
    key = jax.random.fold_in(key, 11)
    block_num = TOKENS // TOK_DEV
    key_first, key_second, key_long = jax.random.split(key, 3)
    long_block = jax.random.randint(key_long, (), 0, block_num - 1)
    block_ids = jnp.arange(block_num, dtype=jnp.int32)
    second_high = jnp.where(block_ids == long_block, TOK_DEV - WINDOW + 1, 7 * TOK_DEV // 8).astype(jnp.int32)
    first_cut = jax.random.randint(key_first, (block_num,), TOK_DEV // 8, 3 * TOK_DEV // 8)
    second_cut = jax.random.randint(key_second, (block_num,), 3 * TOK_DEV // 8, second_high)
    offsets = jnp.arange(TOK_DEV, dtype=jnp.int32)
    cut_marks = (offsets[None, :] == first_cut[:, None]).astype(jnp.int32)
    cut_marks = cut_marks + (offsets[None, :] == second_cut[:, None]).astype(jnp.int32)
    return jnp.cumsum(cut_marks.reshape(-1)).astype(jnp.int32)


def steps_of(own_key, extent, cuts, smallest, largest):
    def one(position, parts):
        heights = jax.random.uniform(jax.random.fold_in(jax.random.fold_in(own_key, 6), position), (parts,), jnp.float32, smallest / len(cuts), largest / len(cuts))
        return jnp.repeat(jnp.exp(heights), extent[position] // parts).reshape((-1,) + (1,) * (len(extent) - position - 1))

    factor_of = one(*cuts[0])
    for cut in cuts[1:]:
        factor_of = factor_of * one(*cut)
    return factor_of


def normal_values(own_key, dims, width, reach, shards=(), kind=jnp.bfloat16):
    array = jax.random.normal(own_key, dims, jnp.float32) * width
    if len(shards) > 0:
        array = steps_of(own_key, dims, shards, -0.22, 0.18) * array
    return jnp.clip(array, min=-reach, max=reach).astype(kind)


def setup_inputs(seed: int = 0) -> dict:
    streams_of = jax.random.split(jax.random.key(seed), 13)
    tokens = normal_values(streams_of[0], (TOKENS, D), 1.0, 6.0, ((0, 32),))
    segments = draw_segments(jax.random.fold_in(streams_of[12], 71), 0)
    attn_gain = jnp.clip(1.0 + 0.18 * jax.random.normal(streams_of[2], (D,), jnp.float32), 0.1, 1.9)
    ffn_gain = jnp.clip(1.0 + 0.18 * jax.random.normal(streams_of[3], (D,), jnp.float32), 0.1, 1.9)
    w_query = normal_values(streams_of[4], (D, HEADS * HEAD_DIM), (D // 2) ** -0.5, 0.1875, ((1, 8),))
    w_key = normal_values(streams_of[5], (D, HEADS * HEAD_DIM), (D // 2) ** -0.5, 0.1875, ((1, 8),))
    w_value = normal_values(streams_of[6], (D, HEADS * HEAD_DIM), D ** -0.5, 0.125, ((1, 8),))
    w_out = normal_values(streams_of[7], (HEADS * HEAD_DIM, D), (D // 32) ** -0.5, 0.75, ((0, 8),))
    w_gate = normal_values(streams_of[8], (D, FF), D ** -0.5, 0.125, ((1, 8),))
    w_up = normal_values(streams_of[9], (D, FF), D ** -0.5, 0.125, ((1, 8),))
    w_down = normal_values(streams_of[10], (FF, D), (FF // 4) ** -0.5, 0.15625, ((0, 8),))
    cotangent = normal_values(streams_of[11], (TOKENS, D), 1.0, 6.0, ((0, 32),))
    return {"tokens": tokens, "segments": segments, "attn_gain": attn_gain, "ffn_gain": ffn_gain, "w_query": w_query, "w_key": w_key, "w_value": w_value, "w_out": w_out, "w_gate": w_gate, "w_up": w_up, "w_down": w_down, "cotangent": cotangent}


@jax.custom_vjp
def low(v):
    return lax.optimization_barrier(v.astype(jnp.bfloat16)).astype(jnp.float32)

@jax.custom_vjp
def low_back(v):
    return v

def low_keep(v):
    return (low(v), None)

def low_pass(kept, grad):
    return (grad,)

def back_keep(v):
    return (v, None)

def back_low(kept, grad):
    return (low(grad),)
low.defvjp(low_keep, low_pass)
low_back.defvjp(back_keep, back_low)
eps_norm = 1e-06
neg_large = -1e+30

def matmul_high(left, right):
    return jnp.dot(left, right, precision=lax.Precision.HIGHEST, preferred_element_type=jnp.float32)

def rms_norm(values, gain_vec):
    inverse = lax.rsqrt(lax.optimization_barrier(jnp.mean(values * values, axis=-1, keepdims=True)) + eps_norm)
    return values * inverse * gain_vec

def rope_tables(positions, head_dim):
    half_dim = head_dim // 2
    frequency = jnp.exp(jnp.arange(half_dim, dtype=jnp.float32) * (-2.0 * math.log(10000.0) / head_dim))
    angles = positions.astype(jnp.float32)[:, None] * frequency[None, :]
    return (jnp.cos(angles), jnp.sin(angles))

def rotate(values, cos_table, sin_table, head_dim):
    row_num = values.shape[0]
    split_heads = values.reshape(row_num, -1, head_dim)
    half_dim = head_dim // 2
    first_half = split_heads[..., :half_dim]
    second_half = split_heads[..., half_dim:]
    cos_part = cos_table[:, None, :]
    sin_part = sin_table[:, None, :]
    joined = jnp.concatenate([first_half * cos_part - second_half * sin_part, second_half * cos_part + first_half * sin_part], axis=-1)
    return joined.reshape(row_num, -1)

def reference(tokens, segments, attn_gain, ffn_gain, w_query, w_key, w_value, w_out, w_gate, w_up, w_down, cotangent):
    total_len = tokens.shape[0]
    query_len = min(512, TOK_DEV)
    key_span = query_len + WINDOW
    head_cols = HEADS * HEAD_DIM
    scale_qk = HEAD_DIM ** (-0.5)
    positions = jnp.arange(total_len, dtype=jnp.int32)
    cos_table, sin_table = rope_tables(positions, HEAD_DIM)
    seg_all = jnp.concatenate([jnp.zeros((WINDOW,), jnp.int32), segments.astype(jnp.int32)])
    pos_all = jnp.arange(total_len + WINDOW, dtype=jnp.int32) - WINDOW

    def forward(input_f, gain_a, gain_f, weight_q, weight_k, weight_v, weight_o, weight_g, weight_u, weight_d):
        x_normed = low(rms_norm(input_f, gain_a))
        query = low_back(matmul_high(x_normed, weight_q))
        key_pre = low_back(matmul_high(x_normed, weight_k))
        value_low = low(low_back(matmul_high(x_normed, weight_v)))
        query_rot = low(rotate(query, cos_table, sin_table, HEAD_DIM))
        key_rot = low(rotate(key_pre, cos_table, sin_table, HEAD_DIM))
        pad_zero = jnp.zeros((WINDOW, head_cols), jnp.float32)
        key_all = jnp.concatenate([pad_zero, key_rot], axis=0)
        value_all = jnp.concatenate([pad_zero, value_low], axis=0)

        def attend(block_id):
            row_start = block_id * query_len
            query_blk = lax.dynamic_slice_in_dim(query_rot, row_start, query_len).reshape(query_len, HEADS, HEAD_DIM)
            key_blk = lax.dynamic_slice_in_dim(key_all, row_start, key_span).reshape(key_span, HEADS, HEAD_DIM)
            value_blk = lax.dynamic_slice_in_dim(value_all, row_start, key_span).reshape(key_span, HEADS, HEAD_DIM)
            query_seg = lax.dynamic_slice_in_dim(segments.astype(jnp.int32), row_start, query_len)
            query_pos = row_start + jnp.arange(query_len, dtype=jnp.int32)
            key_seg = lax.dynamic_slice_in_dim(seg_all, row_start, key_span)
            key_pos = lax.dynamic_slice_in_dim(pos_all, row_start, key_span)
            distance = query_pos[:, None] - key_pos[None, :]
            allowed = (query_seg[:, None] == key_seg[None, :]) & (distance >= 0) & (distance < WINDOW) & (key_pos[None, :] >= 0)
            raw_scores = low_back(jnp.einsum('qhd,khd->hqk', query_blk, key_blk, precision=lax.Precision.HIGHEST) * scale_qk)
            scores = jnp.where(allowed[None], raw_scores, neg_large)
            row_max = lax.optimization_barrier(jnp.max(scores, axis=-1, keepdims=True))
            exp_terms = jnp.exp(scores - row_max)
            row_total = lax.optimization_barrier(jnp.sum(exp_terms, axis=-1, keepdims=True))
            weights_low = low(exp_terms / row_total)
            head_mix = jnp.einsum('hqk,khd->qhd', weights_low, value_blk, precision=lax.Precision.HIGHEST)
            return head_mix.reshape(query_len, head_cols)
        attn_heads = lax.map(jax.checkpoint(attend), jnp.arange(total_len // query_len, dtype=jnp.int32))
        attn_heads = low(low_back(attn_heads.reshape(total_len, head_cols)))
        attn_branch = low_back(matmul_high(attn_heads, weight_o))
        mid_stream = input_f + attn_branch
        h_normed = low(rms_norm(mid_stream, gain_f))
        gate_pre = low_back(matmul_high(h_normed, weight_g))
        up_pre = low_back(matmul_high(h_normed, weight_u))
        hidden = low(jax.nn.silu(gate_pre) * up_pre)
        ffn_branch = low_back(matmul_high(hidden, weight_d))
        result = mid_stream + ffn_branch
        return (result, (attn_branch, ffn_branch))
    primals = (tokens.astype(jnp.float32), attn_gain.astype(jnp.float32), ffn_gain.astype(jnp.float32), w_query.astype(jnp.float32), w_key.astype(jnp.float32), w_value.astype(jnp.float32), w_out.astype(jnp.float32), w_gate.astype(jnp.float32), w_up.astype(jnp.float32), w_down.astype(jnp.float32))
    result, back_fn, branches = jax.vjp(forward, *primals, has_aux=True)
    grads = back_fn(cotangent.astype(jnp.float32))
    attn_branch, ffn_branch = branches
    per_row = jnp.stack([lax.optimization_barrier(jnp.sum(result * result, axis=1)), lax.optimization_barrier(jnp.sum(attn_branch * attn_branch, axis=1)), lax.optimization_barrier(jnp.sum(ffn_branch * ffn_branch, axis=1))], axis=1)
    one_hot = (segments.astype(jnp.int32)[:, None] == jnp.arange(SEGS, dtype=jnp.int32)[None, :]).astype(jnp.float32)
    doc_table = jnp.dot(per_row.T, one_hot, precision=lax.Precision.HIGHEST, preferred_element_type=jnp.float32)
    doc_count = lax.optimization_barrier(jnp.sum(one_hot, axis=0))
    doc_rms = jnp.sqrt(doc_table / (jnp.maximum(doc_count, 1.0) * D))
    return (result.astype(jnp.bfloat16), grads[0].astype(jnp.bfloat16), grads[1], grads[2], grads[3], grads[4], grads[5], grads[6], grads[7], grads[8], grads[9], doc_rms)
```

```python
import functools
import math

import jax
import jax.numpy as jnp
from jax import lax
from jax.experimental import pallas as pl
from jax.experimental.pallas import tpu as pltpu
from jax.sharding import PartitionSpec as P

HEAD_DIM = 128
WINDOW = 1024
EPS = 1e-06
NEG = -1e30
F32 = jnp.float32
BF16 = jnp.bfloat16
Q_BLK = 256
GROUP = 4


def ring_cycle(count):
    if count == 8:
        return [0, 2, 4, 6, 7, 5, 3, 1]
    width = 4 if count % 4 == 0 else count
    order = []
    for row in range(count // width):
        part = list(range(row * width, (row + 1) * width))
        order += part if row % 2 == 0 else part[::-1]
    return order


def group_cycles(count):
    base = [0, 2, 3, 1] if count == 8 else list(range(GROUP))
    return [[g * GROUP + b for b in base] for g in range(count // GROUP)]


def step_pairs(cycles, step):
    return [
        (cyc[i], cyc[(i + step) % len(cyc)]) for cyc in cycles for i in range(len(cyc))
    ]


def owner_of(cycles, rel):
    table = {}
    for cyc in cycles:
        for i, dev in enumerate(cyc):
            table[dev] = cyc[(i + rel) % len(cyc)]
    rows = jnp.array([table[t] for t in range(len(table))], jnp.int32)
    return rows[lax.axis_index("tensor")]


def rel_order(size):
    order = [0]
    for k in range(1, size // 2):
        order += [-k, k]
    return order + [size // 2]


def ring_gather(own, cycles):
    size = len(cycles[0])
    ahead, back = step_pairs(cycles, 1), step_pairs(cycles, -1)
    chunks = {0: own}
    f = b = own
    for k in range(1, size // 2):
        f = lax.ppermute(f, "tensor", ahead)
        b = lax.ppermute(b, "tensor", back)
        chunks[-k], chunks[k] = f, b
    half = own.shape[0] // 2
    f = lax.ppermute(f[:half], "tensor", ahead)
    b = lax.ppermute(b[half:], "tensor", back)
    chunks[size // 2] = jnp.concatenate([f, b], axis=0)
    return chunks


def ring_scatter(partial, cycles):
    size = len(cycles[0])
    ahead, back = step_pairs(cycles, 1), step_pairs(cycles, -1)
    far = partial(size // 2).astype(BF16)
    half = far.shape[0] // 2
    f = lax.ppermute(far[:half], "tensor", ahead)
    b = lax.ppermute(far[half:], "tensor", back)
    first = True
    for k in range(size // 2 - 1, 0, -1):
        pf, pb = partial(k), partial(-k)
        if first:
            pf = jnp.concatenate([pf[:half] + f.astype(F32), pf[half:]], axis=0)
            pb = jnp.concatenate([pb[:half], pb[half:] + b.astype(F32)], axis=0)
            first = False
        else:
            pf = pf + f.astype(F32)
            pb = pb + b.astype(F32)
        f = lax.ppermute(pf.astype(BF16), "tensor", ahead)
        b = lax.ppermute(pb.astype(BF16), "tensor", back)
    return partial(0) + f.astype(F32) + b.astype(F32)


def bits_of(count):
    bit, out = 1, []
    while bit < count:
        out.append(bit)
        bit *= 2
    return out


def swap(value, axis, bit):
    count = lax.axis_size(axis)
    return lax.ppermute(value, axis, [(d, d ^ bit) for d in range(count)])


def halves_scatter(value, axis):
    me = lax.axis_index("dp")
    for bit in bits_of(lax.axis_size("dp")):
        half = value.shape[axis] // 2
        side = (me // bit) % 2
        keep = lax.dynamic_slice_in_dim(value, side * half, half, axis)
        send = lax.dynamic_slice_in_dim(value, (1 - side) * half, half, axis)
        got = swap(send, "dp", bit)
        value = (keep.astype(F32) + got.astype(F32)).astype(BF16)
    return value


def halves_gather(value, axis):
    me = lax.axis_index("dp")
    for bit in reversed(bits_of(lax.axis_size("dp"))):
        other = swap(value, "dp", bit)
        side = (me // bit) % 2
        low = jnp.where(side == 0, value, other)
        high = jnp.where(side == 0, other, value)
        value = jnp.concatenate([low, high], axis=axis)
    return value


def own_part(value, axis):
    me = lax.axis_index("dp")
    for bit in bits_of(lax.axis_size("dp")):
        half = value.shape[axis] // 2
        value = lax.dynamic_slice_in_dim(value, ((me // bit) % 2) * half, half, axis)
    return value


def sum_all(value):
    for axis in ("dp", "tensor"):
        for bit in bits_of(lax.axis_size(axis)):
            value = value + swap(value, axis, bit)
    return value


def shifted(value, axis, steps):
    count = lax.axis_size(axis)
    leading, last = max(0, -steps), min(count, count - steps)
    return lax.ppermute(value, axis, [(s, s + steps) for s in range(leading, last)])


def norm_forward(values, gain):
    inverse = lax.rsqrt(jnp.mean(values * values, axis=-1, keepdims=True) + EPS)
    unit = values * inverse
    return unit * gain, unit, inverse


def norm_backward(grad, unit, inverse, gain):
    scaled = grad * gain
    inner = jnp.mean(scaled * unit, axis=-1, keepdims=True)
    return inverse * (scaled - unit * inner)


def dot_nn(a, b):
    return jnp.dot(a, b, preferred_element_type=F32)


def dot_tn(a, b):
    return lax.dot_general(a, b, (((0,), (0,)), ((), ())), preferred_element_type=F32)


def dot_nt(a, b):
    return lax.dot_general(a, b, (((1,), (1,)), ((), ())), preferred_element_type=F32)


def rope_tables(positions):
    half = HEAD_DIM // 2
    freq = jnp.exp(jnp.arange(half, dtype=F32) * (-2.0 * math.log(10000.0) / HEAD_DIM))
    angles = positions.astype(F32)[:, None] * freq[None, :]
    cos, sin = jnp.cos(angles), jnp.sin(angles)
    return jnp.concatenate([cos, cos], axis=1), jnp.concatenate([-sin, sin], axis=1)


def params(*sem):
    return pltpu.CompilerParams(
        dimension_semantics=sem or None, vmem_limit_bytes=56 * 1024 * 1024
    )


def qkv_body(idx, x_ref, wq, wk, wv, cos_ref, sin_ref, *rest):
    q_out, k_out, v_out, x_out = rest[-4:]
    x = x_ref[...]
    cos, sin = cos_ref[...], sin_ref[...]
    for w, out in ((wq, q_out), (wk, k_out)):
        p = dot_nn(x, w[...])
        for h in range(p.shape[1] // HEAD_DIM):
            cols = slice(h * HEAD_DIM, (h + 1) * HEAD_DIM)
            seg = p[:, cols]
            out[:, cols] = (seg * cos + pltpu.roll(seg, HEAD_DIM // 2, 1) * sin).astype(BF16)
    v_out[...] = dot_nn(x, wv[...]).astype(BF16)
    x_out[...] = x


def qkv_chunk(place, x, wq, wk, wv, cos, sin, bufs):
    rows, feats = x.shape
    cols = wq.shape[1]
    total = cos.shape[0]
    full = lambda shape: pl.BlockSpec(shape, lambda i, idx: (0, 0))
    at = lambda width: pl.BlockSpec((rows, width), lambda i, idx: (idx[0], 0))
    in_specs = [
        full((rows, feats)),
        full((feats, cols)),
        full((feats, cols)),
        full((feats, cols)),
        at(HEAD_DIM),
        at(HEAD_DIM),
    ]
    out_shape = [jax.ShapeDtypeStruct((total, cols), BF16)] * 3 + [
        jax.ShapeDtypeStruct((total, feats), BF16)
    ]
    args = [place.reshape(1), x, wq, wk, wv, cos, sin]
    aliases = {}
    if bufs is not None:
        in_specs += [pl.BlockSpec(memory_space=pl.ANY)] * 4
        args += list(bufs)
        aliases = {7 + i: i for i in range(4)}
    return pl.pallas_call(
        qkv_body,
        grid_spec=pltpu.PrefetchScalarGridSpec(
            num_scalar_prefetch=1,
            grid=(1,),
            in_specs=in_specs,
            out_specs=[at(cols)] * 3 + [at(feats)],
        ),
        out_shape=out_shape,
        input_output_aliases=aliases,
        compiler_params=params("arbitrary"),
        cost_estimate=pl.CostEstimate(
            flops=2 * rows * feats * cols * 3,
            bytes_accessed=2 * (feats * cols * 3 + rows * (2 * feats + 3 * cols)),
            transcendentals=0,
        ),
        name="qkv_chunk",
    )(*args)


LOG2E = 1.4426950408889634
SCALE = HEAD_DIM ** (-0.5)


def attend_body(q_ref, k0, k1, v0, v1, lo_ref, *rest):
    o_ref, ks, vs = rest[-3:]
    i = pl.program_id(1)
    span = Q_BLK + WINDOW

    @pl.when(i == 0)
    def _():
        ks[:WINDOW] = k0[...]
        ks[WINDOW:] = k1[...]
        vs[:WINDOW] = v0[...]
        vs[WINDOW:] = v1[...]

    start = pl.multiple_of(i * Q_BLK, Q_BLK)
    kb = ks[pl.ds(start, span), :]
    vb = vs[pl.ds(start, span), :]
    s = dot_nt(q_ref[...], kb) * (SCALE * LOG2E)
    col = lax.broadcasted_iota(jnp.int32, s.shape, 1)
    row = lax.broadcasted_iota(jnp.int32, s.shape, 0)
    lo = lo_ref[...] - start
    s = jnp.where((col >= lo) & (col <= row + WINDOW), s, NEG)
    p = jnp.exp2(s - jnp.max(s, axis=1, keepdims=True))
    total = jnp.sum(p, axis=1, keepdims=True)
    o = dot_nn(p.astype(BF16), vb) * (1.0 / total)
    o_ref[...] = o.astype(BF16)


def attend(half, q, k_pair, v_pair, lo, buf):
    total, cols = q.shape
    heads = cols // HEAD_DIM
    rows = total // 2
    blocks = rows // Q_BLK
    base = half * blocks
    q_spec = pl.BlockSpec((Q_BLK, HEAD_DIM), lambda h, i: (base + i, h))
    key_spec = lambda b: pl.BlockSpec((WINDOW, HEAD_DIM), lambda h, i: (b, h))
    lo_spec = pl.BlockSpec((Q_BLK, 1), lambda h, i: (base + i, 0))
    in_specs = [
        q_spec,
        key_spec(k_pair[0][1]),
        key_spec(k_pair[1][1]),
        key_spec(v_pair[0][1]),
        key_spec(v_pair[1][1]),
        lo_spec,
    ]
    args = [q, k_pair[0][0], k_pair[1][0], v_pair[0][0], v_pair[1][0], lo]
    aliases = {}
    if buf is not None:
        in_specs.append(pl.BlockSpec(memory_space=pl.ANY))
        args.append(buf)
        aliases = {6: 0}
    return pl.pallas_call(
        attend_body,
        grid=(heads, blocks),
        in_specs=in_specs,
        out_specs=q_spec,
        out_shape=jax.ShapeDtypeStruct((total, cols), BF16),
        scratch_shapes=[pltpu.VMEM((2 * WINDOW, HEAD_DIM), BF16)] * 2,
        input_output_aliases=aliases,
        compiler_params=params("arbitrary", "arbitrary"),
        cost_estimate=pl.CostEstimate(
            flops=4 * rows * (Q_BLK + WINDOW) * cols,
            bytes_accessed=2 * cols * 6 * WINDOW,
            transcendentals=rows * (Q_BLK + WINDOW) * heads,
        ),
        name="attend",
    )(*args)


def attend_back_body(q_ref, g_ref, k0, k1, v0, v1, lo_ref, cos_ref, sin_ref, *rest):
    dq_ref, dk_ref, dv_ref, ks, vs = rest[-5:]
    i = pl.program_id(1)
    span = Q_BLK + WINDOW

    @pl.when(i == 0)
    def _():
        ks[:WINDOW] = k0[...]
        ks[WINDOW:] = k1[...]
        vs[:WINDOW] = v0[...]
        vs[WINDOW:] = v1[...]
        dk_ref[...] = jnp.zeros_like(dk_ref)
        dv_ref[...] = jnp.zeros_like(dv_ref)

    start = pl.multiple_of(i * Q_BLK, Q_BLK)
    kb = ks[pl.ds(start, span), :]
    vb = vs[pl.ds(start, span), :]
    q, g = q_ref[...], g_ref[...]
    s = dot_nt(kb, q) * (SCALE * LOG2E)
    key = lax.broadcasted_iota(jnp.int32, s.shape, 0)
    row = lax.broadcasted_iota(jnp.int32, s.shape, 1)
    lo = lo_ref[...] - start
    s = jnp.where((key >= lo) & (key <= row + WINDOW), s, NEG)
    p = jnp.exp2(s - jnp.max(s, axis=0, keepdims=True))
    p = p * (1.0 / jnp.sum(p, axis=0, keepdims=True))
    dp = dot_nt(vb, g)
    inner = jnp.sum(p * dp, axis=0, keepdims=True)
    ds = (p * (dp - inner)).astype(BF16)
    dq = dot_tn(ds, kb) * SCALE
    dq = dq * cos_ref[...] - pltpu.roll(dq, HEAD_DIM // 2, 1) * sin_ref[...]
    dq_ref[...] = dq.astype(BF16)
    dk_ref[pl.ds(start, span), :] += dot_nn(ds, q) * SCALE
    dv_ref[pl.ds(start, span), :] += dot_nn(p.astype(BF16), g)


def attend_back(half, q, g, k_pair, v_pair, lo_row, cos, sin, buf):
    total, cols = q.shape
    heads = cols // HEAD_DIM
    rows = total // 2
    blocks = rows // Q_BLK
    base = half * blocks
    q_spec = pl.BlockSpec((Q_BLK, HEAD_DIM), lambda h, i: (base + i, h))
    key_spec = lambda b: pl.BlockSpec((WINDOW, HEAD_DIM), lambda h, i: (b, h))
    rope_spec = pl.BlockSpec((Q_BLK, HEAD_DIM), lambda h, i: (base + i, 0))
    lo_spec = pl.BlockSpec((1, Q_BLK), lambda h, i: (0, base + i))
    grad_spec = pl.BlockSpec((2 * WINDOW, HEAD_DIM), lambda h, i: (0, h))
    in_specs = [
        q_spec,
        q_spec,
        key_spec(k_pair[0][1]),
        key_spec(k_pair[1][1]),
        key_spec(v_pair[0][1]),
        key_spec(v_pair[1][1]),
        lo_spec,
        rope_spec,
        rope_spec,
    ]
    args = [q, g, k_pair[0][0], k_pair[1][0], v_pair[0][0], v_pair[1][0], lo_row, cos, sin]
    aliases = {}
    if buf is not None:
        in_specs.append(pl.BlockSpec(memory_space=pl.ANY))
        args.append(buf)
        aliases = {9: 0}
    return pl.pallas_call(
        attend_back_body,
        grid=(heads, blocks),
        in_specs=in_specs,
        out_specs=[
            pl.BlockSpec((Q_BLK, HEAD_DIM), lambda h, i: (base + i, 2 * heads + h)),
            grad_spec,
            grad_spec,
        ],
        out_shape=[
            jax.ShapeDtypeStruct((total, 3 * cols), BF16),
            jax.ShapeDtypeStruct((2 * WINDOW, cols), F32),
            jax.ShapeDtypeStruct((2 * WINDOW, cols), F32),
        ],
        scratch_shapes=[pltpu.VMEM((2 * WINDOW, HEAD_DIM), BF16)] * 2,
        input_output_aliases=aliases,
        compiler_params=params("arbitrary", "arbitrary"),
        cost_estimate=pl.CostEstimate(
            flops=10 * rows * (Q_BLK + WINDOW) * cols,
            bytes_accessed=2 * cols * 14 * WINDOW,
            transcendentals=rows * (Q_BLK + WINDOW) * heads,
        ),
        name="attend_back",
    )(*args)


def finish_body(half, ak, av, ok, ov, cos_ref, sin_ref, _, out_ref):
    cols = ak.shape[1]

    def write(gk, gv):
        for h in range(cols // HEAD_DIM):
            c = slice(h * HEAD_DIM, (h + 1) * HEAD_DIM)
            seg = gk[:, c]
            seg = seg * cos_ref[...] - pltpu.roll(seg, HEAD_DIM // 2, 1) * sin_ref[...]
            out_ref[:, c] = seg.astype(BF16)
        out_ref[:, cols:] = gv.astype(BF16)

    write(ak[...] + ok[...].astype(F32), av[...] + ov[...].astype(F32))


def finish_keys(half, ak, av, ok, ov, other_base, cos, sin, buf):
    cols = ak.shape[1]
    blk = 512
    n = WINDOW // blk
    base = half * n
    own = pl.BlockSpec((blk, cols), lambda i: (base + i, 0))
    oth = pl.BlockSpec((blk, cols), lambda i: (other_base * n + i, 0))
    rope = pl.BlockSpec((blk, HEAD_DIM), lambda i: (base + i, 0))
    return pl.pallas_call(
        functools.partial(finish_body, half),
        grid=(n,),
        in_specs=[own, own, oth, oth, rope, rope, pl.BlockSpec(memory_space=pl.ANY)],
        out_specs=pl.BlockSpec((blk, 2 * cols), lambda i: (base + i, 0)),
        out_shape=jax.ShapeDtypeStruct(buf.shape, BF16),
        input_output_aliases={6: 0},
        compiler_params=params("arbitrary"),
        name="finish_keys",
    )(ak, av, ok, ov, cos, sin, buf)


def shards(
    tokens, segments, attn_gain, ffn_gain, w_query, w_key, w_value, w_out, w_gate, w_up, w_down, cotangent
):
    rows, feats = tokens.shape
    n_tensor = lax.axis_size("tensor")
    n_dp = lax.axis_size("dp")
    block_len = rows * n_tensor
    head_cols = w_query.shape[1]
    dp_idx, t_idx = lax.axis_index("dp"), lax.axis_index("tensor")
    first_pos = dp_idx * block_len
    ring = [ring_cycle(n_tensor)]
    square = group_cycles(n_tensor)
    groups = n_tensor // GROUP

    x_f = tokens.astype(F32)
    x_normed, x_unit, x_inv = norm_forward(x_f, attn_gain)
    x_chunks = ring_gather(x_normed.astype(BF16), ring)

    cos, sin = rope_tables(first_pos + jnp.arange(block_len, dtype=jnp.int32))
    bufs = None
    for rel in rel_order(n_tensor):
        bufs = qkv_chunk(
            owner_of(ring, rel), x_chunks[rel], w_query, w_key, w_value, cos, sin, bufs
        )
    query, key, value, x_all = bufs

    prev_seg = shifted(segments[block_len - WINDOW :].astype(F32), "dp", 1).astype(jnp.int32)
    seg_all = jnp.concatenate([prev_seg, segments], axis=0)
    low_key = jnp.sum((seg_all[None, :] < segments[:, None]).astype(jnp.int32), axis=1)
    low_key = jnp.where(dp_idx == 0, jnp.maximum(low_key, WINDOW), low_key)
    spot = jnp.arange(block_len, dtype=jnp.int32)
    low_key = jnp.maximum(low_key, spot + 1)
    low_key = low_key - jnp.where(spot >= block_len // 2, block_len // 2, 0)
    low_col, low_row = low_key[:, None], low_key[None, :]

    tail = block_len - WINDOW
    prev_k = shifted(key[tail:], "dp", 1)
    prev_v = shifted(value[tail:], "dp", 1)
    k_late, v_late = ((key, 0), (key, 1)), ((value, 0), (value, 1))
    k_early, v_early = ((prev_k, 0), (key, 0)), ((prev_v, 0), (value, 0))
    heads_low = attend(1, query, k_late, v_late, low_col, None)
    heads_low = attend(0, query, k_early, v_early, low_col, heads_low)

    part = own_part(w_out, 0)
    out_chunks = ring_gather(part, ring)
    w_out_all = jnp.zeros((n_tensor,) + part.shape, BF16)
    for rel in rel_order(n_tensor):
        w_out_all = lax.dynamic_update_slice(
            w_out_all, out_chunks[rel][None], (owner_of(ring, rel), 0, 0)
        )
    w_out_all = halves_gather(w_out_all, 1).reshape(-1, feats)
    my_heads = lax.all_to_all(heads_low, "tensor", split_axis=0, concat_axis=1, tiled=True)
    attn_branch = dot_nn(my_heads, w_out_all)
    mid = x_f + attn_branch
    h_normed, h_unit, h_inv = norm_forward(mid, ffn_gain)

    def spread(value, axis):
        piece = own_part(value, axis)
        out = [value]
        for s in range(1, groups):
            pairs = [((t + s * GROUP) % n_tensor, t) for t in range(n_tensor)]
            out.append(halves_gather(lax.ppermute(piece, "tensor", pairs), axis))
        return out

    wg, wu, wd = spread(w_gate, 0), spread(w_up, 0), spread(w_down, 1)

    h_chunks = ring_gather(h_normed.astype(BF16), square)
    y_chunks = ring_gather(cotangent, square)
    hidden, g_gate, g_up = {}, {}, {}
    for rel in rel_order(GROUP):
        h, dy = h_chunks[rel], y_chunks[rel]
        hid, gg, gu = [], [], []
        for s in range(groups):
            gate, up = dot_nn(h, wg[s]), dot_nn(h, wu[s])
            gh = dot_nt(dy, wd[s])
            sig = jax.nn.sigmoid(gate)
            hid.append((gate * sig * up).astype(BF16))
            gg.append((gh * up * sig * (1.0 + gate * (1.0 - sig))).astype(BF16))
            gu.append((gh * gate * sig).astype(BF16))
        hidden[rel], g_gate[rel], g_up[rel] = hid, gg, gu

    def grad_h_part(rel):
        total = 0.0
        for s in range(groups):
            total = total + dot_nt(g_gate[rel][s], wg[s]) + dot_nt(g_up[rel][s], wu[s])
        return total

    def ffn_part(rel):
        total = 0.0
        for s in range(groups):
            total = total + dot_nn(hidden[rel][s], wd[s])
        return total

    grad_h = ring_scatter(grad_h_part, square)
    grad_mid = cotangent.astype(F32) + norm_backward(grad_h, h_unit, h_inv, ffn_gain)
    grad_ffn_gain = jnp.sum(grad_h * h_unit, axis=0)
    grad_mid_low = grad_mid.astype(BF16)
    my_grad_heads = dot_nt(grad_mid_low, w_out_all).astype(BF16)
    grad_heads = lax.all_to_all(my_grad_heads, "tensor", split_axis=1, concat_axis=0, tiled=True)

    d_joint, bk, bv = attend_back(
        0, query, grad_heads, k_early, v_early, low_row, cos, sin, None
    )
    got_k = shifted(bk[:WINDOW].astype(BF16), "dp", -1)
    got_v = shifted(bv[:WINDOW].astype(BF16), "dp", -1)
    d_joint, ak, av = attend_back(
        1, query, grad_heads, k_late, v_late, low_row, cos, sin, d_joint
    )
    d_joint = finish_keys(0, ak, av, bk, bv, 1, cos, sin, d_joint)
    d_joint = finish_keys(1, ak, av, got_k, got_v, 0, cos, sin, d_joint)
    w_joint = jnp.concatenate([w_key, w_value, w_query], axis=1)

    def grad_x_part(rel):
        mine = lax.dynamic_slice_in_dim(d_joint, owner_of(ring, rel) * rows, rows)
        return dot_nt(mine, w_joint)

    grad_x = ring_scatter(grad_x_part, ring)
    input_grad = (grad_mid + norm_backward(grad_x, x_unit, x_inv, attn_gain)).astype(BF16)

    ffn_branch = ring_scatter(ffn_part, square)
    result = mid + ffn_branch

    order = rel_order(GROUP)
    h_cat = jnp.concatenate([h_chunks[r] for r in order], axis=0)
    y_cat = jnp.concatenate([y_chunks[r] for r in order], axis=0)

    def reduce_ffn(parts, axis):
        own = None
        for s in range(groups):
            piece = halves_scatter(parts[s], axis)
            if s == 0:
                own = piece.astype(F32)
            else:
                pairs = [(t, (t + s * GROUP) % n_tensor) for t in range(n_tensor)]
                own = own + lax.ppermute(piece, "tensor", pairs).astype(F32)
        return halves_gather(own.astype(BF16), axis).astype(F32)

    def cat(parts, s):
        return jnp.concatenate([parts[r][s] for r in order], axis=0)

    grad_w_down = reduce_ffn(
        [dot_tn(cat(hidden, s), y_cat).astype(BF16) for s in range(groups)], 1
    )
    grad_w_gate = reduce_ffn(
        [dot_tn(h_cat, cat(g_gate, s)).astype(BF16) for s in range(groups)], 0
    )
    grad_w_up = reduce_ffn(
        [dot_tn(h_cat, cat(g_up, s)).astype(BF16) for s in range(groups)], 0
    )

    out_parts = dot_tn(my_heads, grad_mid_low).astype(BF16).reshape(n_tensor, head_cols, feats)
    out_parts = halves_scatter(out_parts, 1)

    def out_part(rel):
        return lax.dynamic_index_in_dim(
            out_parts, owner_of(ring, rel), 0, keepdims=False
        ).astype(F32)

    grad_w_out = halves_gather(ring_scatter(out_part, ring).astype(BF16), 0).astype(F32)

    joint_local = dot_tn(x_all, d_joint)
    grad_attn_gain = jnp.sum(joint_local * w_joint.astype(F32), axis=1) / attn_gain
    grad_joint = halves_gather(halves_scatter(joint_local.astype(BF16), 0), 0).astype(F32)

    slots = 2 * n_dp + 1
    own_seg = lax.dynamic_slice_in_dim(segments, t_idx * rows, rows)
    one_hot = (own_seg[:, None] == jnp.arange(slots, dtype=jnp.int32)[None, :]).astype(F32)
    per_row = jnp.stack(
        [
            jnp.sum(result * result, axis=1),
            jnp.sum(attn_branch * attn_branch, axis=1),
            jnp.sum(ffn_branch * ffn_branch, axis=1),
            jnp.ones((rows,), F32),
        ],
        axis=1,
    )
    table = jnp.dot(per_row.T, one_hot, precision=lax.Precision.HIGHEST, preferred_element_type=F32)
    packed = jnp.concatenate([grad_attn_gain, grad_ffn_gain, table.reshape(-1)])
    packed = jnp.pad(packed, (0, -packed.shape[0] % 1024)).reshape(-1, 128)
    packed = sum_all(packed).reshape(-1)
    sums = packed[2 * feats : 2 * feats + 4 * slots].reshape(4, slots)
    doc_rms = jnp.sqrt(sums[:3] / (jnp.maximum(sums[3:], 1.0) * feats))

    return (
        result.astype(BF16),
        input_grad,
        packed[:feats],
        packed[feats : 2 * feats],
        grad_joint[:, 2 * head_cols :],
        grad_joint[:, :head_cols],
        grad_joint[:, head_cols : 2 * head_cols],
        grad_w_out,
        grad_w_gate,
        grad_w_up,
        grad_w_down,
        doc_rms,
    )


def solution(mesh):
    both = P(("dp", "tensor"), None)
    col, row = P(None, "tensor"), P("tensor", None)
    return jax.shard_map(
        shards,
        mesh=mesh,
        in_specs=(both, P("dp"), P(), P(), col, col, col, row, col, col, row, both),
        out_specs=(both, both, P(), P(), col, col, col, row, col, col, row, P()),
        check_vma=False,
    )
```

```python
import functools
import math

import jax
import jax.numpy as jnp
from jax import lax
from jax.experimental import pallas as pl
from jax.experimental.pallas import tpu as pltpu
from jax.sharding import PartitionSpec as P

HEAD_DIM = 128
WINDOW = 1024
EPS = 1e-06
NEG = -1e30
F32 = jnp.float32
BF16 = jnp.bfloat16
Q_BLK = 256
COST_PART = 16
GROUP = 4


def ring_cycle(count):
    if count == 8:
        return [0, 2, 4, 6, 7, 5, 3, 1]
    width = 4 if count % 4 == 0 else count
    order = []
    for row in range(count // width):
        part = list(range(row * width, (row + 1) * width))
        order += part if row % 2 == 0 else part[::-1]
    return order


def group_cycles(count):
    base = [0, 2, 3, 1] if count == 8 else list(range(GROUP))
    return [[g * GROUP + b for b in base] for g in range(count // GROUP)]


def step_pairs(cycles, step):
    return [
        (cyc[i], cyc[(i + step) % len(cyc)]) for cyc in cycles for i in range(len(cyc))
    ]


def owners(cycles):
    table = {}
    for cyc in cycles:
        for i, dev in enumerate(cyc):
            table[dev] = [cyc[(i + rel) % len(cyc)] for rel in range(len(cyc))]
    rows = jnp.array([table[t] for t in range(len(table))], jnp.int32)
    return rows[lax.axis_index("tensor")]


def rel_order(size):
    order = [0]
    for k in range(1, size // 2):
        order += [-k, k]
    return order + [size // 2]


def after(value, *deps):
    return lax.optimization_barrier((value,) + deps)[0]


def together(*values):
    return lax.optimization_barrier(values)


class Gather:
    def __init__(self, own, cycles):
        self.size = len(cycles[0])
        self.ahead, self.back = step_pairs(cycles, 1), step_pairs(cycles, -1)
        self.f = self.b = own
        self.chunks = {0: [own]}
        self.k = 0

    def step(self, *deps):
        self.k += 1
        f, b = lax.optimization_barrier((self.f, self.b) + deps)[:2]
        if self.k < self.size // 2:
            self.f = lax.ppermute(f, "tensor", self.ahead)
            self.b = lax.ppermute(b, "tensor", self.back)
            self.chunks[-self.k], self.chunks[self.k] = [self.f], [self.b]
        else:
            half = self.f.shape[0] // 2
            self.f = lax.ppermute(f[:half], "tensor", self.ahead)
            self.b = lax.ppermute(b[half:], "tensor", self.back)
            self.chunks[self.k] = [self.f, self.b]

    def all(self):
        while self.k < self.size // 2:
            self.step()
        return self.chunks


class Scatter:
    def __init__(self, far, cycles):
        self.size = len(cycles[0])
        self.ahead, self.back = step_pairs(cycles, 1), step_pairs(cycles, -1)
        self.k = self.size // 2
        half = far.shape[0] // 2
        self.sent = lax.optimization_barrier((far[:half], far[half:]))
        self.send()

    def send(self):
        self.f = lax.ppermute(self.sent[0], "tensor", self.ahead)
        self.b = lax.ppermute(self.sent[1], "tensor", self.back)

    def step(self, near, first, *deps):
        f, b, near = lax.optimization_barrier((self.f, self.b, near) + deps)[:3]
        self.k -= 1
        self.sent = ring_add(near, f, b, first)
        self.send()


def bits_of(count):
    bit, out = 1, []
    while bit < count:
        out.append(bit)
        bit *= 2
    return out


def swap(value, axis, bit):
    count = lax.axis_size(axis)
    return lax.ppermute(value, axis, [(d, d ^ bit) for d in range(count)])


class Halves:
    def __init__(self, send, keep, axis):
        self.sent, self.keep, self.axis = send, keep, axis
        self.bits = bits_of(lax.axis_size("dp"))

    def send(self, *deps):
        self.sent = after(self.sent, *deps)
        self.got = swap(self.sent, "dp", self.bits[0])

    def add(self, *deps):
        got = after(self.got, *deps)
        self.bits = self.bits[1:]
        if self.bits:
            pair = half_add(self.keep, got, self.axis, dp_side(self.bits[0]))
            self.sent, self.keep = pair
            return self.keep
        self.value = plain_add(self.keep, got)
        return self.value

    def finish(self, *deps):
        self.add(*deps)
        while self.bits:
            self.send()
            self.add()
        return self.value


def dp_side(bit):
    side = (lax.axis_index("dp") // bit) % 2
    return jnp.stack([1 - side, side]).astype(jnp.int32)


def place_of(device, count):
    place = 0
    for bit in bits_of(count):
        place = place * 2 + (device // bit) % 2
    return place


def part_of(place, count):
    device = 0
    for bit in bits_of(count):
        device = device * 2 + place % 2
        place = place // 2
    return device


def all_dp(value):
    return lax.all_gather(value, "dp", axis=0, tiled=False)


def spread_parts(out, bits, *deps):
    for bit in bits:
        out = out + [(x ^ bit, swap(after(v, *deps), "dp", bit)) for x, v in out]
    return out


def sum_all(value):
    for axis in ("tensor", "dp"):
        for bit in bits_of(lax.axis_size(axis)):
            value = value + swap(value, axis, bit)
    return value


def shifted(value, axis, steps):
    count = lax.axis_size(axis)
    leading, last = max(0, -steps), min(count, count - steps)
    return lax.ppermute(value, axis, [(s, s + steps) for s in range(leading, last)])


def norm_forward(values, gain):
    inverse = lax.rsqrt(jnp.mean(values * values, axis=-1, keepdims=True) + EPS)
    unit = values * inverse
    return unit * gain, unit, inverse


def norm_backward(grad, unit, inverse, gain):
    scaled = grad * gain
    inner = jnp.mean(scaled * unit, axis=-1, keepdims=True)
    return inverse * (scaled - unit * inner)


def dot_nn(a, b):
    return jnp.dot(a, b, preferred_element_type=F32)


def dot_tn(a, b):
    return lax.dot_general(a, b, (((0,), (0,)), ((), ())), preferred_element_type=F32)


def dot_nt(a, b):
    return lax.dot_general(a, b, (((1,), (1,)), ((), ())), preferred_element_type=F32)


def rope_tables(positions):
    half = HEAD_DIM // 2
    freq = jnp.exp(jnp.arange(half, dtype=F32) * (-2.0 * math.log(10000.0) / HEAD_DIM))
    angles = positions.astype(F32)[:, None] * freq[None, :]
    cos, sin = jnp.cos(angles), jnp.sin(angles)
    return jnp.concatenate([cos, cos], axis=1), jnp.concatenate([-sin, sin], axis=1)


def cost(flops, bytes_accessed, transcendentals):
    return pl.CostEstimate(
        flops=flops // COST_PART,
        bytes_accessed=bytes_accessed // COST_PART,
        transcendentals=transcendentals // COST_PART,
    )


def params(*sem):
    return pltpu.CompilerParams(
        dimension_semantics=sem or None, vmem_limit_bytes=56 * 1024 * 1024
    )


ANY = pl.BlockSpec(memory_space=pl.ANY)


def qkv_body(n_in, idx, *refs):
    xs, refs = refs[:n_in], refs[n_in:]
    wq, wk, wv, cos_ref, sin_ref = refs[:5]
    q_out, kv_out, x_out = refs[-3:]
    at = 0
    for x in xs:
        x_out[at : at + x.shape[0], :] = x[...]
        at += x.shape[0]
    x = x_out[...]
    cos, sin = cos_ref[...], sin_ref[...]
    cols = wq.shape[1]
    for w, out in ((wq, q_out), (wk, kv_out)):
        p = dot_nn(x, w[...])
        for h in range(cols // HEAD_DIM):
            c = slice(h * HEAD_DIM, (h + 1) * HEAD_DIM)
            seg = p[:, c]
            out[:, c] = (seg * cos + pltpu.roll(seg, HEAD_DIM // 2, 1) * sin).astype(BF16)
    kv_out[:, cols:] = dot_nn(x, wv[...]).astype(BF16)


def qkv_chunk(places, rel, xs, wq, wk, wv, cos, sin, bufs):
    rows = sum(x.shape[0] for x in xs)
    feats, cols = wq.shape
    total = cos.shape[0]
    n_in = len(xs)
    full = lambda a: pl.BlockSpec(a.shape, lambda i, idx: (0, 0))
    at = lambda width: pl.BlockSpec((rows, width), lambda i, idx: (idx[rel], 0))
    args = list(xs) + [wq, wk, wv, cos, sin]
    in_specs = [full(a) for a in args[:-2]] + [at(HEAD_DIM)] * 2
    aliases = {}
    if bufs is not None:
        aliases = {1 + len(args) + i: i for i in range(3)}
        in_specs += [ANY] * 3
        args += list(bufs)
    widths = (cols, 2 * cols, feats)
    return pl.pallas_call(
        functools.partial(qkv_body, n_in),
        grid_spec=pltpu.PrefetchScalarGridSpec(
            num_scalar_prefetch=1,
            grid=(1,),
            in_specs=in_specs,
            out_specs=[at(w) for w in widths],
        ),
        out_shape=[jax.ShapeDtypeStruct((total, w), BF16) for w in widths],
        input_output_aliases=aliases,
        compiler_params=params("arbitrary"),
        cost_estimate=cost(
            flops=2 * rows * feats * cols * 3,
            bytes_accessed=2 * (feats * cols * 3 + rows * (2 * feats + 3 * cols)),
            transcendentals=0,
        ),
        name="qkv_chunk",
    )(places, *args)


def place_body(rels, idx, *refs):
    at = 0
    for rel, src in zip(rels, refs):
        rows = src.shape[0]
        refs[-1][idx[rel], at : at + rows, :] = src[...]
        at = (at + rows) % refs[-1].shape[1]


def place_chunks(places, chunks, count):
    rels = [rel % count for rel in rel_order(count) for _ in chunks[rel]]
    pieces = [c for rel in rel_order(count) for c in chunks[rel]]
    shape = (count,) + pieces[0].shape
    return pl.pallas_call(
        functools.partial(place_body, rels),
        grid_spec=pltpu.PrefetchScalarGridSpec(
            num_scalar_prefetch=1,
            grid=(1,),
            in_specs=[pl.BlockSpec(c.shape, lambda i, idx: (0, 0)) for c in pieces],
            out_specs=pl.BlockSpec(shape, lambda i, idx: (0, 0, 0)),
        ),
        out_shape=jax.ShapeDtypeStruct(shape, BF16),
        compiler_params=params("arbitrary"),
        name="place_chunks",
    )(places, *pieces)


def tn_cols_body(n, idx, a, b, send, keep):
    j = pl.program_id(0)
    out = dot_tn(a[...], b[...]).astype(BF16)

    @pl.when(j < n)
    def _():
        send[...] = out

    @pl.when(j >= n)
    def _():
        keep[...] = out


def half_place(n):
    return lambda j, idx: jnp.where(j < n, idx[0] * n + j, idx[1] * n + j - n)


def tn_cols(a, b):
    k, m = a.shape
    cols = b.shape[1]
    n = 2
    w = cols // (2 * n)
    at = half_place(n)
    return pl.pallas_call(
        functools.partial(tn_cols_body, n),
        grid_spec=pltpu.PrefetchScalarGridSpec(
            num_scalar_prefetch=1,
            grid=(2 * n,),
            in_specs=[
                pl.BlockSpec((k, m), lambda j, idx: (0, 0)),
                pl.BlockSpec((k, w), lambda j, idx: (0, at(j, idx))),
            ],
            out_specs=[
                pl.BlockSpec((m, w), lambda j, idx: (0, jnp.minimum(j, n - 1))),
                pl.BlockSpec((m, w), lambda j, idx: (0, jnp.maximum(j - n, 0))),
            ],
        ),
        out_shape=[jax.ShapeDtypeStruct((m, cols // 2), BF16)] * 2,
        compiler_params=params("arbitrary"),
        cost_estimate=cost(
            flops=2 * k * m * cols, bytes_accessed=2 * (k * m + k * cols + m * cols), transcendentals=0
        ),
        name="tn_cols",
    )(dp_side(1), a, b)


def tn_rows_body(n, idx, a, b, w, send, keep, sums):
    j = pl.program_id(0)
    out = dot_tn(a[...], b[...])
    sums[...] = jnp.sum(out * w[...].astype(F32), axis=1, keepdims=True)

    @pl.when(j < n)
    def _():
        send[...] = out.astype(BF16)

    @pl.when(j >= n)
    def _():
        keep[...] = out.astype(BF16)


def tn_rows(a, b, w):
    k, m = a.shape
    cols = b.shape[1]
    n = 2
    blk = m // (2 * n)
    at = half_place(n)
    return pl.pallas_call(
        functools.partial(tn_rows_body, n),
        grid_spec=pltpu.PrefetchScalarGridSpec(
            num_scalar_prefetch=1,
            grid=(2 * n,),
            in_specs=[
                pl.BlockSpec((k, blk), lambda j, idx: (0, at(j, idx))),
                pl.BlockSpec((k, cols), lambda j, idx: (0, 0)),
                pl.BlockSpec((blk, cols), lambda j, idx: (at(j, idx), 0)),
            ],
            out_specs=[
                pl.BlockSpec((blk, cols), lambda j, idx: (jnp.minimum(j, n - 1), 0)),
                pl.BlockSpec((blk, cols), lambda j, idx: (jnp.maximum(j - n, 0), 0)),
                pl.BlockSpec((blk, 1), lambda j, idx: (at(j, idx), 0)),
            ],
        ),
        out_shape=[jax.ShapeDtypeStruct((m // 2, cols), BF16)] * 2
        + [jax.ShapeDtypeStruct((m, 1), F32)],
        compiler_params=params("arbitrary"),
        cost_estimate=cost(
            flops=2 * k * m * cols, bytes_accessed=2 * (k * m + k * cols + m * cols), transcendentals=0
        ),
        name="tn_rows",
    )(dp_side(1), a, b, w)


def half_add_body(idx, keep, got, send_out, keep_out):
    j = pl.program_id(0)
    out = (keep[...].astype(F32) + got[...].astype(F32)).astype(BF16)

    @pl.when(j == 0)
    def _():
        send_out[...] = out

    @pl.when(j == 1)
    def _():
        keep_out[...] = out


def half_add(keep, got, axis, side):
    shape = list(keep.shape)
    shape[axis] //= 2
    place = lambda j, idx: (0, idx[j]) if axis == 1 else (idx[j], 0)
    one = pl.BlockSpec(tuple(shape), lambda j, idx: (0, 0))
    src = pl.BlockSpec(tuple(shape), place)
    return pl.pallas_call(
        half_add_body,
        grid_spec=pltpu.PrefetchScalarGridSpec(
            num_scalar_prefetch=1, grid=(2,), in_specs=[src, src], out_specs=[one, one]
        ),
        out_shape=[jax.ShapeDtypeStruct(tuple(shape), BF16)] * 2,
        compiler_params=params("arbitrary"),
        cost_estimate=cost(flops=keep.size, bytes_accessed=6 * keep.size, transcendentals=0),
        name="half_add",
    )(side, keep, got)


def plain_add_body(a, b, out):
    out[...] = (a[...].astype(F32) + b[...].astype(F32)).astype(BF16)


def plain_add(a, b):
    rows, cols = a.shape
    blk = pl.BlockSpec((rows // 2, cols), lambda j: (j, 0))
    return pl.pallas_call(
        plain_add_body,
        grid=(2,),
        in_specs=[blk, blk],
        out_specs=blk,
        out_shape=jax.ShapeDtypeStruct(a.shape, BF16),
        compiler_params=params("arbitrary"),
        cost_estimate=cost(flops=a.size, bytes_accessed=6 * a.size, transcendentals=0),
        name="plain_add",
    )(a, b)


def ring_add_body(first, near, f, b, f_out, b_out):
    rows = f_out.shape[0]
    at = 0 if first else rows
    ahead, behind = near[at : at + rows, :].astype(F32), near[rows - at : 2 * rows - at, :].astype(F32)
    n = f.shape[0]
    f_out[:n, :] = (ahead[:n] + f[...].astype(F32)).astype(BF16)
    b_out[rows - n :, :] = (behind[rows - n :] + b[...].astype(F32)).astype(BF16)
    if n < rows:
        f_out[n:, :] = ahead[n:].astype(BF16)
        b_out[: rows - n, :] = behind[: rows - n].astype(BF16)


def ring_add(near, f, b, first):
    rows, cols = near.shape[0] // 2, near.shape[1]
    whole = lambda a: pl.BlockSpec(a.shape, lambda i: (0, 0))
    return pl.pallas_call(
        functools.partial(ring_add_body, first),
        grid=(1,),
        in_specs=[whole(near), whole(f), whole(b)],
        out_specs=[pl.BlockSpec((rows, cols), lambda i: (0, 0))] * 2,
        out_shape=[jax.ShapeDtypeStruct((rows, cols), BF16)] * 2,
        compiler_params=params("arbitrary"),
        cost_estimate=cost(flops=near.size, bytes_accessed=8 * near.size, transcendentals=0),
        name="ring_add",
    )(near, f, b)


def grad_x_body(idx, rows, w, out):
    out[...] = dot_nt(rows[...], w[...]).astype(out.dtype)


def grad_x_terms(places, rels, d_joint, w_joint, rows, kind):
    feats, cols = w_joint.shape
    step = rels[-1] - rels[0]
    return pl.pallas_call(
        grad_x_body,
        grid_spec=pltpu.PrefetchScalarGridSpec(
            num_scalar_prefetch=1,
            grid=(len(rels),),
            in_specs=[
                pl.BlockSpec((rows, cols), lambda j, idx: (idx[rels[0] + j * step], 0)),
                pl.BlockSpec((feats, cols), lambda j, idx: (0, 0)),
            ],
            out_specs=pl.BlockSpec((rows, feats), lambda j, idx: (j, 0)),
        ),
        out_shape=jax.ShapeDtypeStruct((len(rels) * rows, feats), kind),
        compiler_params=params("arbitrary"),
        cost_estimate=cost(
            flops=2 * rows * feats * cols * len(rels), bytes_accessed=2 * feats * cols, transcendentals=0
        ),
        name="grad_x_terms",
    )(places, d_joint, w_joint)


def input_grad_body(own, f, b, mid, x_ref, gain, out):
    grad = own[...] + f[...].astype(F32) + b[...].astype(F32)
    x = x_ref[...].astype(F32)
    inverse = lax.rsqrt(jnp.mean(x * x, axis=-1, keepdims=True) + EPS)
    unit = x * inverse
    scaled = grad * gain[...]
    inner = jnp.mean(scaled * unit, axis=-1, keepdims=True)
    out[...] = (mid[...] + inverse * (scaled - unit * inner)).astype(BF16)


def input_grad_of(own, f, b, mid, tokens, gain):
    rows, feats = tokens.shape
    blk = pl.BlockSpec((rows // 2, feats), lambda i: (i, 0))
    return pl.pallas_call(
        input_grad_body,
        grid=(2,),
        in_specs=[blk] * 5 + [pl.BlockSpec((1, feats), lambda i: (0, 0))],
        out_specs=blk,
        out_shape=jax.ShapeDtypeStruct((rows, feats), BF16),
        compiler_params=params("arbitrary"),
        cost_estimate=cost(flops=9 * rows * feats, bytes_accessed=14 * rows * feats, transcendentals=0),
        name="input_grad",
    )(own, f, b, mid, tokens, gain.reshape(1, -1))


def shard_sum_body(n_back, units, pad, value, *refs):
    out = refs[-1]
    total = value[:units, :].astype(F32)
    for back in refs[:n_back]:
        total = total + back[...].astype(F32)
    out[...] = total.astype(BF16)


def shard_sum(value, backs, units):
    whole = lambda a: pl.BlockSpec(a.shape, lambda i: (0, 0))
    return pl.pallas_call(
        functools.partial(shard_sum_body, len(backs), units, 0),
        grid=(1,),
        in_specs=[whole(a) for a in (value, *backs)],
        out_specs=pl.BlockSpec((units, value.shape[1]), lambda i: (0, 0)),
        out_shape=jax.ShapeDtypeStruct((units, value.shape[1]), BF16),
        compiler_params=params("arbitrary"),
        cost_estimate=cost(flops=value.size, bytes_accessed=4 * value.size, transcendentals=0),
        name="shard_sum",
    )(value, *backs)


def widen_body(src, *outs):
    at = 0
    for out in outs:
        out[...] = src[0, :, at : at + out.shape[1]].astype(F32)
        at += out.shape[1]


def widen_pieces_body(n, idx, *refs):
    p = pl.program_id(0)
    outs = refs[n:]
    for i, src in enumerate(refs[:n]):

        @pl.when(p == i)
        def _():
            at = 0
            for out in outs:
                out[...] = src[:, at : at + out.shape[1]].astype(F32)
                at += out.shape[1]


def widen_pieces(places, pieces, widths):
    n = len(pieces)
    rows, cols = pieces[0].shape
    return pl.pallas_call(
        functools.partial(widen_pieces_body, n),
        grid_spec=pltpu.PrefetchScalarGridSpec(
            num_scalar_prefetch=1,
            grid=(n,),
            in_specs=[pl.BlockSpec((rows, cols), lambda p, idx: (0, 0))] * n,
            out_specs=[pl.BlockSpec((rows, w), lambda p, idx: (idx[p], 0)) for w in widths],
        ),
        out_shape=[jax.ShapeDtypeStruct((n * rows, w), F32) for w in widths],
        compiler_params=params("arbitrary"),
        name="widen_pieces",
    )(places, *pieces)


def widen_cols(got):
    n_dp, rows, cols = got.shape
    return pl.pallas_call(
        widen_body,
        grid=(n_dp,),
        in_specs=[pl.BlockSpec((1, rows, cols), lambda p: (part_of(p, n_dp), 0, 0))],
        out_specs=[pl.BlockSpec((rows, cols), lambda p: (0, p))],
        out_shape=[jax.ShapeDtypeStruct((rows, n_dp * cols), F32)],
        compiler_params=params("arbitrary"),
        name="widen_cols",
    )(got)[0]


def parts_ready(p, srcs, parts, sems):
    copies = [pltpu.make_async_copy(w, parts.at[i], sems.at[i]) for i, w in enumerate(srcs)]

    @pl.when(p == 0)
    def _():
        for c in copies:
            c.start()

    for i, c in enumerate(copies):

        @pl.when(p == i)
        def _():
            c.wait()


def out_body(n_dp, idx, heads, x_ref, gain, *refs):
    srcs, (branch_out, mid_out, h_out, heads_out, parts, sems) = refs[:n_dp], refs[n_dp:]
    p = pl.program_id(0)
    n_t, rows, cols = heads.shape
    width = parts.shape[2]
    parts_ready(p, srcs, parts, sems)

    @pl.when(p == 0)
    def _():
        for t in range(n_t):
            heads_out[:, t * cols : (t + 1) * cols] = heads[t]

    part = pl.ds(pl.multiple_of(idx[p] * width, width), width)
    branch_out[:, part] = dot_nn(heads_out[...], parts[p])

    @pl.when(p == n_dp - 1)
    def _():
        mid = x_ref[...].astype(F32) + branch_out[...]
        mid_out[...] = mid
        inverse = lax.rsqrt(jnp.mean(mid * mid, axis=-1, keepdims=True) + EPS)
        h_out[...] = (mid * inverse * gain[...]).astype(BF16)


def out_project(heads, w_places, w_parts, tokens, gain):
    n_dp = len(w_parts)
    feats_in, width = w_parts[0].shape
    rows, feats = tokens.shape
    full = lambda shape: pl.BlockSpec(shape, lambda p, idx: (0,) * len(shape))
    sq = (rows, feats)
    return pl.pallas_call(
        functools.partial(out_body, n_dp),
        grid_spec=pltpu.PrefetchScalarGridSpec(
            num_scalar_prefetch=1,
            grid=(n_dp,),
            in_specs=[full(heads.shape), full(sq), full((1, feats))] + [ANY] * n_dp,
            out_specs=[full(sq)] * 4,
            scratch_shapes=[
                pltpu.VMEM((n_dp, feats_in, width), BF16),
                pltpu.SemaphoreType.DMA((n_dp,)),
            ],
        ),
        out_shape=[
            jax.ShapeDtypeStruct(sq, F32),
            jax.ShapeDtypeStruct(sq, F32),
            jax.ShapeDtypeStruct(sq, BF16),
            jax.ShapeDtypeStruct((rows, feats_in), BF16),
        ],
        compiler_params=params("arbitrary"),
        cost_estimate=cost(
            flops=2 * rows * feats * feats_in,
            bytes_accessed=2 * feats * feats_in + 16 * rows * feats,
            transcendentals=0,
        ),
        name="out_project",
    )(w_places, heads, tokens, gain.reshape(1, -1), *w_parts)


def out_back_body(n_dp, idx, own, f, b, mid_ref, dy, gain, *refs):
    srcs, (mid_out, low_out, gain_out, heads_out, acc, parts, sems) = refs[:n_dp], refs[n_dp:]
    p = pl.program_id(0)
    n_t, rows, cols = heads_out.shape
    width = parts.shape[2]
    parts_ready(p, srcs, parts, sems)

    @pl.when(p == 0)
    def _():
        grad = own[...] + f[...].astype(F32) + b[...].astype(F32)
        mid = mid_ref[...]
        inverse = lax.rsqrt(jnp.mean(mid * mid, axis=-1, keepdims=True) + EPS)
        unit = mid * inverse
        gain_out[...] = jnp.sum(grad * unit, axis=0, keepdims=True)
        scaled = grad * gain[...]
        inner = jnp.mean(scaled * unit, axis=-1, keepdims=True)
        total = dy[...].astype(F32) + inverse * (scaled - unit * inner)
        mid_out[...] = total
        low_out[...] = total.astype(BF16)
        acc[...] = jnp.zeros_like(acc)

    part = pl.ds(pl.multiple_of(idx[p] * width, width), width)
    acc[...] += dot_nt(low_out[:, part], parts[p])

    @pl.when(p == n_dp - 1)
    def _():
        for t in range(n_t):
            heads_out[t] = acc[:, t * cols : (t + 1) * cols].astype(BF16)


def out_back(own, f, b, mid, dy, gain, w_places, w_parts, n_t):
    n_dp = len(w_parts)
    feats_in, width = w_parts[0].shape
    rows, feats = mid.shape
    full = lambda shape: pl.BlockSpec(shape, lambda p, idx: (0,) * len(shape))
    sq = (rows, feats)
    heads = (n_t, rows, feats_in // n_t)
    return pl.pallas_call(
        functools.partial(out_back_body, n_dp),
        grid_spec=pltpu.PrefetchScalarGridSpec(
            num_scalar_prefetch=1,
            grid=(n_dp,),
            in_specs=[full(sq)] * 5 + [full((1, feats))] + [ANY] * n_dp,
            out_specs=[full(sq), full(sq), full((1, feats)), full(heads)],
            scratch_shapes=[
                pltpu.VMEM((rows, feats_in), F32),
                pltpu.VMEM((n_dp, feats_in, width), BF16),
                pltpu.SemaphoreType.DMA((n_dp,)),
            ],
        ),
        out_shape=[
            jax.ShapeDtypeStruct(sq, F32),
            jax.ShapeDtypeStruct(sq, BF16),
            jax.ShapeDtypeStruct((1, feats), F32),
            jax.ShapeDtypeStruct(heads, BF16),
        ],
        compiler_params=params("arbitrary"),
        cost_estimate=cost(
            flops=2 * rows * feats * feats_in,
            bytes_accessed=2 * feats * feats_in + 20 * rows * feats,
            transcendentals=0,
        ),
        name="out_back",
    )(w_places, own, f, b, mid, dy, gain.reshape(1, -1), *w_parts)


def ffn_body(n_in, n_w, first, units, n_buf, *refs):
    hs, refs = refs[:n_in], refs[n_in:]
    ys, refs = refs[:n_in], refs[n_in:]
    srcs, refs = refs[:n_w], refs[n_w:]
    if first:
        refs = refs[n_buf:]
        h_out, y_out, refs = refs[0], refs[1], refs[2:]
    else:
        dh_in, refs = refs[0], refs[1 + n_buf :]
    hid_out, gg_out, gu_out, dh_ref, weights, sems = refs[:6]
    waits = []
    for j in range(3):
        if first:
            waits.append([pltpu.make_async_copy(srcs[j], weights.at[j], sems.at[j])])
            continue
        src = srcs[j]
        n_dp, _, width = src.shape
        waits.append(
            [
                pltpu.make_async_copy(
                    src.at[p], weights.at[j, :, pl.ds(p * width, width)], sems.at[j]
                )
                for p in range(n_dp)
            ]
        )
    for group in waits:
        for c in group:
            c.start()

    def ready(j):
        for c in waits[j]:
            c.wait()
        return weights[j]

    if not first:
        h_out, y_out = refs[6:]
    at = 0
    for h, y in zip(hs, ys):
        h_out[at : at + h.shape[0], :] = h[...]
        y_out[at : at + h.shape[0], :] = y[...]
        at += h.shape[0]
    gate = dot_nt(h_out[...], ready(0))
    up = dot_nt(h_out[...], ready(1))
    gh = dot_nt(y_out[...], ready(2))
    sig = jax.nn.sigmoid(gate)
    act = gate * sig
    hid_out[:, :units] = (act * up).astype(BF16)
    gg = (gh * up * (sig + act * (1.0 - sig))).astype(BF16)
    gu = (gh * act).astype(BF16)
    gg_out[:, :units] = gg
    gu_out[:, :units] = gu
    pad = hid_out.shape[1] - units
    if pad > 0:
        for o in (hid_out, gg_out, gu_out):
            o[:, units:] = jnp.zeros((o.shape[0], pad), BF16)
    part = dot_nn(gg, weights[0]) + dot_nn(gu, weights[1])
    if not first:
        part = part + dh_in[...]
    dh_ref[...] = part


def ffn_set(hs, ys, srcs, units, shard, shards, total, place, dh, bufs):
    n_in, n_w, first = len(hs), len(srcs), shard == 0
    feats = hs[0].shape[1]
    m = sum(h.shape[0] for h in hs)
    pad = -(-units // 128) * 128
    whole = lambda a: pl.BlockSpec(a.shape, lambda i: (0, 0))
    args = list(hs) + list(ys) + list(srcs)
    in_specs = [whole(a) for a in args[: 2 * n_in]] + [ANY] * n_w
    if not first:
        args.append(dh)
        in_specs.append(whole(dh))
    out_specs = [pl.BlockSpec((m, pad), lambda i: (place, shard))] * 3
    out_shape = [jax.ShapeDtypeStruct((total, pad * shards), BF16)] * 3
    held = list(bufs[2:])
    if first:
        out_specs = [pl.BlockSpec((m, feats), lambda i: (place, 0))] * 2 + out_specs
        out_shape = [jax.ShapeDtypeStruct((total, feats), BF16)] * 2 + out_shape
        held = list(bufs)
    aliases = {len(args) + i: i for i in range(len(held))}
    args += held
    in_specs += [ANY] * len(held)
    scratch = [pltpu.VMEM((3, units, feats), BF16), pltpu.SemaphoreType.DMA((3,))]
    if not first:
        scratch += [pltpu.VMEM((m, feats), BF16)] * 2
    out = pl.pallas_call(
        functools.partial(ffn_body, n_in, n_w, first, units, len(held)),
        grid=(1,),
        in_specs=in_specs,
        out_specs=out_specs + [pl.BlockSpec((m, feats), lambda i: (0, 0))],
        out_shape=out_shape + [jax.ShapeDtypeStruct((m, feats), F32)],
        scratch_shapes=scratch,
        input_output_aliases=aliases,
        compiler_params=params("arbitrary"),
        cost_estimate=cost(
            flops=10 * m * feats * units,
            bytes_accessed=6 * feats * units + 16 * m * feats,
            transcendentals=m * units,
        ),
        name="ffn_set",
    )(*args)
    new, dh = list(out[:-1]), out[-1]
    return (new if first else list(bufs[:2]) + new), dh


def down_body(n_got, units, hid, own, *refs):
    got, (out, weights, sems) = refs[:n_got], refs[n_got:]
    waits = [[pltpu.make_async_copy(own, weights.at[0], sems.at[0])]]
    for s, src in enumerate(got):
        n_dp, _, width = src.shape
        waits.append(
            [
                pltpu.make_async_copy(
                    src.at[p], weights.at[s + 1, :, pl.ds(p * width, width)], sems.at[s + 1]
                )
                for p in range(n_dp)
            ]
        )
    for group in waits:
        for c in group:
            c.start()
    pad = hid.shape[1] // (n_got + 1)
    total = None
    for s, group in enumerate(waits):
        for c in group:
            c.wait()
        part = dot_nn(hid[:, s * pad : s * pad + units], weights[s])
        total = part if total is None else total + part
    out[...] = total.astype(BF16)


def down_rows(hid, own, got):
    m = hid.shape[0]
    units, feats = own.shape
    n_w = len(got) + 1
    return pl.pallas_call(
        functools.partial(down_body, len(got), units),
        grid=(1,),
        in_specs=[pl.BlockSpec(hid.shape, lambda i: (0, 0))] + [ANY] * n_w,
        out_specs=pl.BlockSpec((m, feats), lambda i: (0, 0)),
        out_shape=jax.ShapeDtypeStruct((m, feats), BF16),
        scratch_shapes=[
            pltpu.VMEM((n_w, units, feats), BF16),
            pltpu.SemaphoreType.DMA((n_w,)),
        ],
        compiler_params=params("arbitrary"),
        cost_estimate=cost(
            flops=2 * m * units * feats * n_w,
            bytes_accessed=2 * units * feats * n_w + 6 * m * feats,
            transcendentals=0,
        ),
        name="down_rows",
    )(hid, own, *got)


LOG2E = 1.4426950408889634
SCALE = HEAD_DIM ** (-0.5)


def attend_body(q_ref, k0, k1, v0, v1, lo_ref, *rest):
    o_ref, ks, vs = rest[-3:]
    i = pl.program_id(1)
    span = Q_BLK + WINDOW

    @pl.when(i == 0)
    def _():
        ks[:WINDOW] = k0[...]
        ks[WINDOW:] = k1[...]
        vs[:WINDOW] = v0[...]
        vs[WINDOW:] = v1[...]

    start = pl.multiple_of(i * Q_BLK, Q_BLK)
    kb = ks[pl.ds(start, span), :]
    vb = vs[pl.ds(start, span), :]
    s = dot_nt(q_ref[...], kb) * (SCALE * LOG2E)
    col = lax.broadcasted_iota(jnp.int32, s.shape, 1)
    row = lax.broadcasted_iota(jnp.int32, s.shape, 0)
    lo = lo_ref[...] - start
    s = jnp.where((col >= lo) & (col <= row + WINDOW), s, NEG)
    p = jnp.exp2(s - jnp.max(s, axis=1, keepdims=True))
    total = jnp.sum(p, axis=1, keepdims=True)
    o = dot_nn(p.astype(BF16), vb) * (1.0 / total)
    o_ref[...] = o.astype(BF16)


def attend(half, q, pair, lo, buf):
    total, cols = q.shape
    heads = cols // HEAD_DIM
    rows = total // 2
    blocks = rows // Q_BLK
    base = half * blocks
    q_spec = pl.BlockSpec((Q_BLK, HEAD_DIM), lambda h, i: (base + i, h))
    key_spec = lambda b, c: pl.BlockSpec((WINDOW, HEAD_DIM), lambda h, i: (b, c + h))
    lo_spec = pl.BlockSpec((Q_BLK, 1), lambda h, i: (base + i, 0))
    in_specs = [
        q_spec,
        key_spec(pair[0][1], 0),
        key_spec(pair[1][1], 0),
        key_spec(pair[0][1], heads),
        key_spec(pair[1][1], heads),
        lo_spec,
    ]
    args = [q, pair[0][0], pair[1][0], pair[0][0], pair[1][0], lo]
    aliases = {}
    if buf is not None:
        in_specs.append(pl.BlockSpec(memory_space=pl.ANY))
        args.append(buf)
        aliases = {6: 0}
    return pl.pallas_call(
        attend_body,
        grid=(heads, blocks),
        in_specs=in_specs,
        out_specs=q_spec,
        out_shape=jax.ShapeDtypeStruct((total, cols), BF16),
        scratch_shapes=[pltpu.VMEM((2 * WINDOW, HEAD_DIM), BF16)] * 2,
        input_output_aliases=aliases,
        compiler_params=params("arbitrary", "arbitrary"),
        cost_estimate=cost(
            flops=4 * rows * (Q_BLK + WINDOW) * cols,
            bytes_accessed=2 * cols * 6 * WINDOW,
            transcendentals=rows * (Q_BLK + WINDOW) * heads,
        ),
        name="attend",
    )(*args)


def attend_back_body(q_ref, g_ref, k0, k1, v0, v1, lo_ref, cos_ref, sin_ref, *rest):
    dq_ref, dk_ref, dv_ref, ks, vs = rest[-5:]
    i = pl.program_id(1)
    span = Q_BLK + WINDOW

    @pl.when(i == 0)
    def _():
        ks[:WINDOW] = k0[...]
        ks[WINDOW:] = k1[...]
        vs[:WINDOW] = v0[...]
        vs[WINDOW:] = v1[...]
        dk_ref[...] = jnp.zeros_like(dk_ref)
        dv_ref[...] = jnp.zeros_like(dv_ref)

    start = pl.multiple_of(i * Q_BLK, Q_BLK)
    kb = ks[pl.ds(start, span), :]
    vb = vs[pl.ds(start, span), :]
    q, g = q_ref[...], g_ref[...]
    s = dot_nt(kb, q) * (SCALE * LOG2E)
    key = lax.broadcasted_iota(jnp.int32, s.shape, 0)
    row = lax.broadcasted_iota(jnp.int32, s.shape, 1)
    lo = lo_ref[...] - start
    s = jnp.where((key >= lo) & (key <= row + WINDOW), s, NEG)
    p = jnp.exp2(s - jnp.max(s, axis=0, keepdims=True))
    p = p * (1.0 / jnp.sum(p, axis=0, keepdims=True))
    dp = dot_nt(vb, g)
    inner = jnp.sum(p * dp, axis=0, keepdims=True)
    ds = (p * (dp - inner)).astype(BF16)
    dq = dot_tn(ds, kb) * SCALE
    dq = dq * cos_ref[...] - pltpu.roll(dq, HEAD_DIM // 2, 1) * sin_ref[...]
    dq_ref[...] = dq.astype(BF16)
    dk_ref[pl.ds(start, span), :] += dot_nn(ds, q) * SCALE
    dv_ref[pl.ds(start, span), :] += dot_nn(p.astype(BF16), g)


def attend_back(half, q, g, pair, lo_row, cos, sin, buf):
    total, cols = q.shape
    heads = cols // HEAD_DIM
    rows = total // 2
    blocks = rows // Q_BLK
    base = half * blocks
    q_spec = pl.BlockSpec((Q_BLK, HEAD_DIM), lambda h, i: (base + i, h))
    key_spec = lambda b, c: pl.BlockSpec((WINDOW, HEAD_DIM), lambda h, i: (b, c + h))
    rope_spec = pl.BlockSpec((Q_BLK, HEAD_DIM), lambda h, i: (base + i, 0))
    lo_spec = pl.BlockSpec((1, Q_BLK), lambda h, i: (0, base + i))
    grad_spec = pl.BlockSpec((2 * WINDOW, HEAD_DIM), lambda h, i: (0, h))
    in_specs = [
        q_spec,
        q_spec,
        key_spec(pair[0][1], 0),
        key_spec(pair[1][1], 0),
        key_spec(pair[0][1], heads),
        key_spec(pair[1][1], heads),
        lo_spec,
        rope_spec,
        rope_spec,
    ]
    args = [q, g, pair[0][0], pair[1][0], pair[0][0], pair[1][0], lo_row, cos, sin]
    aliases = {}
    if buf is not None:
        in_specs.append(pl.BlockSpec(memory_space=pl.ANY))
        args.append(buf)
        aliases = {9: 0}
    return pl.pallas_call(
        attend_back_body,
        grid=(heads, blocks),
        in_specs=in_specs,
        out_specs=[
            pl.BlockSpec((Q_BLK, HEAD_DIM), lambda h, i: (base + i, 2 * heads + h)),
            grad_spec,
            grad_spec,
        ],
        out_shape=[
            jax.ShapeDtypeStruct((total, 3 * cols), BF16),
            jax.ShapeDtypeStruct((2 * WINDOW, cols), F32),
            jax.ShapeDtypeStruct((2 * WINDOW, cols), F32),
        ],
        scratch_shapes=[pltpu.VMEM((2 * WINDOW, HEAD_DIM), BF16)] * 2,
        input_output_aliases=aliases,
        compiler_params=params("arbitrary", "arbitrary"),
        cost_estimate=cost(
            flops=10 * rows * (Q_BLK + WINDOW) * cols,
            bytes_accessed=2 * cols * 14 * WINDOW,
            transcendentals=rows * (Q_BLK + WINDOW) * heads,
        ),
        name="attend_back",
    )(*args)


def finish_body(half, ak, av, ok, ov, cos_ref, sin_ref, _, out_ref):
    cols = ak.shape[1]

    def write(gk, gv):
        for h in range(cols // HEAD_DIM):
            c = slice(h * HEAD_DIM, (h + 1) * HEAD_DIM)
            seg = gk[:, c]
            seg = seg * cos_ref[...] - pltpu.roll(seg, HEAD_DIM // 2, 1) * sin_ref[...]
            out_ref[:, c] = seg.astype(BF16)
        out_ref[:, cols:] = gv.astype(BF16)

    write(ak[...] + ok[...].astype(F32), av[...] + ov[...].astype(F32))


def finish_keys(half, ak, av, other_k, other_v, cos, sin, buf):
    cols = ak.shape[1]
    blk = 512
    n = WINDOW // blk
    base = half * n
    own = pl.BlockSpec((blk, cols), lambda i: (base + i, 0))
    oth = lambda o: pl.BlockSpec((blk, cols), lambda i: (o[1] * n + i, o[2]))
    rope = pl.BlockSpec((blk, HEAD_DIM), lambda i: (base + i, 0))
    return pl.pallas_call(
        functools.partial(finish_body, half),
        grid=(n,),
        in_specs=[own, own, oth(other_k), oth(other_v), rope, rope, ANY],
        out_specs=pl.BlockSpec((blk, 2 * cols), lambda i: (base + i, 0)),
        out_shape=jax.ShapeDtypeStruct(buf.shape, BF16),
        input_output_aliases={6: 0},
        compiler_params=params("arbitrary"),
        name="finish_keys",
    )(ak, av, other_k[0], other_v[0], cos, sin, buf)


def shards(
    tokens, segments, attn_gain, ffn_gain, w_query, w_key, w_value, w_out, w_gate, w_up, w_down, cotangent
):
    rows, feats = tokens.shape
    n_tensor = lax.axis_size("tensor")
    n_dp = lax.axis_size("dp")
    block_len = rows * n_tensor
    head_cols = w_query.shape[1]
    units = w_gate.shape[1]
    unit_pad = -(-units // 128) * 128
    dp_idx, t_idx = lax.axis_index("dp"), lax.axis_index("tensor")
    first_pos = dp_idx * block_len
    ring = [ring_cycle(n_tensor)]
    square = group_cycles(n_tensor)
    groups = n_tensor // GROUP
    far = n_tensor // 2
    part_cols = feats // n_dp
    own_w = (w_gate.T, w_up.T, w_down)

    def to_group(piece, s):
        pairs = [(t, (t + s * GROUP) % n_tensor) for t in range(n_tensor)]
        return lax.ppermute(piece, "tensor", pairs)

    def dp_cols(value):
        return lax.dynamic_slice_in_dim(value, dp_idx * part_cols, part_cols, 1)

    ring_owners = owners(ring)
    x_f = tokens.astype(F32)
    x_normed, x_unit, x_inv = norm_forward(x_f, attn_gain)
    x_low = x_normed.astype(BF16)
    go = Gather(dp_cols(w_out), ring)
    go.all()
    w_joint = jnp.concatenate([w_key, w_value, w_query], axis=1)
    gx = Gather(after(x_low, go.f, go.b), ring)
    gx.step()
    w_out_part = place_chunks(ring_owners, go.chunks, n_tensor)
    cos, sin = rope_tables(first_pos + jnp.arange(block_len, dtype=jnp.int32))
    cos, sin = after(cos, w_joint, w_out_part), after(sin, w_joint)

    def qkv(rel, bufs):
        return qkv_chunk(
            ring_owners, rel % n_tensor, gx.chunks[rel], w_query, w_key, w_value, cos, sin, bufs
        )

    bufs = qkv(0, None)
    for k in range(1, far):
        came = (gx.f, gx.b)
        gx.step(bufs[0])
        if k == 1:
            seg_tail = after(segments[block_len - WINDOW :].astype(F32), *came)
            prev_seg = shifted(seg_tail, "dp", 1).astype(jnp.int32)
            w_out_part = w_out_part.reshape(n_tensor * head_cols, part_cols)
            low_bits = bits_of(n_dp)
            w_spread = spread_parts([(0, w_out_part)], low_bits[-1:])
        if k == far - 1:
            w_spread = spread_parts(w_spread, low_bits[:-1], *came)
        bufs = qkv(k, qkv(-k, bufs))
    w_places = jnp.stack([dp_idx ^ x for x, _ in w_spread]).astype(jnp.int32)
    w_out_parts = [w for _, w in w_spread]

    seg_all = jnp.concatenate([prev_seg, segments], axis=0)
    low_key = jnp.sum((seg_all[None, :] < segments[:, None]).astype(jnp.int32), axis=1)
    low_key = jnp.where(dp_idx == 0, jnp.maximum(low_key, WINDOW), low_key)
    spot = jnp.arange(block_len, dtype=jnp.int32)
    low_key = jnp.maximum(low_key, spot + 1)
    low_key = low_key - jnp.where(spot >= block_len // 2, block_len // 2, 0)
    low_col, low_row = low_key[:, None], low_key[None, :]

    came = (gx.f, gx.b)
    mine, low_col, low_row, *w_out_parts = lax.optimization_barrier(
        (tuple(dp_cols(w) for w in own_w), low_col, low_row, *w_out_parts)
    )
    first = after(mine[0], *came)
    gate_got = [to_group(first, s) for s in range(1, groups)]
    bufs = list(bufs)
    bufs[0] = after(bufs[0], low_col, low_row, first, *w_out_parts)
    bufs = qkv(far, bufs)
    query, key_value, x_all = bufs
    tail_kv = after(key_value[block_len - WINDOW :])
    prev = shifted(tail_kv, "dp", 1)
    gy = Gather(after(cotangent, *came), square)
    gy.step()

    late, early = ((key_value, 0), (key_value, 1)), ((prev, 0), (key_value, 0))
    heads_late = attend(1, query, late, low_col, None)
    gy_came = (gy.f, gy.b)
    heads_late = after(heads_late, *gy_came)
    heads_low = attend(0, query, early, low_col, heads_late)
    heads_low = heads_low.reshape(n_tensor, rows, head_cols)
    heads_low = after(heads_low, *gate_got)

    heads_got = lax.all_to_all(heads_low, "tensor", split_axis=0, concat_axis=0, tiled=True)
    gate_all_got = [all_dp(after(g, heads_low)) for g in gate_got]
    second = after(mine[1], heads_got)
    up_got = [to_group(second, s) for s in range(1, groups)]
    gy.step(heads_got)
    y_chunks = gy.chunks
    attn_branch, mid, h_low, my_heads = out_project(
        heads_got, w_places, w_out_parts, tokens, ffn_gain
    )

    gh = Gather(h_low, square)
    sets = {0: ([0], 2), 1: ([-1, 1], 0), 2: ([2], 3)}
    ffn_bufs, dhs = [], {}

    def ffn(i, shard, *deps):
        rels, place = sets[i]
        hs = [c for r in rels for c in gh.chunks[r]]
        ys = [c for r in rels for c in y_chunks[r]]
        srcs = own_w if shard == 0 else got[shard - 1]
        hs[0] = after(hs[0], *deps)
        return ffn_set(
            hs, ys, srcs, units, shard, groups, GROUP * rows, place, dhs.get(i), ffn_bufs
        )

    gh.step()
    ffn_bufs, dhs[0] = ffn(0, 0)
    third = after(mine[2], h_low, *up_got)
    down_got = [to_group(third, s) for s in range(1, groups)]
    came = (*gh.chunks[1], *gh.chunks[-1], *gate_all_got)
    up_all_got = [all_dp(after(g, dhs[0], *came)) for g in up_got]
    gh.step(dhs[0])
    ffn_bufs, dhs[1] = ffn(1, 0)
    came = (*gh.chunks[2], *y_chunks[2], *up_all_got)
    down_all_got = [all_dp(after(d, dhs[1], *came)) for d in down_got]
    got = list(zip(gate_all_got, up_all_got, down_all_got))
    ffn_bufs, dhs[2] = ffn(2, 0)
    for s in range(1, groups):
        ffn_bufs, dhs[2] = ffn(2, s)
    sh = Scatter(dhs[2].astype(BF16), square)
    for s in range(1, groups):
        ffn_bufs, dhs[1] = ffn(1, s, *sh.sent)
    sh.step(dhs[1], False)
    for s in range(1, groups):
        ffn_bufs, dhs[0] = ffn(0, s, *sh.sent)
    h_all, y_all, hid_all, gate_all, up_all = ffn_bufs

    def send_back(red, *deps):
        cut = lambda s: red.value[s * unit_pad : s * unit_pad + units]
        return [to_group(after(cut(s), *deps), groups - s) for s in range(1, groups)]

    red_down = Halves(*tn_cols(hid_all, y_all), 1)
    red_down.send()
    red_gate = Halves(*tn_cols(after(gate_all, red_down.sent), h_all), 1)
    sh.f, sh.b, dhs[0], red_down.got, red_gate.sent = together(
        sh.f, sh.b, dhs[0], red_down.got, red_gate.sent
    )
    grad_mid, grad_mid_low, grad_ffn_gain, my_grad_heads = out_back(
        dhs[0], sh.f, sh.b, mid, cotangent, ffn_gain, w_places, w_out_parts, n_tensor
    )
    grad_heads = lax.all_to_all(
        my_grad_heads, "tensor", split_axis=0, concat_axis=0, tiled=True
    ).reshape(block_len, head_cols)

    red_down.add()
    red_down.send(my_grad_heads)
    red_gate.send(red_down.sent)
    sf_all = down_rows(after(hid_all, red_down.sent), own_w[2], [g[2] for g in got])
    red_up = Halves(*tn_cols(after(up_all, red_down.sent), h_all), 1)
    grad_heads, red_down.got, red_gate.got, sf_all, red_up.sent = together(
        grad_heads, red_down.got, red_gate.got, sf_all, red_up.sent
    )
    red_down.finish()
    down_back = send_back(red_down)
    red_gate.add()
    red_gate.send()
    red_up.send()
    sf = Scatter(sf_all[3 * rows :], square)

    grad_heads = after(grad_heads, red_down.value, *sf.sent, red_gate.sent)
    d_joint, bk, bv = attend_back(0, query, grad_heads, early, low_row, cos, sin, None)
    d_joint, bk, bv, sf.f, sf.b, red_up.got = together(d_joint, bk, bv, sf.f, sf.b, red_up.got)
    back = after(jnp.concatenate([bk[:WINDOW], bv[:WINDOW]], axis=1).astype(BF16))
    got_back = shifted(back, "dp", -1)
    sf.step(after(sf_all[: 2 * rows], back), False)
    red_up.add()
    out_local = dot_tn(my_heads, after(grad_mid_low, back)).astype(BF16)
    out_dp = lax.psum_scatter(out_local, "dp", scatter_dimension=1, tiled=True)
    d_joint, ak, av = attend_back(
        1, query, after(grad_heads, back, *sf.sent, red_up.sent, out_local),
        late, low_row, cos, sin, d_joint,
    )
    d_joint, ak, av, got_back, sf.f, sf.b, red_gate.got, *down_back = together(
        d_joint, ak, av, got_back, sf.f, sf.b, red_gate.got, *down_back
    )
    red_gate.finish()
    gate_back = send_back(red_gate)
    red_up.send(red_gate.value)
    d_joint = finish_keys(0, after(ak, red_gate.value), av, (bk, 1, 0), (bv, 1, 0), cos, sin, d_joint)
    d_joint = finish_keys(1, ak, av, (got_back, 0, 0), (got_back, 0, 1), cos, sin, d_joint)

    def terms(rels, kind, *deps):
        rels = [r % n_tensor for r in rels]
        return grad_x_terms(after(ring_owners, *deps), rels, d_joint, w_joint, rows, kind)

    sx = Scatter(terms([far], BF16), ring)
    near = terms([far - 1, 1 - far], F32, *sx.sent)
    down_own = shard_sum(after(red_down.value, *sx.sent), down_back, units)
    down_dp = all_dp(down_own)
    joint = tn_rows(after(x_all, *sx.sent), d_joint, w_joint)
    grad_attn_gain = joint[2][:, 0] / attn_gain
    sx.f, sx.b, near, down_own, joint, out_dp, *gate_back = together(
        sx.f, sx.b, near, down_own, tuple(joint), out_dp, *gate_back
    )
    out_own = lax.psum_scatter(out_dp, "tensor", scatter_dimension=0, tiled=True)
    red_joint = Halves(*joint[:2], 0)
    red_joint.send()
    sx.step(near, True)
    gate_own = shard_sum(after(red_gate.value, *sx.sent), gate_back, units)
    gate_dp = all_dp(gate_own)
    near = terms([far - 2, 2 - far], F32, gate_own)
    sx.f, sx.b, near, red_up.got, red_joint.got, gate_own = together(
        sx.f, sx.b, near, red_up.got, red_joint.got, gate_own
    )
    red_up.finish()
    red_joint.add()
    up_back = send_back(red_up)
    red_joint.send()
    sx.step(near, True, red_up.value, red_joint.sent)
    ffn_branch = after(sf_all[2 * rows : 3 * rows], *sx.sent).astype(F32)
    ffn_branch = ffn_branch + sf.f.astype(F32) + sf.b.astype(F32)
    result = mid + ffn_branch
    slots = 2 * n_dp + 1
    own_seg = lax.dynamic_slice_in_dim(segments, t_idx * rows, rows)
    one_hot = (own_seg[:, None] == jnp.arange(slots, dtype=jnp.int32)[None, :]).astype(F32)
    per_row = jnp.stack(
        [
            jnp.sum(result * result, axis=1),
            jnp.sum(attn_branch * attn_branch, axis=1),
            jnp.sum(ffn_branch * ffn_branch, axis=1),
            jnp.ones((rows,), F32),
        ],
        axis=1,
    )
    table = jnp.dot(per_row.T, one_hot, precision=lax.Precision.HIGHEST, preferred_element_type=F32)
    packed = jnp.concatenate([grad_attn_gain, grad_ffn_gain[0], table.reshape(-1)])
    packed = jnp.pad(packed, (0, -packed.shape[0] % 1024)).reshape(-1, 128)
    near = terms([far - 3, 3 - far], F32, packed)
    grad_w_down = widen_cols(after(down_dp, near))
    sx.f, sx.b, near, red_joint.got, grad_w_down, out_own, *up_back = together(
        sx.f, sx.b, near, red_joint.got, grad_w_down, out_own, *up_back
    )
    out_all = all_dp(out_own)
    sx.step(near, True)
    for k in range(far - 4, 0, -1):
        sx.step(terms([k, -k], F32, *sx.sent), True)
    up_own = shard_sum(after(red_up.value, *sx.sent), up_back, units)
    up_dp = all_dp(up_own)
    red_joint.finish(*sx.sent)
    joint_parts = spread_parts([(0, red_joint.value)], bits_of(n_dp)[::-1])
    joint_places = jnp.stack([place_of(dp_idx ^ x, n_dp) for x, _ in joint_parts])
    grad_w_gate = widen_cols(after(gate_dp, up_own, red_joint.value)).T
    own = terms([0], F32, grad_w_gate)
    packed = sum_all(after(packed, *sx.sent))
    sx.f, sx.b, own, packed = together(sx.f, sx.b, own, packed)
    input_grad = input_grad_of(own, sx.f, sx.b, grad_mid, tokens, attn_gain)
    grad_w_out = jnp.concatenate(list(out_all), axis=1).astype(F32)
    grad_w_key, grad_w_value, grad_w_query = widen_pieces(
        joint_places.astype(jnp.int32), [v for _, v in joint_parts], [head_cols] * 3
    )
    grad_w_up = widen_cols(up_dp).T

    packed = packed.reshape(-1)
    sums = packed[2 * feats : 2 * feats + 4 * slots].reshape(4, slots)
    doc_rms = jnp.sqrt(sums[:3] / (jnp.maximum(sums[3:], 1.0) * feats))

    return (
        result.astype(BF16),
        input_grad,
        packed[:feats],
        packed[feats : 2 * feats],
        grad_w_query,
        grad_w_key,
        grad_w_value,
        grad_w_out,
        grad_w_gate,
        grad_w_up,
        grad_w_down,
        doc_rms,
    )


def solution(mesh):
    both = P(("dp", "tensor"), None)
    col, row = P(None, "tensor"), P("tensor", None)
    return jax.shard_map(
        shards,
        mesh=mesh,
        in_specs=(both, P("dp"), P(), P(), col, col, col, row, col, col, row, both),
        out_specs=(both, both, P(), P(), col, col, col, row, col, col, row, P()),
        check_vma=False,
    )
```

```python
import functools
import math

import jax
import jax.numpy as jnp
from jax import lax
from jax.experimental import pallas as pl
from jax.experimental.pallas import tpu as pltpu
from jax.sharding import PartitionSpec as P

HEAD_DIM = 128
WINDOW = 1024
EPS = 1e-06
NEG = -1e30
F32 = jnp.float32
BF16 = jnp.bfloat16
Q_BLK = 256
COST_PART = 16
GROUP = 4


def ring_cycle(count):
    if count == 8:
        return [0, 2, 4, 6, 7, 5, 3, 1]
    width = 4 if count % 4 == 0 else count
    order = []
    for row in range(count // width):
        part = list(range(row * width, (row + 1) * width))
        order += part if row % 2 == 0 else part[::-1]
    return order


def group_cycles(count):
    base = [0, 2, 3, 1] if count == 8 else list(range(GROUP))
    return [[g * GROUP + b for b in base] for g in range(count // GROUP)]


def step_pairs(cycles, step):
    return [
        (cyc[i], cyc[(i + step) % len(cyc)]) for cyc in cycles for i in range(len(cyc))
    ]


def owners(cycles, rels=None):
    table = {}
    for cyc in cycles:
        for i, dev in enumerate(cyc):
            steps = range(len(cyc)) if rels is None else rels
            table[dev] = [cyc[(i + rel) % len(cyc)] for rel in steps]
    rows = jnp.array([table[t] for t in range(len(table))], jnp.int32)
    return rows[lax.axis_index("tensor")]


def rel_order(size):
    order = [0]
    for k in range(1, size // 2):
        order += [-k, k]
    return order + [size // 2]


def after(value, *deps):
    return lax.optimization_barrier((value,) + deps)[0]


def together(*values):
    return lax.optimization_barrier(values)


class Gather:
    def __init__(self, own, cycles):
        self.size = len(cycles[0])
        self.ahead, self.back = step_pairs(cycles, 1), step_pairs(cycles, -1)
        self.f = self.b = own
        self.chunks = {0: [own]}
        self.k = 0

    def step(self, *deps):
        self.k += 1
        f, b = lax.optimization_barrier((self.f, self.b) + deps)[:2]
        if self.k < self.size // 2:
            self.f = lax.ppermute(f, "tensor", self.ahead)
            self.b = lax.ppermute(b, "tensor", self.back)
            self.chunks[-self.k], self.chunks[self.k] = [self.f], [self.b]
        else:
            half = self.f.shape[0] // 2
            self.f = lax.ppermute(f[:half], "tensor", self.ahead)
            self.b = lax.ppermute(b[half:], "tensor", self.back)
            self.chunks[self.k] = [self.f, self.b]

    def all(self):
        while self.k < self.size // 2:
            self.step()
        return self.chunks


class Scatter:
    def __init__(self, far, cycles):
        self.size = len(cycles[0])
        self.ahead, self.back = step_pairs(cycles, 1), step_pairs(cycles, -1)
        self.k = self.size // 2
        half = self.half = far.shape[0] // 2
        self.sent = lax.optimization_barrier((far[:half], far[half:]))
        self.send()

    def send(self):
        self.f = lax.ppermute(self.sent[0], "tensor", self.ahead)
        self.b = lax.ppermute(self.sent[1], "tensor", self.back)

    def step(self, near, first, *deps, at=0):
        f, b, near = lax.optimization_barrier((self.f, self.b, near) + deps)[:3]
        self.k -= 1
        self.sent = ring_add(near, f, b, first, 2 * self.half, at)
        self.send()


def bits_of(count):
    bit, out = 1, []
    while bit < count:
        out.append(bit)
        bit *= 2
    return out


def swap(value, axis, bit):
    count = lax.axis_size(axis)
    return lax.ppermute(value, axis, [(d, d ^ bit) for d in range(count)])


class Halves:
    def __init__(self, send, keep, axis):
        self.sent, self.keep, self.axis = send, keep, axis
        self.bits = bits_of(lax.axis_size("dp"))

    def send(self, *deps):
        self.sent = after(self.sent, *deps)
        self.got = swap(self.sent, "dp", self.bits[0])

    def add(self, *deps):
        got = after(self.got, *deps)
        self.bits = self.bits[1:]
        if self.bits:
            pair = half_add(self.keep, got, self.axis, dp_side(self.bits[0]))
            self.sent, self.keep = pair
            return self.keep
        self.value = plain_add(self.keep, got)
        return self.value

    def finish(self, *deps):
        self.add(*deps)
        while self.bits:
            self.send()
            self.add()
        return self.value


def dp_side(bit):
    side = (lax.axis_index("dp") // bit) % 2
    return jnp.stack([1 - side, side]).astype(jnp.int32)


def place_of(device, count):
    place = 0
    for bit in bits_of(count):
        place = place * 2 + (device // bit) % 2
    return place


def part_of(place, count):
    device = 0
    for bit in bits_of(count):
        device = device * 2 + place % 2
        place = place // 2
    return device


def all_dp(value):
    return lax.all_gather(value, "dp", axis=0, tiled=False)


def spread_parts(out, bits, *deps):
    for bit in bits:
        out = out + [(x ^ bit, swap(after(v, *deps), "dp", bit)) for x, v in out]
    return out


def hops():
    return [(a, bit) for a in ("tensor", "dp") for bit in bits_of(lax.axis_size(a))]


def shifted(value, axis, steps):
    count = lax.axis_size(axis)
    leading, last = max(0, -steps), min(count, count - steps)
    return lax.ppermute(value, axis, [(s, s + steps) for s in range(leading, last)])


def norm_forward(values, gain):
    inverse = lax.rsqrt(jnp.mean(values * values, axis=-1, keepdims=True) + EPS)
    unit = values * inverse
    return unit * gain, unit, inverse


def norm_backward(grad, unit, inverse, gain):
    scaled = grad * gain
    inner = jnp.mean(scaled * unit, axis=-1, keepdims=True)
    return inverse * (scaled - unit * inner)


def dot_nn(a, b):
    return jnp.dot(a, b, preferred_element_type=F32)


def dot_tn(a, b):
    return lax.dot_general(a, b, (((0,), (0,)), ((), ())), preferred_element_type=F32)


def dot_nt(a, b):
    return lax.dot_general(a, b, (((1,), (1,)), ((), ())), preferred_element_type=F32)


def rope_tables(positions):
    half = HEAD_DIM // 2
    freq = jnp.exp(jnp.arange(half, dtype=F32) * (-2.0 * math.log(10000.0) / HEAD_DIM))
    angles = positions.astype(F32)[:, None] * freq[None, :]
    cos, sin = jnp.cos(angles), jnp.sin(angles)
    return jnp.concatenate([cos, cos], axis=1), jnp.concatenate([-sin, sin], axis=1)


def cost(flops, bytes_accessed, transcendentals):
    return pl.CostEstimate(
        flops=flops // COST_PART,
        bytes_accessed=bytes_accessed // COST_PART,
        transcendentals=transcendentals // COST_PART,
    )


def params(*sem):
    return pltpu.CompilerParams(
        dimension_semantics=sem or None, vmem_limit_bytes=56 * 1024 * 1024
    )


ANY = pl.BlockSpec(memory_space=pl.ANY)


def qkv_body(n_in, idx, *refs):
    xs, refs = refs[:n_in], refs[n_in:]
    wq, wk, wv, cos_ref, sin_ref = refs[:5]
    q_out, kv_out, x_out = refs[-3:]
    at = 0
    for x in xs:
        x_out[at : at + x.shape[0], :] = x[...]
        at += x.shape[0]
    x = x_out[...]
    cos, sin = cos_ref[...], sin_ref[...]
    cols = wq.shape[1]
    for w, out in ((wq, q_out), (wk, kv_out)):
        p = dot_nn(x, w[...])
        for h in range(cols // HEAD_DIM):
            c = slice(h * HEAD_DIM, (h + 1) * HEAD_DIM)
            seg = p[:, c]
            out[:, c] = (seg * cos + pltpu.roll(seg, HEAD_DIM // 2, 1) * sin).astype(BF16)
    kv_out[:, cols:] = dot_nn(x, wv[...]).astype(BF16)


def qkv_chunk(places, rel, xs, wq, wk, wv, cos, sin, bufs):
    rows = sum(x.shape[0] for x in xs)
    feats, cols = wq.shape
    total = cos.shape[0]
    n_in = len(xs)
    full = lambda a: pl.BlockSpec(a.shape, lambda i, idx: (0, 0))
    at = lambda width: pl.BlockSpec((rows, width), lambda i, idx: (idx[rel], 0))
    args = list(xs) + [wq, wk, wv, cos, sin]
    in_specs = [full(a) for a in args[:-2]] + [at(HEAD_DIM)] * 2
    aliases = {}
    if bufs is not None:
        aliases = {1 + len(args) + i: i for i in range(3)}
        in_specs += [ANY] * 3
        args += list(bufs)
    widths = (cols, 2 * cols, feats)
    return pl.pallas_call(
        functools.partial(qkv_body, n_in),
        grid_spec=pltpu.PrefetchScalarGridSpec(
            num_scalar_prefetch=1,
            grid=(1,),
            in_specs=in_specs,
            out_specs=[at(w) for w in widths],
        ),
        out_shape=[jax.ShapeDtypeStruct((total, w), BF16) for w in widths],
        input_output_aliases=aliases,
        compiler_params=params("arbitrary"),
        cost_estimate=cost(
            flops=2 * rows * feats * cols * 3,
            bytes_accessed=2 * (feats * cols * 3 + rows * (2 * feats + 3 * cols)),
            transcendentals=0,
        ),
        name="qkv_chunk",
    )(places, *args)


def place_body(rels, idx, *refs):
    at = 0
    for rel, src in zip(rels, refs):
        rows = src.shape[0]
        refs[-1][idx[rel], at : at + rows, :] = src[...]
        at = (at + rows) % refs[-1].shape[1]


def place_chunks(places, chunks, count):
    rels = [rel % count for rel in rel_order(count) for _ in chunks[rel]]
    pieces = [c for rel in rel_order(count) for c in chunks[rel]]
    shape = (count,) + pieces[0].shape
    return pl.pallas_call(
        functools.partial(place_body, rels),
        grid_spec=pltpu.PrefetchScalarGridSpec(
            num_scalar_prefetch=1,
            grid=(1,),
            in_specs=[pl.BlockSpec(c.shape, lambda i, idx: (0, 0)) for c in pieces],
            out_specs=pl.BlockSpec(shape, lambda i, idx: (0, 0, 0)),
        ),
        out_shape=jax.ShapeDtypeStruct(shape, BF16),
        compiler_params=params("arbitrary"),
        name="place_chunks",
    )(places, *pieces)


def tn_cols_body(n, idx, a, b, send, keep):
    j = pl.program_id(0)
    out = dot_tn(a[...], b[...]).astype(BF16)

    @pl.when(j < n)
    def _():
        send[...] = out

    @pl.when(j >= n)
    def _():
        keep[...] = out


def half_place(n):
    return lambda j, idx: jnp.where(j < n, idx[0] * n + j, idx[1] * n + j - n)


def tn_cols(a, b):
    k, m = a.shape
    cols = b.shape[1]
    n = 2
    w = cols // (2 * n)
    at = half_place(n)
    return pl.pallas_call(
        functools.partial(tn_cols_body, n),
        grid_spec=pltpu.PrefetchScalarGridSpec(
            num_scalar_prefetch=1,
            grid=(2 * n,),
            in_specs=[
                pl.BlockSpec((k, m), lambda j, idx: (0, 0)),
                pl.BlockSpec((k, w), lambda j, idx: (0, at(j, idx))),
            ],
            out_specs=[
                pl.BlockSpec((m, w), lambda j, idx: (0, jnp.minimum(j, n - 1))),
                pl.BlockSpec((m, w), lambda j, idx: (0, jnp.maximum(j - n, 0))),
            ],
        ),
        out_shape=[jax.ShapeDtypeStruct((m, cols // 2), BF16)] * 2,
        compiler_params=params("arbitrary"),
        cost_estimate=cost(
            flops=2 * k * m * cols, bytes_accessed=2 * (k * m + k * cols + m * cols), transcendentals=0
        ),
        name="tn_cols",
    )(dp_side(1), a, b)


def pick_body(idx, src, out):
    out[...] = src[...]


def pick_rows(places, src):
    n = places.shape[0]
    rows, cols = src.shape[0] // n, src.shape[1]
    return pl.pallas_call(
        pick_body,
        grid_spec=pltpu.PrefetchScalarGridSpec(
            num_scalar_prefetch=1,
            grid=(n,),
            in_specs=[pl.BlockSpec((rows, cols), lambda j, idx: (idx[j], 0))],
            out_specs=pl.BlockSpec((rows, cols), lambda j, idx: (j, 0)),
        ),
        out_shape=jax.ShapeDtypeStruct(src.shape, src.dtype),
        compiler_params=params("arbitrary"),
        cost_estimate=cost(flops=0, bytes_accessed=4 * src.size, transcendentals=0),
        name="pick_rows",
    )(places, src)


def tn_whole_body(a, b, out):
    out[...] = dot_tn(a[...], b[...]).astype(BF16)


def tn_whole(a, b):
    k, m = a.shape
    cols = b.shape[1]
    w = cols // 4
    return pl.pallas_call(
        tn_whole_body,
        grid=(4,),
        in_specs=[
            pl.BlockSpec((k, m), lambda j: (0, 0)),
            pl.BlockSpec((k, w), lambda j: (0, j)),
        ],
        out_specs=pl.BlockSpec((m, w), lambda j: (0, j)),
        out_shape=jax.ShapeDtypeStruct((m, cols), BF16),
        compiler_params=params("arbitrary"),
        cost_estimate=cost(
            flops=2 * k * m * cols, bytes_accessed=2 * (k * m + k * cols + m * cols), transcendentals=0
        ),
        name="tn_whole",
    )(a, b)


def tn_rows_body(n, idx, a, b, w, send, keep, sums):
    j = pl.program_id(0)
    out = dot_tn(a[...], b[...])
    sums[...] = jnp.sum(out * w[...].astype(F32), axis=1, keepdims=True)

    @pl.when(j < n)
    def _():
        send[...] = out.astype(BF16)

    @pl.when(j >= n)
    def _():
        keep[...] = out.astype(BF16)


def tn_rows(a, b, w):
    k, m = a.shape
    cols = b.shape[1]
    n = 2
    blk = m // (2 * n)
    at = half_place(n)
    return pl.pallas_call(
        functools.partial(tn_rows_body, n),
        grid_spec=pltpu.PrefetchScalarGridSpec(
            num_scalar_prefetch=1,
            grid=(2 * n,),
            in_specs=[
                pl.BlockSpec((k, blk), lambda j, idx: (0, at(j, idx))),
                pl.BlockSpec((k, cols), lambda j, idx: (0, 0)),
                pl.BlockSpec((blk, cols), lambda j, idx: (at(j, idx), 0)),
            ],
            out_specs=[
                pl.BlockSpec((blk, cols), lambda j, idx: (jnp.minimum(j, n - 1), 0)),
                pl.BlockSpec((blk, cols), lambda j, idx: (jnp.maximum(j - n, 0), 0)),
                pl.BlockSpec((blk, 1), lambda j, idx: (at(j, idx), 0)),
            ],
        ),
        out_shape=[jax.ShapeDtypeStruct((m // 2, cols), BF16)] * 2
        + [jax.ShapeDtypeStruct((m, 1), F32)],
        compiler_params=params("arbitrary"),
        cost_estimate=cost(
            flops=2 * k * m * cols, bytes_accessed=2 * (k * m + k * cols + m * cols), transcendentals=0
        ),
        name="tn_rows",
    )(dp_side(1), a, b, w)


def half_add_body(idx, keep, got, send_out, keep_out):
    j = pl.program_id(0)
    out = (keep[...].astype(F32) + got[...].astype(F32)).astype(BF16)

    @pl.when(j == 0)
    def _():
        send_out[...] = out

    @pl.when(j == 1)
    def _():
        keep_out[...] = out


def half_add(keep, got, axis, side):
    shape = list(keep.shape)
    shape[axis] //= 2
    place = lambda j, idx: (0, idx[j]) if axis == 1 else (idx[j], 0)
    one = pl.BlockSpec(tuple(shape), lambda j, idx: (0, 0))
    src = pl.BlockSpec(tuple(shape), place)
    return pl.pallas_call(
        half_add_body,
        grid_spec=pltpu.PrefetchScalarGridSpec(
            num_scalar_prefetch=1, grid=(2,), in_specs=[src, src], out_specs=[one, one]
        ),
        out_shape=[jax.ShapeDtypeStruct(tuple(shape), BF16)] * 2,
        compiler_params=params("arbitrary"),
        cost_estimate=cost(flops=keep.size, bytes_accessed=6 * keep.size, transcendentals=0),
        name="half_add",
    )(side, keep, got)


def plain_add_body(a, b, out):
    out[...] = (a[...].astype(F32) + b[...].astype(F32)).astype(BF16)


def plain_add(a, b):
    rows, cols = a.shape
    blk = pl.BlockSpec((rows // 2, cols), lambda j: (j, 0))
    return pl.pallas_call(
        plain_add_body,
        grid=(2,),
        in_specs=[blk, blk],
        out_specs=blk,
        out_shape=jax.ShapeDtypeStruct(a.shape, BF16),
        compiler_params=params("arbitrary"),
        cost_estimate=cost(flops=a.size, bytes_accessed=6 * a.size, transcendentals=0),
        name="plain_add",
    )(a, b)


def ring_add_body(first, near, f, b, f_out, b_out):
    rows = f_out.shape[0]
    at = 0 if first else rows
    ahead, behind = near[at : at + rows, :].astype(F32), near[rows - at : 2 * rows - at, :].astype(F32)
    n = f.shape[0]
    f_out[:n, :] = (ahead[:n] + f[...].astype(F32)).astype(BF16)
    b_out[rows - n :, :] = (behind[rows - n :] + b[...].astype(F32)).astype(BF16)
    if n < rows:
        f_out[n:, :] = ahead[n:].astype(BF16)
        b_out[: rows - n, :] = behind[: rows - n].astype(BF16)


def ring_add(near, f, b, first, rows, at):
    cols = near.shape[1]
    whole = lambda a: pl.BlockSpec(a.shape, lambda i: (0, 0))
    return pl.pallas_call(
        functools.partial(ring_add_body, first),
        grid=(1,),
        in_specs=[pl.BlockSpec((2 * rows, cols), lambda i: (at, 0)), whole(f), whole(b)],
        out_specs=[pl.BlockSpec((rows, cols), lambda i: (0, 0))] * 2,
        out_shape=[jax.ShapeDtypeStruct((rows, cols), BF16)] * 2,
        compiler_params=params("arbitrary"),
        cost_estimate=cost(flops=near.size, bytes_accessed=8 * near.size, transcendentals=0),
        name="ring_add",
    )(near, f, b)


def grad_x_body(idx, rows, w, out):
    out[...] = dot_nt(rows[...], w[...]).astype(out.dtype)


def grad_x_terms(places, rels, d_joint, w_joint, rows, kind):
    feats, cols = w_joint.shape
    step = rels[-1] - rels[0]
    return pl.pallas_call(
        grad_x_body,
        grid_spec=pltpu.PrefetchScalarGridSpec(
            num_scalar_prefetch=1,
            grid=(len(rels),),
            in_specs=[
                pl.BlockSpec((rows, cols), lambda j, idx: (idx[rels[0] + j * step], 0)),
                pl.BlockSpec((feats, cols), lambda j, idx: (0, 0)),
            ],
            out_specs=pl.BlockSpec((rows, feats), lambda j, idx: (j, 0)),
        ),
        out_shape=jax.ShapeDtypeStruct((len(rels) * rows, feats), kind),
        compiler_params=params("arbitrary"),
        cost_estimate=cost(
            flops=2 * rows * feats * cols * len(rels), bytes_accessed=2 * feats * cols, transcendentals=0
        ),
        name="grad_x_terms",
    )(places, d_joint, w_joint)


def input_grad_body(own, f, b, mid, x_ref, gain, out):
    grad = own[...] + f[...].astype(F32) + b[...].astype(F32)
    x = x_ref[...].astype(F32)
    inverse = lax.rsqrt(jnp.mean(x * x, axis=-1, keepdims=True) + EPS)
    unit = x * inverse
    scaled = grad * gain[...]
    inner = jnp.mean(scaled * unit, axis=-1, keepdims=True)
    out[...] = (mid[...] + inverse * (scaled - unit * inner)).astype(BF16)


def input_grad_of(own, f, b, mid, tokens, gain):
    rows, feats = tokens.shape
    blk = pl.BlockSpec((rows // 2, feats), lambda i: (i, 0))
    return pl.pallas_call(
        input_grad_body,
        grid=(2,),
        in_specs=[blk] * 5 + [pl.BlockSpec((1, feats), lambda i: (0, 0))],
        out_specs=blk,
        out_shape=jax.ShapeDtypeStruct((rows, feats), BF16),
        compiler_params=params("arbitrary"),
        cost_estimate=cost(flops=9 * rows * feats, bytes_accessed=14 * rows * feats, transcendentals=0),
        name="input_grad",
    )(own, f, b, mid, tokens, gain.reshape(1, -1))


def shard_sum_body(n_back, units, pad, value, *refs):
    out = refs[-1]
    total = value[:units, :].astype(F32)
    for back in refs[:n_back]:
        total = total + back[...].astype(F32)
    out[...] = total.astype(BF16)


def shard_sum(value, backs, units):
    whole = lambda a: pl.BlockSpec(a.shape, lambda i: (0, 0))
    return pl.pallas_call(
        functools.partial(shard_sum_body, len(backs), units, 0),
        grid=(1,),
        in_specs=[whole(a) for a in (value, *backs)],
        out_specs=pl.BlockSpec((units, value.shape[1]), lambda i: (0, 0)),
        out_shape=jax.ShapeDtypeStruct((units, value.shape[1]), BF16),
        compiler_params=params("arbitrary"),
        cost_estimate=cost(flops=value.size, bytes_accessed=4 * value.size, transcendentals=0),
        name="shard_sum",
    )(value, *backs)


def widen_body(src, *outs):
    at = 0
    for out in outs:
        out[...] = src[0, :, at : at + out.shape[1]].astype(F32)
        at += out.shape[1]


def widen_pieces_body(n, idx, *refs):
    p = pl.program_id(0)
    outs = refs[n:]
    for i, src in enumerate(refs[:n]):

        @pl.when(p == i)
        def _():
            at = 0
            for out in outs:
                out[...] = src[:, at : at + out.shape[1]].astype(F32)
                at += out.shape[1]


def widen_pieces(places, pieces, widths):
    n = len(pieces)
    rows, cols = pieces[0].shape
    return pl.pallas_call(
        functools.partial(widen_pieces_body, n),
        grid_spec=pltpu.PrefetchScalarGridSpec(
            num_scalar_prefetch=1,
            grid=(n,),
            in_specs=[pl.BlockSpec((rows, cols), lambda p, idx: (0, 0))] * n,
            out_specs=[pl.BlockSpec((rows, w), lambda p, idx: (idx[p], 0)) for w in widths],
        ),
        out_shape=[jax.ShapeDtypeStruct((n * rows, w), F32) for w in widths],
        compiler_params=params("arbitrary"),
        name="widen_pieces",
    )(places, *pieces)


def widen_cols(got):
    n_dp, rows, cols = got.shape
    return pl.pallas_call(
        widen_body,
        grid=(n_dp,),
        in_specs=[pl.BlockSpec((1, rows, cols), lambda p: (part_of(p, n_dp), 0, 0))],
        out_specs=[pl.BlockSpec((rows, cols), lambda p: (0, p))],
        out_shape=[jax.ShapeDtypeStruct((rows, n_dp * cols), F32)],
        compiler_params=params("arbitrary"),
        name="widen_cols",
    )(got)[0]


def parts_ready(p, srcs, parts, sems):
    copies = [pltpu.make_async_copy(w, parts.at[i], sems.at[i]) for i, w in enumerate(srcs)]

    @pl.when(p == 0)
    def _():
        for c in copies:
            c.start()

    for i, c in enumerate(copies):

        @pl.when(p == i)
        def _():
            c.wait()


def out_body(n_dp, idx, heads, x_ref, gain, *refs):
    srcs, (branch_out, mid_out, h_out, heads_out, parts, sems) = refs[:n_dp], refs[n_dp:]
    p = pl.program_id(0)
    n_t, rows, cols = heads.shape
    width = parts.shape[2]
    parts_ready(p, srcs, parts, sems)

    @pl.when(p == 0)
    def _():
        for t in range(n_t):
            heads_out[:, t * cols : (t + 1) * cols] = heads[t]

    part = pl.ds(pl.multiple_of(idx[p] * width, width), width)
    branch_out[:, part] = dot_nn(heads_out[...], parts[p])

    @pl.when(p == n_dp - 1)
    def _():
        mid = x_ref[...].astype(F32) + branch_out[...]
        mid_out[...] = mid
        inverse = lax.rsqrt(jnp.mean(mid * mid, axis=-1, keepdims=True) + EPS)
        h_out[...] = (mid * inverse * gain[...]).astype(BF16)


def out_project(heads, w_places, w_parts, tokens, gain):
    n_dp = len(w_parts)
    feats_in, width = w_parts[0].shape
    rows, feats = tokens.shape
    full = lambda shape: pl.BlockSpec(shape, lambda p, idx: (0,) * len(shape))
    sq = (rows, feats)
    return pl.pallas_call(
        functools.partial(out_body, n_dp),
        grid_spec=pltpu.PrefetchScalarGridSpec(
            num_scalar_prefetch=1,
            grid=(n_dp,),
            in_specs=[full(heads.shape), full(sq), full((1, feats))] + [ANY] * n_dp,
            out_specs=[full(sq)] * 4,
            scratch_shapes=[
                pltpu.VMEM((n_dp, feats_in, width), BF16),
                pltpu.SemaphoreType.DMA((n_dp,)),
            ],
        ),
        out_shape=[
            jax.ShapeDtypeStruct(sq, F32),
            jax.ShapeDtypeStruct(sq, F32),
            jax.ShapeDtypeStruct(sq, BF16),
            jax.ShapeDtypeStruct((rows, feats_in), BF16),
        ],
        compiler_params=params("arbitrary"),
        cost_estimate=cost(
            flops=2 * rows * feats * feats_in,
            bytes_accessed=2 * feats * feats_in + 16 * rows * feats,
            transcendentals=0,
        ),
        name="out_project",
    )(w_places, heads, tokens, gain.reshape(1, -1), *w_parts)


def out_back_body(n_dp, idx, own, f, b, mid_ref, dy, gain, *refs):
    srcs, (mid_out, low_out, gain_out, heads_out, acc, parts, sems) = refs[:n_dp], refs[n_dp:]
    p = pl.program_id(0)
    n_t, rows, cols = heads_out.shape
    width = parts.shape[2]
    parts_ready(p, srcs, parts, sems)

    @pl.when(p == 0)
    def _():
        grad = own[...] + f[...].astype(F32) + b[...].astype(F32)
        mid = mid_ref[...]
        inverse = lax.rsqrt(jnp.mean(mid * mid, axis=-1, keepdims=True) + EPS)
        unit = mid * inverse
        gain_out[...] = jnp.sum(grad * unit, axis=0, keepdims=True)
        scaled = grad * gain[...]
        inner = jnp.mean(scaled * unit, axis=-1, keepdims=True)
        total = dy[...].astype(F32) + inverse * (scaled - unit * inner)
        mid_out[...] = total
        low_out[...] = total.astype(BF16)
        acc[...] = jnp.zeros_like(acc)

    part = pl.ds(pl.multiple_of(idx[p] * width, width), width)
    acc[...] += dot_nt(low_out[:, part], parts[p])

    @pl.when(p == n_dp - 1)
    def _():
        for t in range(n_t):
            heads_out[t] = acc[:, t * cols : (t + 1) * cols].astype(BF16)


def out_back(own, f, b, mid, dy, gain, w_places, w_parts, n_t):
    n_dp = len(w_parts)
    feats_in, width = w_parts[0].shape
    rows, feats = mid.shape
    full = lambda shape: pl.BlockSpec(shape, lambda p, idx: (0,) * len(shape))
    sq = (rows, feats)
    heads = (n_t, rows, feats_in // n_t)
    return pl.pallas_call(
        functools.partial(out_back_body, n_dp),
        grid_spec=pltpu.PrefetchScalarGridSpec(
            num_scalar_prefetch=1,
            grid=(n_dp,),
            in_specs=[full(sq)] * 5 + [full((1, feats))] + [ANY] * n_dp,
            out_specs=[full(sq), full(sq), full((1, feats)), full(heads)],
            scratch_shapes=[
                pltpu.VMEM((rows, feats_in), F32),
                pltpu.VMEM((n_dp, feats_in, width), BF16),
                pltpu.SemaphoreType.DMA((n_dp,)),
            ],
        ),
        out_shape=[
            jax.ShapeDtypeStruct(sq, F32),
            jax.ShapeDtypeStruct(sq, BF16),
            jax.ShapeDtypeStruct((1, feats), F32),
            jax.ShapeDtypeStruct(heads, BF16),
        ],
        compiler_params=params("arbitrary"),
        cost_estimate=cost(
            flops=2 * rows * feats * feats_in,
            bytes_accessed=2 * feats * feats_in + 20 * rows * feats,
            transcendentals=0,
        ),
        name="out_back",
    )(w_places, own, f, b, mid, dy, gain.reshape(1, -1), *w_parts)


def ffn_body(n_in, n_w, first, units, n_buf, *refs):
    hs, refs = refs[:n_in], refs[n_in:]
    ys, refs = refs[:n_in], refs[n_in:]
    srcs, refs = refs[:n_w], refs[n_w:]
    if first:
        refs = refs[n_buf:]
        h_out, y_out, refs = refs[0], refs[1], refs[2:]
    else:
        dh_in, refs = refs[0], refs[1 + n_buf :]
    hid_out, gg_out, gu_out, dh_ref, weights, sems = refs[:6]
    waits = []
    for j in range(3):
        if first:
            waits.append([pltpu.make_async_copy(srcs[j], weights.at[j], sems.at[j])])
            continue
        src = srcs[j]
        n_dp, _, width = src.shape
        waits.append(
            [
                pltpu.make_async_copy(
                    src.at[p], weights.at[j, :, pl.ds(p * width, width)], sems.at[j]
                )
                for p in range(n_dp)
            ]
        )
    for group in waits:
        for c in group:
            c.start()

    def ready(j):
        for c in waits[j]:
            c.wait()
        return weights[j]

    if not first:
        h_out, y_out = refs[6:]
    at = 0
    for h, y in zip(hs, ys):
        h_out[at : at + h.shape[0], :] = h[...]
        y_out[at : at + h.shape[0], :] = y[...]
        at += h.shape[0]
    gate = dot_nt(h_out[...], ready(0))
    up = dot_nt(h_out[...], ready(1))
    gh = dot_nt(y_out[...], ready(2))
    sig = jax.nn.sigmoid(gate)
    act = gate * sig
    hid_out[:, :units] = (act * up).astype(BF16)
    gg = (gh * up * (sig + act * (1.0 - sig))).astype(BF16)
    gu = (gh * act).astype(BF16)
    gg_out[:, :units] = gg
    gu_out[:, :units] = gu
    pad = hid_out.shape[1] - units
    if pad > 0:
        for o in (hid_out, gg_out, gu_out):
            o[:, units:] = jnp.zeros((o.shape[0], pad), BF16)
    part = dot_nn(gg, weights[0]) + dot_nn(gu, weights[1])
    if not first:
        part = part + dh_in[...]
    dh_ref[...] = part


def ffn_set(hs, ys, srcs, units, shard, shards, total, place, dh, bufs):
    n_in, n_w, first = len(hs), len(srcs), shard == 0
    feats = hs[0].shape[1]
    m = sum(h.shape[0] for h in hs)
    pad = -(-units // 128) * 128
    whole = lambda a: pl.BlockSpec(a.shape, lambda i: (0, 0))
    args = list(hs) + list(ys) + list(srcs)
    in_specs = [whole(a) for a in args[: 2 * n_in]] + [ANY] * n_w
    if not first:
        args.append(dh)
        in_specs.append(whole(dh))
    out_specs = [pl.BlockSpec((m, pad), lambda i: (place, shard))] * 3
    out_shape = [jax.ShapeDtypeStruct((total, pad * shards), BF16)] * 3
    held = list(bufs[2:])
    if first:
        out_specs = [pl.BlockSpec((m, feats), lambda i: (place, 0))] * 2 + out_specs
        out_shape = [jax.ShapeDtypeStruct((total, feats), BF16)] * 2 + out_shape
        held = list(bufs)
    aliases = {len(args) + i: i for i in range(len(held))}
    args += held
    in_specs += [ANY] * len(held)
    scratch = [pltpu.VMEM((3, units, feats), BF16), pltpu.SemaphoreType.DMA((3,))]
    if not first:
        scratch += [pltpu.VMEM((m, feats), BF16)] * 2
    out = pl.pallas_call(
        functools.partial(ffn_body, n_in, n_w, first, units, len(held)),
        grid=(1,),
        in_specs=in_specs,
        out_specs=out_specs + [pl.BlockSpec((m, feats), lambda i: (0, 0))],
        out_shape=out_shape + [jax.ShapeDtypeStruct((m, feats), F32)],
        scratch_shapes=scratch,
        input_output_aliases=aliases,
        compiler_params=params("arbitrary"),
        cost_estimate=cost(
            flops=10 * m * feats * units,
            bytes_accessed=6 * feats * units + 16 * m * feats,
            transcendentals=m * units,
        ),
        name="ffn_set",
    )(*args)
    new, dh = list(out[:-1]), out[-1]
    return (new if first else list(bufs[:2]) + new), dh


def down_body(n_got, units, hid, own, *refs):
    got, (out, weights, sems) = refs[:n_got], refs[n_got:]
    waits = [[pltpu.make_async_copy(own, weights.at[0], sems.at[0])]]
    for s, src in enumerate(got):
        n_dp, _, width = src.shape
        waits.append(
            [
                pltpu.make_async_copy(
                    src.at[p], weights.at[s + 1, :, pl.ds(p * width, width)], sems.at[s + 1]
                )
                for p in range(n_dp)
            ]
        )
    for group in waits:
        for c in group:
            c.start()
    pad = hid.shape[1] // (n_got + 1)
    total = None
    for s, group in enumerate(waits):
        for c in group:
            c.wait()
        part = dot_nn(hid[:, s * pad : s * pad + units], weights[s])
        total = part if total is None else total + part
    out[...] = total.astype(BF16)


def down_rows(hid, own, got):
    m = hid.shape[0]
    units, feats = own.shape
    n_w = len(got) + 1
    return pl.pallas_call(
        functools.partial(down_body, len(got), units),
        grid=(1,),
        in_specs=[pl.BlockSpec(hid.shape, lambda i: (0, 0))] + [ANY] * n_w,
        out_specs=pl.BlockSpec((m, feats), lambda i: (0, 0)),
        out_shape=jax.ShapeDtypeStruct((m, feats), BF16),
        scratch_shapes=[
            pltpu.VMEM((n_w, units, feats), BF16),
            pltpu.SemaphoreType.DMA((n_w,)),
        ],
        compiler_params=params("arbitrary"),
        cost_estimate=cost(
            flops=2 * m * units * feats * n_w,
            bytes_accessed=2 * units * feats * n_w + 6 * m * feats,
            transcendentals=0,
        ),
        name="down_rows",
    )(hid, own, *got)


LOG2E = 1.4426950408889634
SCALE = HEAD_DIM ** (-0.5)


def attend_body(q_ref, k0, k1, v0, v1, lo_ref, *rest):
    o_ref, ks, vs = rest[-3:]
    i = pl.program_id(1)
    span = Q_BLK + WINDOW

    @pl.when(i == 0)
    def _():
        ks[:WINDOW] = k0[...]
        ks[WINDOW:] = k1[...]
        vs[:WINDOW] = v0[...]
        vs[WINDOW:] = v1[...]

    start = pl.multiple_of(i * Q_BLK, Q_BLK)
    kb = ks[pl.ds(start, span), :]
    vb = vs[pl.ds(start, span), :]
    s = dot_nt(q_ref[...], kb) * (SCALE * LOG2E)
    col = lax.broadcasted_iota(jnp.int32, s.shape, 1)
    row = lax.broadcasted_iota(jnp.int32, s.shape, 0)
    lo = lo_ref[...] - start
    s = jnp.where((col >= lo) & (col <= row + WINDOW), s, NEG)
    p = jnp.exp2(s - jnp.max(s, axis=1, keepdims=True))
    total = jnp.sum(p, axis=1, keepdims=True)
    o = dot_nn(p.astype(BF16), vb) * (1.0 / total)
    o_ref[...] = o.astype(BF16)


def attend(half, q, pair, lo, buf):
    total, cols = q.shape
    heads = cols // HEAD_DIM
    rows = total // 2
    blocks = rows // Q_BLK
    base = half * blocks
    q_spec = pl.BlockSpec((Q_BLK, HEAD_DIM), lambda h, i: (base + i, h))
    key_spec = lambda b, c: pl.BlockSpec((WINDOW, HEAD_DIM), lambda h, i: (b, c + h))
    lo_spec = pl.BlockSpec((Q_BLK, 1), lambda h, i: (base + i, 0))
    in_specs = [
        q_spec,
        key_spec(pair[0][1], 0),
        key_spec(pair[1][1], 0),
        key_spec(pair[0][1], heads),
        key_spec(pair[1][1], heads),
        lo_spec,
    ]
    args = [q, pair[0][0], pair[1][0], pair[0][0], pair[1][0], lo]
    aliases = {}
    if buf is not None:
        in_specs.append(pl.BlockSpec(memory_space=pl.ANY))
        args.append(buf)
        aliases = {6: 0}
    return pl.pallas_call(
        attend_body,
        grid=(heads, blocks),
        in_specs=in_specs,
        out_specs=q_spec,
        out_shape=jax.ShapeDtypeStruct((total, cols), BF16),
        scratch_shapes=[pltpu.VMEM((2 * WINDOW, HEAD_DIM), BF16)] * 2,
        input_output_aliases=aliases,
        compiler_params=params("arbitrary", "arbitrary"),
        cost_estimate=cost(
            flops=4 * rows * (Q_BLK + WINDOW) * cols,
            bytes_accessed=2 * cols * 6 * WINDOW,
            transcendentals=rows * (Q_BLK + WINDOW) * heads,
        ),
        name="attend",
    )(*args)


def attend_back_body(q_ref, g_ref, k0, k1, v0, v1, lo_ref, cos_ref, sin_ref, *rest):
    dq_ref, dk_ref, dv_ref, ks, vs = rest[-5:]
    i = pl.program_id(1)
    span = Q_BLK + WINDOW

    @pl.when(i == 0)
    def _():
        ks[:WINDOW] = k0[...]
        ks[WINDOW:] = k1[...]
        vs[:WINDOW] = v0[...]
        vs[WINDOW:] = v1[...]
        dk_ref[...] = jnp.zeros_like(dk_ref)
        dv_ref[...] = jnp.zeros_like(dv_ref)

    start = pl.multiple_of(i * Q_BLK, Q_BLK)
    kb = ks[pl.ds(start, span), :]
    vb = vs[pl.ds(start, span), :]
    q, g = q_ref[...], g_ref[...]
    s = dot_nt(kb, q) * (SCALE * LOG2E)
    key = lax.broadcasted_iota(jnp.int32, s.shape, 0)
    row = lax.broadcasted_iota(jnp.int32, s.shape, 1)
    lo = lo_ref[...] - start
    s = jnp.where((key >= lo) & (key <= row + WINDOW), s, NEG)
    p = jnp.exp2(s - jnp.max(s, axis=0, keepdims=True))
    p = p * (1.0 / jnp.sum(p, axis=0, keepdims=True))
    dp = dot_nt(vb, g)
    inner = jnp.sum(p * dp, axis=0, keepdims=True)
    ds = (p * (dp - inner)).astype(BF16)
    dq = dot_tn(ds, kb) * SCALE
    dq = dq * cos_ref[...] - pltpu.roll(dq, HEAD_DIM // 2, 1) * sin_ref[...]
    dq_ref[...] = dq.astype(BF16)
    dk_ref[pl.ds(start, span), :] += dot_nn(ds, q) * SCALE
    dv_ref[pl.ds(start, span), :] += dot_nn(p.astype(BF16), g)


def attend_back(half, q, g, pair, lo_row, cos, sin, buf):
    total, cols = q.shape
    heads = cols // HEAD_DIM
    rows = total // 2
    blocks = rows // Q_BLK
    base = half * blocks
    q_spec = pl.BlockSpec((Q_BLK, HEAD_DIM), lambda h, i: (base + i, h))
    key_spec = lambda b, c: pl.BlockSpec((WINDOW, HEAD_DIM), lambda h, i: (b, c + h))
    rope_spec = pl.BlockSpec((Q_BLK, HEAD_DIM), lambda h, i: (base + i, 0))
    lo_spec = pl.BlockSpec((1, Q_BLK), lambda h, i: (0, base + i))
    grad_spec = pl.BlockSpec((2 * WINDOW, HEAD_DIM), lambda h, i: (0, h))
    in_specs = [
        q_spec,
        q_spec,
        key_spec(pair[0][1], 0),
        key_spec(pair[1][1], 0),
        key_spec(pair[0][1], heads),
        key_spec(pair[1][1], heads),
        lo_spec,
        rope_spec,
        rope_spec,
    ]
    args = [q, g, pair[0][0], pair[1][0], pair[0][0], pair[1][0], lo_row, cos, sin]
    aliases = {}
    if buf is not None:
        in_specs.append(pl.BlockSpec(memory_space=pl.ANY))
        args.append(buf)
        aliases = {9: 0}
    return pl.pallas_call(
        attend_back_body,
        grid=(heads, blocks),
        in_specs=in_specs,
        out_specs=[
            pl.BlockSpec((Q_BLK, HEAD_DIM), lambda h, i: (base + i, 2 * heads + h)),
            grad_spec,
            grad_spec,
        ],
        out_shape=[
            jax.ShapeDtypeStruct((total, 3 * cols), BF16),
            jax.ShapeDtypeStruct((2 * WINDOW, cols), F32),
            jax.ShapeDtypeStruct((2 * WINDOW, cols), F32),
        ],
        scratch_shapes=[pltpu.VMEM((2 * WINDOW, HEAD_DIM), BF16)] * 2,
        input_output_aliases=aliases,
        compiler_params=params("arbitrary", "arbitrary"),
        cost_estimate=cost(
            flops=10 * rows * (Q_BLK + WINDOW) * cols,
            bytes_accessed=2 * cols * 14 * WINDOW,
            transcendentals=rows * (Q_BLK + WINDOW) * heads,
        ),
        name="attend_back",
    )(*args)


def finish_body(half, ak, av, ok, ov, cos_ref, sin_ref, _, out_ref):
    cols = ak.shape[1]

    def write(gk, gv):
        for h in range(cols // HEAD_DIM):
            c = slice(h * HEAD_DIM, (h + 1) * HEAD_DIM)
            seg = gk[:, c]
            seg = seg * cos_ref[...] - pltpu.roll(seg, HEAD_DIM // 2, 1) * sin_ref[...]
            out_ref[:, c] = seg.astype(BF16)
        out_ref[:, cols:] = gv.astype(BF16)

    write(ak[...] + ok[...].astype(F32), av[...] + ov[...].astype(F32))


def finish_keys(half, ak, av, other_k, other_v, cos, sin, buf):
    cols = ak.shape[1]
    blk = 512
    n = WINDOW // blk
    base = half * n
    own = pl.BlockSpec((blk, cols), lambda i: (base + i, 0))
    oth = lambda o: pl.BlockSpec((blk, cols), lambda i: (o[1] * n + i, o[2]))
    rope = pl.BlockSpec((blk, HEAD_DIM), lambda i: (base + i, 0))
    return pl.pallas_call(
        functools.partial(finish_body, half),
        grid=(n,),
        in_specs=[own, own, oth(other_k), oth(other_v), rope, rope, ANY],
        out_specs=pl.BlockSpec((blk, 2 * cols), lambda i: (base + i, 0)),
        out_shape=jax.ShapeDtypeStruct(buf.shape, BF16),
        input_output_aliases={6: 0},
        compiler_params=params("arbitrary"),
        name="finish_keys",
    )(ak, av, other_k[0], other_v[0], cos, sin, buf)


def shards(
    tokens, segments, attn_gain, ffn_gain, w_query, w_key, w_value, w_out, w_gate, w_up, w_down, cotangent
):
    rows, feats = tokens.shape
    n_tensor = lax.axis_size("tensor")
    n_dp = lax.axis_size("dp")
    block_len = rows * n_tensor
    head_cols = w_query.shape[1]
    units = w_gate.shape[1]
    unit_pad = -(-units // 128) * 128
    dp_idx, t_idx = lax.axis_index("dp"), lax.axis_index("tensor")
    first_pos = dp_idx * block_len
    ring = [ring_cycle(n_tensor)]
    square = group_cycles(n_tensor)
    groups = n_tensor // GROUP
    far = n_tensor // 2
    part_cols = feats // n_dp
    own_w = (w_gate.T, w_up.T, w_down)

    def to_group(piece, s):
        pairs = [(t, (t + s * GROUP) % n_tensor) for t in range(n_tensor)]
        return lax.ppermute(piece, "tensor", pairs)

    def dp_cols(value):
        return lax.dynamic_slice_in_dim(value, dp_idx * part_cols, part_cols, 1)

    ring_owners = owners(ring)
    ring_pairs = owners(ring, [r for k in range(far - 1, 0, -1) for r in (k, -k)] + [far, 0])
    x_f = tokens.astype(F32)
    x_normed, x_unit, x_inv = norm_forward(x_f, attn_gain)
    x_low = x_normed.astype(BF16)
    go = Gather(dp_cols(w_out), ring)
    w_joint = jnp.concatenate([w_key, w_value, w_query], axis=1)
    gx = Gather(x_low, ring)
    gx.step()
    go.step(x_low)
    cos, sin = rope_tables(first_pos + jnp.arange(block_len, dtype=jnp.int32))
    cos, sin = after(cos, w_joint, x_low), after(sin, w_joint)

    def qkv(rel, bufs):
        return qkv_chunk(
            ring_owners, rel % n_tensor, gx.chunks[rel], w_query, w_key, w_value, cos, sin, bufs
        )

    bufs = qkv(0, None)
    for k in range(1, far + 1):
        gx.f, gx.b, go.f, go.b, bufs = together(gx.f, gx.b, go.f, go.b, tuple(bufs))
        if k == far:
            break
        if k == 1:
            seg_tail = after(segments[block_len - WINDOW :].astype(F32), gx.f, gx.b)
            prev_seg = shifted(seg_tail, "dp", 1).astype(jnp.int32)
        gx.step()
        go.step()
        bufs = qkv(k, qkv(-k, bufs))
    w_out_part = place_chunks(after(ring_owners, go.f, go.b), go.chunks, n_tensor)
    w_out_part = w_out_part.reshape(n_tensor * head_cols, part_cols)
    low_bits = bits_of(n_dp)
    w_spread = spread_parts([(0, w_out_part)], low_bits[-1:])

    seg_all = jnp.concatenate([prev_seg, segments], axis=0)
    low_key = jnp.sum((seg_all[None, :] < segments[:, None]).astype(jnp.int32), axis=1)
    low_key = jnp.where(dp_idx == 0, jnp.maximum(low_key, WINDOW), low_key)
    spot = jnp.arange(block_len, dtype=jnp.int32)
    low_key = jnp.maximum(low_key, spot + 1)
    low_key = low_key - jnp.where(spot >= block_len // 2, block_len // 2, 0)
    low_col, low_row = low_key[:, None], low_key[None, :]

    came = (gx.f, gx.b)
    mine, low_col, low_row = together(tuple(dp_cols(w) for w in own_w), low_col, low_row)
    first = after(mine[0], *came)
    gate_got = [to_group(first, s) for s in range(1, groups)]
    bufs = list(bufs)
    bufs[0] = after(bufs[0], low_col, low_row, first, w_out_part)
    bufs = qkv(far, bufs)
    query, key_value, x_all = bufs
    tail_kv = after(key_value[block_len - WINDOW :])
    prev = shifted(tail_kv, "dp", 1)
    gy = Gather(after(cotangent, *came), square)
    gy.step()

    late = ((key_value, 0), (key_value, 1))
    heads_late = attend(1, query, late, low_col, None)
    heads_late, prev, gy.f, gy.b = together(heads_late, prev, gy.f, gy.b)
    early = ((prev, 0), (key_value, 0))
    heads_low = attend(0, query, early, low_col, heads_late)
    heads_low = heads_low.reshape(n_tensor, rows, head_cols)
    w_first = w_spread[-1][1]
    heads_low, w_first, *gate_got = together(heads_low, w_first, *gate_got)
    w_spread[-1] = (w_spread[-1][0], w_first)

    heads_got = lax.all_to_all(heads_low, "tensor", split_axis=0, concat_axis=0, tiled=True)
    w_spread = spread_parts(w_spread, low_bits[:-1], heads_low)
    w_places = jnp.stack([dp_idx ^ x for x, _ in w_spread]).astype(jnp.int32)
    heads_got, *w_out_parts = together(heads_got, *[w for _, w in w_spread])
    second = after(mine[1], heads_got)
    up_got = [to_group(second, s) for s in range(1, groups)]
    gate_all_got = [all_dp(after(g, heads_low)) for g in gate_got]
    gy.step(heads_got)
    y_chunks = gy.chunks
    attn_branch, mid, h_low, my_heads = out_project(
        heads_got, w_places, w_out_parts, tokens, ffn_gain
    )

    gh = Gather(h_low, square)
    sets = {0: ([0], 2), 1: ([-1, 1], 0), 2: ([2], 3)}
    ffn_bufs, dhs = [], {}

    def ffn(i, shard, *deps):
        rels, place = sets[i]
        hs = [c for r in rels for c in gh.chunks[r]]
        ys = [c for r in rels for c in y_chunks[r]]
        srcs = own_w if shard == 0 else got[shard - 1]
        hs[0] = after(hs[0], *deps)
        return ffn_set(
            hs, ys, srcs, units, shard, groups, GROUP * rows, place, dhs.get(i), ffn_bufs
        )

    gh.step()
    ffn_bufs, dhs[0] = ffn(0, 0)
    third = after(mine[2], h_low, *up_got)
    down_got = [to_group(third, s) for s in range(1, groups)]
    came = (*gh.chunks[1], *gh.chunks[-1], *gate_all_got)
    up_all_got = [all_dp(after(g, dhs[0], *came)) for g in up_got]
    gh.step(dhs[0])
    ffn_bufs, dhs[1] = ffn(1, 0)
    came = (*gh.chunks[2], *y_chunks[2], *up_all_got)
    down_all_got = [all_dp(after(d, dhs[1], *came)) for d in down_got]
    got = list(zip(gate_all_got, up_all_got, down_all_got))
    ffn_bufs, dhs[2] = ffn(2, 0)
    for s in range(1, groups):
        ffn_bufs, dhs[2] = ffn(2, s)
    sh = Scatter(dhs[2].astype(BF16), square)
    for s in range(1, groups):
        ffn_bufs, dhs[1] = ffn(1, s, *sh.sent)
    sh.step(dhs[1], False)
    for s in range(1, groups):
        ffn_bufs, dhs[0] = ffn(0, s, *sh.sent)
    h_all, y_all, hid_all, gate_all, up_all = ffn_bufs

    def send_back(red, *deps):
        cut = lambda s: red.value[s * unit_pad : s * unit_pad + units]
        return [to_group(after(cut(s), *deps), groups - s) for s in range(1, groups)]

    red_down = Halves(*tn_cols(hid_all, y_all), 1)
    red_down.send()
    red_gate = Halves(*tn_cols(after(gate_all, red_down.sent), h_all), 1)
    sh.f, sh.b, dhs[0], red_down.got, red_gate.sent = together(
        sh.f, sh.b, dhs[0], red_down.got, red_gate.sent
    )
    grad_mid, grad_mid_low, grad_ffn_gain, my_grad_heads = out_back(
        dhs[0], sh.f, sh.b, mid, cotangent, ffn_gain, w_places, w_out_parts, n_tensor
    )
    grad_heads = lax.all_to_all(
        my_grad_heads, "tensor", split_axis=0, concat_axis=0, tiled=True
    ).reshape(block_len, head_cols)

    red_down.add()
    red_down.send(my_grad_heads)
    red_gate.send(red_down.sent)
    sf_all = down_rows(after(hid_all, red_down.sent), own_w[2], [g[2] for g in got])
    red_up = Halves(*tn_cols(after(up_all, red_down.sent), h_all), 1)
    grad_heads, red_down.got, red_gate.got, sf_all, red_up.sent = together(
        grad_heads, red_down.got, red_gate.got, sf_all, red_up.sent
    )
    red_down.finish()
    down_back = send_back(red_down)
    red_gate.add()
    red_gate.send()
    red_up.send()
    sf = Scatter(sf_all[3 * rows :], square)

    grad_heads = after(grad_heads, red_down.value, *sf.sent, red_gate.sent)
    d_joint, bk, bv = attend_back(0, query, grad_heads, early, low_row, cos, sin, None)
    d_joint, bk, bv, sf.f, sf.b, red_up.got, red_gate.got, *down_back = together(
        d_joint, bk, bv, sf.f, sf.b, red_up.got, red_gate.got, *down_back
    )
    red_gate.finish()
    gate_back = send_back(red_gate)
    back = after(jnp.concatenate([bk[:WINDOW], bv[:WINDOW]], axis=1).astype(BF16))
    got_back = shifted(back, "dp", -1)
    sf.step(after(sf_all, back), False)
    red_up.add()
    red_up.send(back)
    d_joint, ak, av = attend_back(
        1, query, after(grad_heads, back, *sf.sent, red_up.sent, red_gate.value),
        late, low_row, cos, sin, d_joint,
    )
    d_joint, ak, av, got_back, sf.f, sf.b, red_up.got, *gate_back = together(
        d_joint, ak, av, got_back, sf.f, sf.b, red_up.got, *gate_back
    )
    out_local = tn_whole(my_heads, after(grad_mid_low, ak))
    out_dp = lax.psum_scatter(out_local, "dp", scatter_dimension=1, tiled=True)
    ak = after(ak, out_local)
    d_joint = finish_keys(0, ak, av, (bk, 1, 0), (bv, 1, 0), cos, sin, d_joint)
    d_joint = finish_keys(1, ak, av, (got_back, 0, 0), (got_back, 0, 1), cos, sin, d_joint)

    def terms(rels, kind, *deps):
        rels = [r % n_tensor for r in rels]
        return grad_x_terms(after(ring_owners, *deps), rels, d_joint, w_joint, rows, kind)

    red_up.finish(out_local)
    up_back = send_back(red_up)
    sx = Scatter(after(terms([far], BF16), red_up.value), ring)
    near = terms([far - 1, 1 - far], F32, red_up.value)
    down_own = shard_sum(after(red_down.value, red_up.value), down_back, units)
    down_dp = all_dp(down_own)
    gate_own = shard_sum(after(red_gate.value, down_own), gate_back, units)
    gate_dp = all_dp(gate_own)
    joint = tn_rows(after(x_all, *sx.sent), d_joint, w_joint)
    grad_attn_gain = joint[2][:, 0] / attn_gain
    ffn_branch = after(sf_all[2 * rows : 3 * rows], *sx.sent).astype(F32)
    ffn_branch = ffn_branch + sf.f.astype(F32) + sf.b.astype(F32)
    result = mid + ffn_branch
    slots = 2 * n_dp + 1
    own_seg = lax.dynamic_slice_in_dim(segments, t_idx * rows, rows)
    one_hot = (own_seg[:, None] == jnp.arange(slots, dtype=jnp.int32)[None, :]).astype(F32)
    per_row = jnp.stack(
        [
            jnp.sum(result * result, axis=1),
            jnp.sum(attn_branch * attn_branch, axis=1),
            jnp.sum(ffn_branch * ffn_branch, axis=1),
            jnp.ones((rows,), F32),
        ],
        axis=1,
    )
    table = jnp.dot(per_row.T, one_hot, precision=lax.Precision.HIGHEST, preferred_element_type=F32)
    packed = jnp.concatenate([grad_attn_gain, grad_ffn_gain[0], table.reshape(-1)])
    packed = jnp.pad(packed, (0, -packed.shape[0] % 1024)).reshape(-1, 128)
    sx.f, sx.b, near, down_own, gate_own, joint, packed, out_dp, *up_back = together(
        sx.f, sx.b, near, down_own, gate_own, tuple(joint), packed, out_dp, *up_back
    )
    red_joint = Halves(*joint[:2], 0)
    red_joint.send()
    far_out = lax.dynamic_slice_in_dim(out_dp, ring_owners[far] * head_cols, head_cols)
    so = Scatter(far_out, ring)
    todo = hops()
    hop = swap(after(packed, red_joint.got), *todo[0])
    sx.step(near, True)
    up_own = shard_sum(after(red_up.value, *sx.sent), up_back, units)
    up_dp = all_dp(up_own)
    near = terms([far - 2, 2 - far], F32, up_own)
    picked = pick_rows(after(ring_pairs, near), out_dp)
    sx.f, sx.b, near, red_joint.got, up_own, picked, hop, so.f, so.b = together(
        sx.f, sx.b, near, red_joint.got, up_own, picked, hop, so.f, so.b
    )
    packed = packed + hop
    so.step(picked, True, at=0)
    red_joint.add()
    red_joint.send()
    sx.step(near, True, red_joint.sent)
    near = terms([far - 3, 3 - far], F32, *sx.sent)
    grad_w_down = widen_cols(after(down_dp, near))
    sx.f, sx.b, near, red_joint.got, grad_w_down, so.f, so.b = together(
        sx.f, sx.b, near, red_joint.got, grad_w_down, so.f, so.b
    )
    so.step(picked, True, at=1)
    sx.step(near, True)
    for k in range(far - 4, 0, -1):
        sx.step(terms([k, -k], F32, *sx.sent), True)
    red_joint.finish()
    joint_parts = spread_parts([(0, red_joint.value)], low_bits[-1:])
    grad_w_gate = widen_cols(after(gate_dp, red_joint.value)).T
    own = terms([0], F32, grad_w_gate)
    sx.f, sx.b, own, so.f, so.b, joint_first = together(
        sx.f, sx.b, own, so.f, so.b, joint_parts[-1][1]
    )
    joint_parts[-1] = (joint_parts[-1][0], joint_first)
    joint_parts = spread_parts(joint_parts, low_bits[:-1][::-1])
    joint_places = jnp.stack([place_of(dp_idx ^ x, n_dp) for x, _ in joint_parts])
    for i in range(2, far - 1):
        so.step(picked, True, at=i)
    for axis, bit in todo[1:]:
        packed = packed + swap(after(packed, sx.f, sx.b), axis, bit)
    out_own = picked[-head_cols:].astype(F32) + so.f.astype(F32) + so.b.astype(F32)
    out_all = all_dp(out_own.astype(BF16))
    input_grad = input_grad_of(own, sx.f, sx.b, grad_mid, tokens, attn_gain)
    grad_w_out = jnp.concatenate(list(out_all), axis=1).astype(F32)
    grad_w_key, grad_w_value, grad_w_query = widen_pieces(
        joint_places.astype(jnp.int32), [v for _, v in joint_parts], [head_cols] * 3
    )
    grad_w_up = widen_cols(up_dp).T

    packed = packed.reshape(-1)
    sums = packed[2 * feats : 2 * feats + 4 * slots].reshape(4, slots)
    doc_rms = jnp.sqrt(sums[:3] / (jnp.maximum(sums[3:], 1.0) * feats))

    return (
        result.astype(BF16),
        input_grad,
        packed[:feats],
        packed[feats : 2 * feats],
        grad_w_query,
        grad_w_key,
        grad_w_value,
        grad_w_out,
        grad_w_gate,
        grad_w_up,
        grad_w_down,
        doc_rms,
    )


def solution(mesh):
    both = P(("dp", "tensor"), None)
    col, row = P(None, "tensor"), P("tensor", None)
    return jax.shard_map(
        shards,
        mesh=mesh,
        in_specs=(both, P("dp"), P(), P(), col, col, col, row, col, col, row, both),
        out_specs=(both, both, P(), P(), col, col, col, row, col, col, row, P()),
        check_vma=False,
    )
```

```python
import functools
import math

import jax
import jax.numpy as jnp
from jax import lax
from jax.experimental import pallas as pl
from jax.experimental.pallas import tpu as pltpu
from jax.sharding import PartitionSpec as P

HEAD_DIM = 128
WINDOW = 1024
EPS = 1e-06
NEG = -1e30
F32 = jnp.float32
BF16 = jnp.bfloat16
Q_BLK = 256
COST_PART = 16
GROUP = 4


def ring_cycle(count):
    if count == 8:
        return [0, 2, 4, 6, 7, 5, 3, 1]
    width = 4 if count % 4 == 0 else count
    order = []
    for row in range(count // width):
        part = list(range(row * width, (row + 1) * width))
        order += part if row % 2 == 0 else part[::-1]
    return order


def group_cycles(count):
    base = [0, 2, 3, 1] if count == 8 else list(range(GROUP))
    return [[g * GROUP + b for b in base] for g in range(count // GROUP)]


def step_pairs(cycles, step):
    return [
        (cyc[i], cyc[(i + step) % len(cyc)]) for cyc in cycles for i in range(len(cyc))
    ]


def owners(cycles, rels=None):
    table = {}
    for cyc in cycles:
        for i, dev in enumerate(cyc):
            steps = range(len(cyc)) if rels is None else rels
            table[dev] = [cyc[(i + rel) % len(cyc)] for rel in steps]
    rows = jnp.array([table[t] for t in range(len(table))], jnp.int32)
    return rows[lax.axis_index("tensor")]


def rel_order(size):
    order = [0]
    for k in range(1, size // 2):
        order += [-k, k]
    return order + [size // 2]


def after(value, *deps):
    return lax.optimization_barrier((value,) + deps)[0]


def together(*values):
    return lax.optimization_barrier(values)


class Gather:
    def __init__(self, own, cycles):
        self.size = len(cycles[0])
        self.ahead, self.back = step_pairs(cycles, 1), step_pairs(cycles, -1)
        self.f = self.b = own
        self.chunks = {0: [own]}
        self.k = 0

    def step(self, *deps):
        self.k += 1
        f, b = lax.optimization_barrier((self.f, self.b) + deps)[:2]
        if self.k < self.size // 2:
            self.f = lax.ppermute(f, "tensor", self.ahead)
            self.b = lax.ppermute(b, "tensor", self.back)
            self.chunks[-self.k], self.chunks[self.k] = [self.f], [self.b]
        else:
            half = self.f.shape[0] // 2
            self.f = lax.ppermute(f[:half], "tensor", self.ahead)
            self.b = lax.ppermute(b[half:], "tensor", self.back)
            self.chunks[self.k] = [self.f, self.b]

    def all(self):
        while self.k < self.size // 2:
            self.step()
        return self.chunks


class Scatter:
    def __init__(self, far, cycles):
        self.size = len(cycles[0])
        self.ahead, self.back = step_pairs(cycles, 1), step_pairs(cycles, -1)
        self.k = self.size // 2
        half = self.half = far.shape[0] // 2
        self.sent = lax.optimization_barrier((far[:half], far[half:]))
        self.send()

    def send(self):
        self.f = lax.ppermute(self.sent[0], "tensor", self.ahead)
        self.b = lax.ppermute(self.sent[1], "tensor", self.back)

    def step(self, near, first, *deps, at=0):
        f, b, near = lax.optimization_barrier((self.f, self.b, near) + deps)[:3]
        self.k -= 1
        self.sent = ring_add(near, f, b, first, 2 * self.half, at)
        self.send()


def bits_of(count):
    bit, out = 1, []
    while bit < count:
        out.append(bit)
        bit *= 2
    return out


def swap(value, axis, bit):
    count = lax.axis_size(axis)
    return lax.ppermute(value, axis, [(d, d ^ bit) for d in range(count)])


class Halves:
    def __init__(self, send, keep, axis):
        self.sent, self.keep, self.axis = send, keep, axis
        self.bits = bits_of(lax.axis_size("dp"))

    def send(self, *deps):
        self.sent = after(self.sent, *deps)
        self.got = swap(self.sent, "dp", self.bits[0])

    def add(self, *deps):
        got = after(self.got, *deps)
        self.bits = self.bits[1:]
        if self.bits:
            pair = half_add(self.keep, got, self.axis, dp_side(self.bits[0]))
            self.sent, self.keep = pair
            return self.keep
        self.value = plain_add(self.keep, got)
        return self.value

    def finish(self, *deps):
        self.add(*deps)
        while self.bits:
            self.send()
            self.add()
        return self.value


def dp_side(bit):
    side = (lax.axis_index("dp") // bit) % 2
    return jnp.stack([1 - side, side]).astype(jnp.int32)


def place_of(device, count):
    place = 0
    for bit in bits_of(count):
        place = place * 2 + (device // bit) % 2
    return place


def part_of(place, count):
    device = 0
    for bit in bits_of(count):
        device = device * 2 + place % 2
        place = place // 2
    return device


def all_dp(value):
    return lax.all_gather(value, "dp", axis=0, tiled=False)


def spread_parts(out, bits, *deps):
    for bit in bits:
        out = out + [(x ^ bit, swap(after(v, *deps), "dp", bit)) for x, v in out]
    return out


def hops():
    return [(a, bit) for a in ("tensor", "dp") for bit in bits_of(lax.axis_size(a))]


def shifted(value, axis, steps):
    count = lax.axis_size(axis)
    leading, last = max(0, -steps), min(count, count - steps)
    return lax.ppermute(value, axis, [(s, s + steps) for s in range(leading, last)])


def norm_forward(values, gain):
    inverse = lax.rsqrt(jnp.mean(values * values, axis=-1, keepdims=True) + EPS)
    unit = values * inverse
    return unit * gain, unit, inverse


def norm_backward(grad, unit, inverse, gain):
    scaled = grad * gain
    inner = jnp.mean(scaled * unit, axis=-1, keepdims=True)
    return inverse * (scaled - unit * inner)


def dot_nn(a, b):
    return jnp.dot(a, b, preferred_element_type=F32)


def dot_tn(a, b):
    return lax.dot_general(a, b, (((0,), (0,)), ((), ())), preferred_element_type=F32)


def dot_nt(a, b):
    return lax.dot_general(a, b, (((1,), (1,)), ((), ())), preferred_element_type=F32)


def rope_tables(positions):
    half = HEAD_DIM // 2
    freq = jnp.exp(jnp.arange(half, dtype=F32) * (-2.0 * math.log(10000.0) / HEAD_DIM))
    angles = positions.astype(F32)[:, None] * freq[None, :]
    cos, sin = jnp.cos(angles), jnp.sin(angles)
    return jnp.concatenate([cos, cos], axis=1), jnp.concatenate([-sin, sin], axis=1)


def cost(flops, bytes_accessed, transcendentals):
    return pl.CostEstimate(
        flops=flops // COST_PART,
        bytes_accessed=bytes_accessed // COST_PART,
        transcendentals=transcendentals // COST_PART,
    )


def params(*sem):
    return pltpu.CompilerParams(
        dimension_semantics=sem or None, vmem_limit_bytes=56 * 1024 * 1024
    )


ANY = pl.BlockSpec(memory_space=pl.ANY)


def qkv_body(n_in, idx, *refs):
    xs, refs = refs[:n_in], refs[n_in:]
    wq, wk, wv, cos_ref, sin_ref = refs[:5]
    q_out, kv_out, x_out = refs[-3:]
    at = 0
    for x in xs:
        x_out[at : at + x.shape[0], :] = x[...]
        at += x.shape[0]
    x = x_out[...]
    cos, sin = cos_ref[...], sin_ref[...]
    cols = wq.shape[1]
    for w, out in ((wq, q_out), (wk, kv_out)):
        p = dot_nn(x, w[...])
        for h in range(cols // HEAD_DIM):
            c = slice(h * HEAD_DIM, (h + 1) * HEAD_DIM)
            seg = p[:, c]
            out[:, c] = (seg * cos + pltpu.roll(seg, HEAD_DIM // 2, 1) * sin).astype(BF16)
    kv_out[:, cols:] = dot_nn(x, wv[...]).astype(BF16)


def qkv_chunk(places, rel, xs, wq, wk, wv, cos, sin, bufs):
    rows = sum(x.shape[0] for x in xs)
    feats, cols = wq.shape
    total = cos.shape[0]
    n_in = len(xs)
    full = lambda a: pl.BlockSpec(a.shape, lambda i, idx: (0, 0))
    at = lambda width: pl.BlockSpec((rows, width), lambda i, idx: (idx[rel], 0))
    args = list(xs) + [wq, wk, wv, cos, sin]
    in_specs = [full(a) for a in args[:-2]] + [at(HEAD_DIM)] * 2
    aliases = {}
    if bufs is not None:
        aliases = {1 + len(args) + i: i for i in range(3)}
        in_specs += [ANY] * 3
        args += list(bufs)
    widths = (cols, 2 * cols, feats)
    return pl.pallas_call(
        functools.partial(qkv_body, n_in),
        grid_spec=pltpu.PrefetchScalarGridSpec(
            num_scalar_prefetch=1,
            grid=(1,),
            in_specs=in_specs,
            out_specs=[at(w) for w in widths],
        ),
        out_shape=[jax.ShapeDtypeStruct((total, w), BF16) for w in widths],
        input_output_aliases=aliases,
        compiler_params=params("arbitrary"),
        cost_estimate=cost(
            flops=2 * rows * feats * cols * 3,
            bytes_accessed=2 * (feats * cols * 3 + rows * (2 * feats + 3 * cols)),
            transcendentals=0,
        ),
        name="qkv_chunk",
    )(places, *args)


def place_body(rels, idx, *refs):
    at = 0
    for rel, src in zip(rels, refs):
        rows = src.shape[0]
        refs[-1][idx[rel], at : at + rows, :] = src[...]
        at = (at + rows) % refs[-1].shape[1]


def place_chunks(places, chunks, count):
    rels = [rel % count for rel in rel_order(count) for _ in chunks[rel]]
    pieces = [c for rel in rel_order(count) for c in chunks[rel]]
    shape = (count,) + pieces[0].shape
    return pl.pallas_call(
        functools.partial(place_body, rels),
        grid_spec=pltpu.PrefetchScalarGridSpec(
            num_scalar_prefetch=1,
            grid=(1,),
            in_specs=[pl.BlockSpec(c.shape, lambda i, idx: (0, 0)) for c in pieces],
            out_specs=pl.BlockSpec(shape, lambda i, idx: (0, 0, 0)),
        ),
        out_shape=jax.ShapeDtypeStruct(shape, BF16),
        compiler_params=params("arbitrary"),
        name="place_chunks",
    )(places, *pieces)


def tn_cols_body(n, idx, a, b, send, keep):
    j = pl.program_id(0)
    out = dot_tn(a[...], b[...]).astype(BF16)

    @pl.when(j < n)
    def _():
        send[...] = out

    @pl.when(j >= n)
    def _():
        keep[...] = out


def half_place(n):
    return lambda j, idx: jnp.where(j < n, idx[0] * n + j, idx[1] * n + j - n)


def tn_cols(a, b):
    k, m = a.shape
    cols = b.shape[1]
    n = 2
    w = cols // (2 * n)
    at = half_place(n)
    return pl.pallas_call(
        functools.partial(tn_cols_body, n),
        grid_spec=pltpu.PrefetchScalarGridSpec(
            num_scalar_prefetch=1,
            grid=(2 * n,),
            in_specs=[
                pl.BlockSpec((k, m), lambda j, idx: (0, 0)),
                pl.BlockSpec((k, w), lambda j, idx: (0, at(j, idx))),
            ],
            out_specs=[
                pl.BlockSpec((m, w), lambda j, idx: (0, jnp.minimum(j, n - 1))),
                pl.BlockSpec((m, w), lambda j, idx: (0, jnp.maximum(j - n, 0))),
            ],
        ),
        out_shape=[jax.ShapeDtypeStruct((m, cols // 2), BF16)] * 2,
        compiler_params=params("arbitrary"),
        cost_estimate=cost(
            flops=2 * k * m * cols, bytes_accessed=2 * (k * m + k * cols + m * cols), transcendentals=0
        ),
        name="tn_cols",
    )(dp_side(1), a, b)


def pick_body(idx, src, out):
    out[...] = src[...]


def pick_rows(places, src):
    n = places.shape[0]
    rows, cols = src.shape[0] // n, src.shape[1]
    return pl.pallas_call(
        pick_body,
        grid_spec=pltpu.PrefetchScalarGridSpec(
            num_scalar_prefetch=1,
            grid=(n,),
            in_specs=[pl.BlockSpec((rows, cols), lambda j, idx: (idx[j], 0))],
            out_specs=pl.BlockSpec((rows, cols), lambda j, idx: (j, 0)),
        ),
        out_shape=jax.ShapeDtypeStruct(src.shape, src.dtype),
        compiler_params=params("arbitrary"),
        cost_estimate=cost(flops=0, bytes_accessed=4 * src.size, transcendentals=0),
        name="pick_rows",
    )(places, src)


def tn_whole_body(a, b, out):
    out[...] = dot_tn(a[...], b[...]).astype(BF16)


def tn_whole(a, b):
    k, m = a.shape
    cols = b.shape[1]
    w = cols // 4
    return pl.pallas_call(
        tn_whole_body,
        grid=(4,),
        in_specs=[
            pl.BlockSpec((k, m), lambda j: (0, 0)),
            pl.BlockSpec((k, w), lambda j: (0, j)),
        ],
        out_specs=pl.BlockSpec((m, w), lambda j: (0, j)),
        out_shape=jax.ShapeDtypeStruct((m, cols), BF16),
        compiler_params=params("arbitrary"),
        cost_estimate=cost(
            flops=2 * k * m * cols, bytes_accessed=2 * (k * m + k * cols + m * cols), transcendentals=0
        ),
        name="tn_whole",
    )(a, b)


def tn_rows_body(n, idx, a, b, w, send, keep, sums):
    j = pl.program_id(0)
    out = dot_tn(a[...], b[...])
    sums[...] = jnp.sum(out * w[...].astype(F32), axis=1, keepdims=True)

    @pl.when(j < n)
    def _():
        send[...] = out.astype(BF16)

    @pl.when(j >= n)
    def _():
        keep[...] = out.astype(BF16)


def tn_rows(a, b, w):
    k, m = a.shape
    cols = b.shape[1]
    n = 2
    blk = m // (2 * n)
    at = half_place(n)
    return pl.pallas_call(
        functools.partial(tn_rows_body, n),
        grid_spec=pltpu.PrefetchScalarGridSpec(
            num_scalar_prefetch=1,
            grid=(2 * n,),
            in_specs=[
                pl.BlockSpec((k, blk), lambda j, idx: (0, at(j, idx))),
                pl.BlockSpec((k, cols), lambda j, idx: (0, 0)),
                pl.BlockSpec((blk, cols), lambda j, idx: (at(j, idx), 0)),
            ],
            out_specs=[
                pl.BlockSpec((blk, cols), lambda j, idx: (jnp.minimum(j, n - 1), 0)),
                pl.BlockSpec((blk, cols), lambda j, idx: (jnp.maximum(j - n, 0), 0)),
                pl.BlockSpec((blk, 1), lambda j, idx: (at(j, idx), 0)),
            ],
        ),
        out_shape=[jax.ShapeDtypeStruct((m // 2, cols), BF16)] * 2
        + [jax.ShapeDtypeStruct((m, 1), F32)],
        compiler_params=params("arbitrary"),
        cost_estimate=cost(
            flops=2 * k * m * cols, bytes_accessed=2 * (k * m + k * cols + m * cols), transcendentals=0
        ),
        name="tn_rows",
    )(dp_side(1), a, b, w)


def half_add_body(idx, keep, got, send_out, keep_out):
    j = pl.program_id(0)
    out = (keep[...].astype(F32) + got[...].astype(F32)).astype(BF16)

    @pl.when(j == 0)
    def _():
        send_out[...] = out

    @pl.when(j == 1)
    def _():
        keep_out[...] = out


def half_add(keep, got, axis, side):
    shape = list(keep.shape)
    shape[axis] //= 2
    place = lambda j, idx: (0, idx[j]) if axis == 1 else (idx[j], 0)
    one = pl.BlockSpec(tuple(shape), lambda j, idx: (0, 0))
    src = pl.BlockSpec(tuple(shape), place)
    return pl.pallas_call(
        half_add_body,
        grid_spec=pltpu.PrefetchScalarGridSpec(
            num_scalar_prefetch=1, grid=(2,), in_specs=[src, src], out_specs=[one, one]
        ),
        out_shape=[jax.ShapeDtypeStruct(tuple(shape), BF16)] * 2,
        compiler_params=params("arbitrary"),
        cost_estimate=cost(flops=keep.size, bytes_accessed=6 * keep.size, transcendentals=0),
        name="half_add",
    )(side, keep, got)


def plain_add_body(a, b, out):
    out[...] = (a[...].astype(F32) + b[...].astype(F32)).astype(BF16)


def plain_add(a, b):
    rows, cols = a.shape
    blk = pl.BlockSpec((rows // 2, cols), lambda j: (j, 0))
    return pl.pallas_call(
        plain_add_body,
        grid=(2,),
        in_specs=[blk, blk],
        out_specs=blk,
        out_shape=jax.ShapeDtypeStruct(a.shape, BF16),
        compiler_params=params("arbitrary"),
        cost_estimate=cost(flops=a.size, bytes_accessed=6 * a.size, transcendentals=0),
        name="plain_add",
    )(a, b)


def ring_add_body(first, near, f, b, f_out, b_out):
    rows = f_out.shape[0]
    at = 0 if first else rows
    ahead, behind = near[at : at + rows, :].astype(F32), near[rows - at : 2 * rows - at, :].astype(F32)
    n = f.shape[0]
    f_out[:n, :] = (ahead[:n] + f[...].astype(F32)).astype(BF16)
    b_out[rows - n :, :] = (behind[rows - n :] + b[...].astype(F32)).astype(BF16)
    if n < rows:
        f_out[n:, :] = ahead[n:].astype(BF16)
        b_out[: rows - n, :] = behind[: rows - n].astype(BF16)


def ring_add(near, f, b, first, rows, at):
    cols = near.shape[1]
    whole = lambda a: pl.BlockSpec(a.shape, lambda i: (0, 0))
    return pl.pallas_call(
        functools.partial(ring_add_body, first),
        grid=(1,),
        in_specs=[pl.BlockSpec((2 * rows, cols), lambda i: (at, 0)), whole(f), whole(b)],
        out_specs=[pl.BlockSpec((rows, cols), lambda i: (0, 0))] * 2,
        out_shape=[jax.ShapeDtypeStruct((rows, cols), BF16)] * 2,
        compiler_params=params("arbitrary"),
        cost_estimate=cost(flops=near.size, bytes_accessed=8 * near.size, transcendentals=0),
        name="ring_add",
    )(near, f, b)


def grad_x_body(idx, rows, w, out):
    out[...] = dot_nt(rows[...], w[...]).astype(out.dtype)


def grad_x_terms(places, rels, d_joint, w_joint, rows, kind):
    feats, cols = w_joint.shape
    step = rels[-1] - rels[0]
    return pl.pallas_call(
        grad_x_body,
        grid_spec=pltpu.PrefetchScalarGridSpec(
            num_scalar_prefetch=1,
            grid=(len(rels),),
            in_specs=[
                pl.BlockSpec((rows, cols), lambda j, idx: (idx[rels[0] + j * step], 0)),
                pl.BlockSpec((feats, cols), lambda j, idx: (0, 0)),
            ],
            out_specs=pl.BlockSpec((rows, feats), lambda j, idx: (j, 0)),
        ),
        out_shape=jax.ShapeDtypeStruct((len(rels) * rows, feats), kind),
        compiler_params=params("arbitrary"),
        cost_estimate=cost(
            flops=2 * rows * feats * cols * len(rels), bytes_accessed=2 * feats * cols, transcendentals=0
        ),
        name="grad_x_terms",
    )(places, d_joint, w_joint)


def input_grad_body(own, f, b, mid, x_ref, gain, out):
    grad = own[...] + f[...].astype(F32) + b[...].astype(F32)
    x = x_ref[...].astype(F32)
    inverse = lax.rsqrt(jnp.mean(x * x, axis=-1, keepdims=True) + EPS)
    unit = x * inverse
    scaled = grad * gain[...]
    inner = jnp.mean(scaled * unit, axis=-1, keepdims=True)
    out[...] = (mid[...] + inverse * (scaled - unit * inner)).astype(BF16)


def input_grad_of(own, f, b, mid, tokens, gain):
    rows, feats = tokens.shape
    blk = pl.BlockSpec((rows // 2, feats), lambda i: (i, 0))
    return pl.pallas_call(
        input_grad_body,
        grid=(2,),
        in_specs=[blk] * 5 + [pl.BlockSpec((1, feats), lambda i: (0, 0))],
        out_specs=blk,
        out_shape=jax.ShapeDtypeStruct((rows, feats), BF16),
        compiler_params=params("arbitrary"),
        cost_estimate=cost(flops=9 * rows * feats, bytes_accessed=14 * rows * feats, transcendentals=0),
        name="input_grad",
    )(own, f, b, mid, tokens, gain.reshape(1, -1))


def shard_sum_body(n_back, units, pad, value, *refs):
    out = refs[-1]
    total = value[:units, :].astype(F32)
    for back in refs[:n_back]:
        total = total + back[...].astype(F32)
    out[...] = total.astype(BF16)


def shard_sum(value, backs, units):
    whole = lambda a: pl.BlockSpec(a.shape, lambda i: (0, 0))
    return pl.pallas_call(
        functools.partial(shard_sum_body, len(backs), units, 0),
        grid=(1,),
        in_specs=[whole(a) for a in (value, *backs)],
        out_specs=pl.BlockSpec((units, value.shape[1]), lambda i: (0, 0)),
        out_shape=jax.ShapeDtypeStruct((units, value.shape[1]), BF16),
        compiler_params=params("arbitrary"),
        cost_estimate=cost(flops=value.size, bytes_accessed=4 * value.size, transcendentals=0),
        name="shard_sum",
    )(value, *backs)


def widen_body(src, *outs):
    at = 0
    for out in outs:
        out[...] = src[0, :, at : at + out.shape[1]].astype(F32)
        at += out.shape[1]


def widen_pieces_body(n, idx, *refs):
    p = pl.program_id(0)
    outs = refs[n:]
    for i, src in enumerate(refs[:n]):

        @pl.when(p == i)
        def _():
            at = 0
            for out in outs:
                out[...] = src[:, at : at + out.shape[1]].astype(F32)
                at += out.shape[1]


def widen_pieces(places, pieces, widths):
    n = len(pieces)
    rows, cols = pieces[0].shape
    return pl.pallas_call(
        functools.partial(widen_pieces_body, n),
        grid_spec=pltpu.PrefetchScalarGridSpec(
            num_scalar_prefetch=1,
            grid=(n,),
            in_specs=[pl.BlockSpec((rows, cols), lambda p, idx: (0, 0))] * n,
            out_specs=[pl.BlockSpec((rows, w), lambda p, idx: (idx[p], 0)) for w in widths],
        ),
        out_shape=[jax.ShapeDtypeStruct((n * rows, w), F32) for w in widths],
        compiler_params=params("arbitrary"),
        name="widen_pieces",
    )(places, *pieces)


def widen_cols(got):
    n_dp, rows, cols = got.shape
    return pl.pallas_call(
        widen_body,
        grid=(n_dp,),
        in_specs=[pl.BlockSpec((1, rows, cols), lambda p: (part_of(p, n_dp), 0, 0))],
        out_specs=[pl.BlockSpec((rows, cols), lambda p: (0, p))],
        out_shape=[jax.ShapeDtypeStruct((rows, n_dp * cols), F32)],
        compiler_params=params("arbitrary"),
        name="widen_cols",
    )(got)[0]


def parts_ready(p, srcs, parts, sems):
    copies = [pltpu.make_async_copy(w, parts.at[i], sems.at[i]) for i, w in enumerate(srcs)]

    @pl.when(p == 0)
    def _():
        for c in copies:
            c.start()

    for i, c in enumerate(copies):

        @pl.when(p == i)
        def _():
            c.wait()


def out_body(n_dp, idx, heads, x_ref, gain, *refs):
    srcs, (branch_out, mid_out, h_out, heads_out, parts, sems) = refs[:n_dp], refs[n_dp:]
    p = pl.program_id(0)
    n_t, rows, cols = heads.shape
    width = parts.shape[2]
    parts_ready(p, srcs, parts, sems)

    @pl.when(p == 0)
    def _():
        for t in range(n_t):
            heads_out[:, t * cols : (t + 1) * cols] = heads[t]

    part = pl.ds(pl.multiple_of(idx[p] * width, width), width)
    branch_out[:, part] = dot_nn(heads_out[...], parts[p])

    @pl.when(p == n_dp - 1)
    def _():
        mid = x_ref[...].astype(F32) + branch_out[...]
        mid_out[...] = mid
        inverse = lax.rsqrt(jnp.mean(mid * mid, axis=-1, keepdims=True) + EPS)
        h_out[...] = (mid * inverse * gain[...]).astype(BF16)


def out_project(heads, w_places, w_parts, tokens, gain):
    n_dp = len(w_parts)
    feats_in, width = w_parts[0].shape
    rows, feats = tokens.shape
    full = lambda shape: pl.BlockSpec(shape, lambda p, idx: (0,) * len(shape))
    sq = (rows, feats)
    return pl.pallas_call(
        functools.partial(out_body, n_dp),
        grid_spec=pltpu.PrefetchScalarGridSpec(
            num_scalar_prefetch=1,
            grid=(n_dp,),
            in_specs=[full(heads.shape), full(sq), full((1, feats))] + [ANY] * n_dp,
            out_specs=[full(sq)] * 4,
            scratch_shapes=[
                pltpu.VMEM((n_dp, feats_in, width), BF16),
                pltpu.SemaphoreType.DMA((n_dp,)),
            ],
        ),
        out_shape=[
            jax.ShapeDtypeStruct(sq, F32),
            jax.ShapeDtypeStruct(sq, F32),
            jax.ShapeDtypeStruct(sq, BF16),
            jax.ShapeDtypeStruct((rows, feats_in), BF16),
        ],
        compiler_params=params("arbitrary"),
        cost_estimate=cost(
            flops=2 * rows * feats * feats_in,
            bytes_accessed=2 * feats * feats_in + 16 * rows * feats,
            transcendentals=0,
        ),
        name="out_project",
    )(w_places, heads, tokens, gain.reshape(1, -1), *w_parts)


def out_back_body(n_dp, idx, own, f, b, mid_ref, dy, gain, *refs):
    srcs, (mid_out, low_out, gain_out, heads_out, acc, parts, sems) = refs[:n_dp], refs[n_dp:]
    p = pl.program_id(0)
    n_t, rows, cols = heads_out.shape
    width = parts.shape[2]
    parts_ready(p, srcs, parts, sems)

    @pl.when(p == 0)
    def _():
        grad = own[...] + f[...].astype(F32) + b[...].astype(F32)
        mid = mid_ref[...]
        inverse = lax.rsqrt(jnp.mean(mid * mid, axis=-1, keepdims=True) + EPS)
        unit = mid * inverse
        gain_out[...] = jnp.sum(grad * unit, axis=0, keepdims=True)
        scaled = grad * gain[...]
        inner = jnp.mean(scaled * unit, axis=-1, keepdims=True)
        total = dy[...].astype(F32) + inverse * (scaled - unit * inner)
        mid_out[...] = total
        low_out[...] = total.astype(BF16)
        acc[...] = jnp.zeros_like(acc)

    part = pl.ds(pl.multiple_of(idx[p] * width, width), width)
    acc[...] += dot_nt(low_out[:, part], parts[p])

    @pl.when(p == n_dp - 1)
    def _():
        for t in range(n_t):
            heads_out[t] = acc[:, t * cols : (t + 1) * cols].astype(BF16)


def out_back(own, f, b, mid, dy, gain, w_places, w_parts, n_t):
    n_dp = len(w_parts)
    feats_in, width = w_parts[0].shape
    rows, feats = mid.shape
    full = lambda shape: pl.BlockSpec(shape, lambda p, idx: (0,) * len(shape))
    sq = (rows, feats)
    heads = (n_t, rows, feats_in // n_t)
    return pl.pallas_call(
        functools.partial(out_back_body, n_dp),
        grid_spec=pltpu.PrefetchScalarGridSpec(
            num_scalar_prefetch=1,
            grid=(n_dp,),
            in_specs=[full(sq)] * 5 + [full((1, feats))] + [ANY] * n_dp,
            out_specs=[full(sq), full(sq), full((1, feats)), full(heads)],
            scratch_shapes=[
                pltpu.VMEM((rows, feats_in), F32),
                pltpu.VMEM((n_dp, feats_in, width), BF16),
                pltpu.SemaphoreType.DMA((n_dp,)),
            ],
        ),
        out_shape=[
            jax.ShapeDtypeStruct(sq, F32),
            jax.ShapeDtypeStruct(sq, BF16),
            jax.ShapeDtypeStruct((1, feats), F32),
            jax.ShapeDtypeStruct(heads, BF16),
        ],
        compiler_params=params("arbitrary"),
        cost_estimate=cost(
            flops=2 * rows * feats * feats_in,
            bytes_accessed=2 * feats * feats_in + 20 * rows * feats,
            transcendentals=0,
        ),
        name="out_back",
    )(w_places, own, f, b, mid, dy, gain.reshape(1, -1), *w_parts)


def ffn_body(n_in, n_w, first, units, n_buf, *refs):
    hs, refs = refs[:n_in], refs[n_in:]
    ys, refs = refs[:n_in], refs[n_in:]
    srcs, refs = refs[:n_w], refs[n_w:]
    if first:
        refs = refs[n_buf:]
        h_out, y_out, refs = refs[0], refs[1], refs[2:]
    else:
        dh_in, refs = refs[0], refs[1 + n_buf :]
    hid_out, gg_out, gu_out, dh_ref, weights, sems = refs[:6]
    waits = []
    for j in range(3):
        if first:
            waits.append([pltpu.make_async_copy(srcs[j], weights.at[j], sems.at[j])])
            continue
        src = srcs[j]
        n_dp, _, width = src.shape
        waits.append(
            [
                pltpu.make_async_copy(
                    src.at[p], weights.at[j, :, pl.ds(p * width, width)], sems.at[j]
                )
                for p in range(n_dp)
            ]
        )
    for group in waits:
        for c in group:
            c.start()

    def ready(j):
        for c in waits[j]:
            c.wait()
        return weights[j]

    if not first:
        h_out, y_out = refs[6:]
    at = 0
    for h, y in zip(hs, ys):
        h_out[at : at + h.shape[0], :] = h[...]
        y_out[at : at + h.shape[0], :] = y[...]
        at += h.shape[0]
    gate = dot_nt(h_out[...], ready(0))
    up = dot_nt(h_out[...], ready(1))
    gh = dot_nt(y_out[...], ready(2))
    sig = jax.nn.sigmoid(gate)
    act = gate * sig
    hid_out[:, :units] = (act * up).astype(BF16)
    gg = (gh * up * (sig + act * (1.0 - sig))).astype(BF16)
    gu = (gh * act).astype(BF16)
    gg_out[:, :units] = gg
    gu_out[:, :units] = gu
    pad = hid_out.shape[1] - units
    if pad > 0:
        for o in (hid_out, gg_out, gu_out):
            o[:, units:] = jnp.zeros((o.shape[0], pad), BF16)
    part = dot_nn(gg, weights[0]) + dot_nn(gu, weights[1])
    if not first:
        part = part + dh_in[...]
    dh_ref[...] = part


def ffn_set(hs, ys, srcs, units, shard, shards, total, place, dh, bufs):
    n_in, n_w, first = len(hs), len(srcs), shard == 0
    feats = hs[0].shape[1]
    m = sum(h.shape[0] for h in hs)
    pad = -(-units // 128) * 128
    whole = lambda a: pl.BlockSpec(a.shape, lambda i: (0, 0))
    args = list(hs) + list(ys) + list(srcs)
    in_specs = [whole(a) for a in args[: 2 * n_in]] + [ANY] * n_w
    if not first:
        args.append(dh)
        in_specs.append(whole(dh))
    out_specs = [pl.BlockSpec((m, pad), lambda i: (place, shard))] * 3
    out_shape = [jax.ShapeDtypeStruct((total, pad * shards), BF16)] * 3
    held = list(bufs[2:])
    if first:
        out_specs = [pl.BlockSpec((m, feats), lambda i: (place, 0))] * 2 + out_specs
        out_shape = [jax.ShapeDtypeStruct((total, feats), BF16)] * 2 + out_shape
        held = list(bufs)
    aliases = {len(args) + i: i for i in range(len(held))}
    args += held
    in_specs += [ANY] * len(held)
    scratch = [pltpu.VMEM((3, units, feats), BF16), pltpu.SemaphoreType.DMA((3,))]
    if not first:
        scratch += [pltpu.VMEM((m, feats), BF16)] * 2
    out = pl.pallas_call(
        functools.partial(ffn_body, n_in, n_w, first, units, len(held)),
        grid=(1,),
        in_specs=in_specs,
        out_specs=out_specs + [pl.BlockSpec((m, feats), lambda i: (0, 0))],
        out_shape=out_shape + [jax.ShapeDtypeStruct((m, feats), F32)],
        scratch_shapes=scratch,
        input_output_aliases=aliases,
        compiler_params=params("arbitrary"),
        cost_estimate=cost(
            flops=10 * m * feats * units,
            bytes_accessed=6 * feats * units + 16 * m * feats,
            transcendentals=m * units,
        ),
        name="ffn_set",
    )(*args)
    new, dh = list(out[:-1]), out[-1]
    return (new if first else list(bufs[:2]) + new), dh


def down_body(n_got, units, hid, own, *refs):
    got, (out, weights, sems) = refs[:n_got], refs[n_got:]
    waits = [[pltpu.make_async_copy(own, weights.at[0], sems.at[0])]]
    for s, src in enumerate(got):
        n_dp, _, width = src.shape
        waits.append(
            [
                pltpu.make_async_copy(
                    src.at[p], weights.at[s + 1, :, pl.ds(p * width, width)], sems.at[s + 1]
                )
                for p in range(n_dp)
            ]
        )
    for group in waits:
        for c in group:
            c.start()
    pad = hid.shape[1] // (n_got + 1)
    total = None
    for s, group in enumerate(waits):
        for c in group:
            c.wait()
        part = dot_nn(hid[:, s * pad : s * pad + units], weights[s])
        total = part if total is None else total + part
    out[...] = total.astype(BF16)


def down_rows(hid, own, got):
    m = hid.shape[0]
    units, feats = own.shape
    n_w = len(got) + 1
    return pl.pallas_call(
        functools.partial(down_body, len(got), units),
        grid=(1,),
        in_specs=[pl.BlockSpec(hid.shape, lambda i: (0, 0))] + [ANY] * n_w,
        out_specs=pl.BlockSpec((m, feats), lambda i: (0, 0)),
        out_shape=jax.ShapeDtypeStruct((m, feats), BF16),
        scratch_shapes=[
            pltpu.VMEM((n_w, units, feats), BF16),
            pltpu.SemaphoreType.DMA((n_w,)),
        ],
        compiler_params=params("arbitrary"),
        cost_estimate=cost(
            flops=2 * m * units * feats * n_w,
            bytes_accessed=2 * units * feats * n_w + 6 * m * feats,
            transcendentals=0,
        ),
        name="down_rows",
    )(hid, own, *got)


LOG2E = 1.4426950408889634
SCALE = HEAD_DIM ** (-0.5)


def attend_body(q_ref, k0, k1, v0, v1, lo_ref, *rest):
    o_ref, ks, vs = rest[-3:]
    i = pl.program_id(1)
    span = Q_BLK + WINDOW

    @pl.when(i == 0)
    def _():
        ks[:WINDOW] = k0[...]
        ks[WINDOW:] = k1[...]
        vs[:WINDOW] = v0[...]
        vs[WINDOW:] = v1[...]

    start = pl.multiple_of(i * Q_BLK, Q_BLK)
    kb = ks[pl.ds(start, span), :]
    vb = vs[pl.ds(start, span), :]
    s = dot_nt(q_ref[...], kb) * (SCALE * LOG2E)
    col = lax.broadcasted_iota(jnp.int32, s.shape, 1)
    row = lax.broadcasted_iota(jnp.int32, s.shape, 0)
    lo = lo_ref[...] - start
    s = jnp.where((col >= lo) & (col <= row + WINDOW), s, NEG)
    p = jnp.exp2(s - jnp.max(s, axis=1, keepdims=True))
    total = jnp.sum(p, axis=1, keepdims=True)
    o = dot_nn(p.astype(BF16), vb) * (1.0 / total)
    o_ref[...] = o.astype(BF16)


def attend(half, q, pair, lo, buf):
    total, cols = q.shape
    heads = cols // HEAD_DIM
    rows = total // 2
    blocks = rows // Q_BLK
    base = half * blocks
    q_spec = pl.BlockSpec((Q_BLK, HEAD_DIM), lambda h, i: (base + i, h))
    key_spec = lambda b, c: pl.BlockSpec((WINDOW, HEAD_DIM), lambda h, i: (b, c + h))
    lo_spec = pl.BlockSpec((Q_BLK, 1), lambda h, i: (base + i, 0))
    in_specs = [
        q_spec,
        key_spec(pair[0][1], 0),
        key_spec(pair[1][1], 0),
        key_spec(pair[0][1], heads),
        key_spec(pair[1][1], heads),
        lo_spec,
    ]
    args = [q, pair[0][0], pair[1][0], pair[0][0], pair[1][0], lo]
    aliases = {}
    if buf is not None:
        in_specs.append(pl.BlockSpec(memory_space=pl.ANY))
        args.append(buf)
        aliases = {6: 0}
    return pl.pallas_call(
        attend_body,
        grid=(heads, blocks),
        in_specs=in_specs,
        out_specs=q_spec,
        out_shape=jax.ShapeDtypeStruct((total, cols), BF16),
        scratch_shapes=[pltpu.VMEM((2 * WINDOW, HEAD_DIM), BF16)] * 2,
        input_output_aliases=aliases,
        compiler_params=params("arbitrary", "arbitrary"),
        cost_estimate=cost(
            flops=4 * rows * (Q_BLK + WINDOW) * cols,
            bytes_accessed=2 * cols * 6 * WINDOW,
            transcendentals=rows * (Q_BLK + WINDOW) * heads,
        ),
        name="attend",
    )(*args)


def attend_back_body(q_ref, g_ref, k0, k1, v0, v1, lo_ref, cos_ref, sin_ref, *rest):
    dq_ref, dk_ref, dv_ref, ks, vs = rest[-5:]
    i = pl.program_id(1)
    span = Q_BLK + WINDOW

    @pl.when(i == 0)
    def _():
        ks[:WINDOW] = k0[...]
        ks[WINDOW:] = k1[...]
        vs[:WINDOW] = v0[...]
        vs[WINDOW:] = v1[...]
        dk_ref[...] = jnp.zeros_like(dk_ref)
        dv_ref[...] = jnp.zeros_like(dv_ref)

    start = pl.multiple_of(i * Q_BLK, Q_BLK)
    kb = ks[pl.ds(start, span), :]
    vb = vs[pl.ds(start, span), :]
    q, g = q_ref[...], g_ref[...]
    s = dot_nt(kb, q) * (SCALE * LOG2E)
    key = lax.broadcasted_iota(jnp.int32, s.shape, 0)
    row = lax.broadcasted_iota(jnp.int32, s.shape, 1)
    lo = lo_ref[...] - start
    s = jnp.where((key >= lo) & (key <= row + WINDOW), s, NEG)
    p = jnp.exp2(s - jnp.max(s, axis=0, keepdims=True))
    p = p * (1.0 / jnp.sum(p, axis=0, keepdims=True))
    dp = dot_nt(vb, g)
    inner = jnp.sum(p * dp, axis=0, keepdims=True)
    ds = (p * (dp - inner)).astype(BF16)
    dq = dot_tn(ds, kb) * SCALE
    dq = dq * cos_ref[...] - pltpu.roll(dq, HEAD_DIM // 2, 1) * sin_ref[...]
    dq_ref[...] = dq.astype(BF16)
    dk_ref[pl.ds(start, span), :] += dot_nn(ds, q) * SCALE
    dv_ref[pl.ds(start, span), :] += dot_nn(p.astype(BF16), g)


def attend_back(half, q, g, pair, lo_row, cos, sin, buf):
    total, cols = q.shape
    heads = cols // HEAD_DIM
    rows = total // 2
    blocks = rows // Q_BLK
    base = half * blocks
    q_spec = pl.BlockSpec((Q_BLK, HEAD_DIM), lambda h, i: (base + i, h))
    key_spec = lambda b, c: pl.BlockSpec((WINDOW, HEAD_DIM), lambda h, i: (b, c + h))
    rope_spec = pl.BlockSpec((Q_BLK, HEAD_DIM), lambda h, i: (base + i, 0))
    lo_spec = pl.BlockSpec((1, Q_BLK), lambda h, i: (0, base + i))
    grad_spec = pl.BlockSpec((2 * WINDOW, HEAD_DIM), lambda h, i: (0, h))
    in_specs = [
        q_spec,
        q_spec,
        key_spec(pair[0][1], 0),
        key_spec(pair[1][1], 0),
        key_spec(pair[0][1], heads),
        key_spec(pair[1][1], heads),
        lo_spec,
        rope_spec,
        rope_spec,
    ]
    args = [q, g, pair[0][0], pair[1][0], pair[0][0], pair[1][0], lo_row, cos, sin]
    aliases = {}
    if buf is not None:
        in_specs.append(pl.BlockSpec(memory_space=pl.ANY))
        args.append(buf)
        aliases = {9: 0}
    return pl.pallas_call(
        attend_back_body,
        grid=(heads, blocks),
        in_specs=in_specs,
        out_specs=[
            pl.BlockSpec((Q_BLK, HEAD_DIM), lambda h, i: (base + i, 2 * heads + h)),
            grad_spec,
            grad_spec,
        ],
        out_shape=[
            jax.ShapeDtypeStruct((total, 3 * cols), BF16),
            jax.ShapeDtypeStruct((2 * WINDOW, cols), F32),
            jax.ShapeDtypeStruct((2 * WINDOW, cols), F32),
        ],
        scratch_shapes=[pltpu.VMEM((2 * WINDOW, HEAD_DIM), BF16)] * 2,
        input_output_aliases=aliases,
        compiler_params=params("arbitrary", "arbitrary"),
        cost_estimate=cost(
            flops=10 * rows * (Q_BLK + WINDOW) * cols,
            bytes_accessed=2 * cols * 14 * WINDOW,
            transcendentals=rows * (Q_BLK + WINDOW) * heads,
        ),
        name="attend_back",
    )(*args)


def finish_body(half, ak, av, ok, ov, cos_ref, sin_ref, _, out_ref):
    cols = ak.shape[1]

    def write(gk, gv):
        for h in range(cols // HEAD_DIM):
            c = slice(h * HEAD_DIM, (h + 1) * HEAD_DIM)
            seg = gk[:, c]
            seg = seg * cos_ref[...] - pltpu.roll(seg, HEAD_DIM // 2, 1) * sin_ref[...]
            out_ref[:, c] = seg.astype(BF16)
        out_ref[:, cols:] = gv.astype(BF16)

    write(ak[...] + ok[...].astype(F32), av[...] + ov[...].astype(F32))


def finish_keys(half, ak, av, other_k, other_v, cos, sin, buf):
    cols = ak.shape[1]
    blk = 512
    n = WINDOW // blk
    base = half * n
    own = pl.BlockSpec((blk, cols), lambda i: (base + i, 0))
    oth = lambda o: pl.BlockSpec((blk, cols), lambda i: (o[1] * n + i, o[2]))
    rope = pl.BlockSpec((blk, HEAD_DIM), lambda i: (base + i, 0))
    return pl.pallas_call(
        functools.partial(finish_body, half),
        grid=(n,),
        in_specs=[own, own, oth(other_k), oth(other_v), rope, rope, ANY],
        out_specs=pl.BlockSpec((blk, 2 * cols), lambda i: (base + i, 0)),
        out_shape=jax.ShapeDtypeStruct(buf.shape, BF16),
        input_output_aliases={6: 0},
        compiler_params=params("arbitrary"),
        name="finish_keys",
    )(ak, av, other_k[0], other_v[0], cos, sin, buf)


def shards(
    tokens, segments, attn_gain, ffn_gain, w_query, w_key, w_value, w_out, w_gate, w_up, w_down, cotangent
):
    rows, feats = tokens.shape
    n_tensor = lax.axis_size("tensor")
    n_dp = lax.axis_size("dp")
    block_len = rows * n_tensor
    head_cols = w_query.shape[1]
    units = w_gate.shape[1]
    unit_pad = -(-units // 128) * 128
    dp_idx, t_idx = lax.axis_index("dp"), lax.axis_index("tensor")
    first_pos = dp_idx * block_len
    ring = [ring_cycle(n_tensor)]
    square = group_cycles(n_tensor)
    groups = n_tensor // GROUP
    far = n_tensor // 2
    part_cols = feats // n_dp
    own_w = (w_gate.T, w_up.T, w_down)

    def to_group(piece, s):
        pairs = [(t, (t + s * GROUP) % n_tensor) for t in range(n_tensor)]
        return lax.ppermute(piece, "tensor", pairs)

    def dp_cols(value):
        return lax.dynamic_slice_in_dim(value, dp_idx * part_cols, part_cols, 1)

    ring_owners = owners(ring)
    ring_pairs = owners(ring, [r for k in range(far - 1, 0, -1) for r in (k, -k)] + [far, 0])
    x_f = tokens.astype(F32)
    x_normed, x_unit, x_inv = norm_forward(x_f, attn_gain)
    x_low = x_normed.astype(BF16)
    go = Gather(dp_cols(w_out), ring)
    w_joint = jnp.concatenate([w_key, w_value, w_query], axis=1)
    gx = Gather(x_low, ring)
    gx.step()
    go.step(x_low)
    cos, sin = rope_tables(first_pos + jnp.arange(block_len, dtype=jnp.int32))
    cos, sin = after(cos, w_joint, x_low), after(sin, w_joint)

    def qkv(rel, bufs):
        return qkv_chunk(
            ring_owners, rel % n_tensor, gx.chunks[rel], w_query, w_key, w_value, cos, sin, bufs
        )

    bufs = qkv(0, None)
    for k in range(1, far + 1):
        gx.f, gx.b, go.f, go.b, bufs = together(gx.f, gx.b, go.f, go.b, tuple(bufs))
        if k == far:
            break
        if k == 1:
            seg_tail = after(segments[block_len - WINDOW :].astype(F32), gx.f, gx.b)
            prev_seg = shifted(seg_tail, "dp", 1).astype(jnp.int32)
        gx.step()
        go.step()
        bufs = qkv(k, qkv(-k, bufs))
    w_out_part = place_chunks(after(ring_owners, go.f, go.b), go.chunks, n_tensor)
    w_out_part = w_out_part.reshape(n_tensor * head_cols, part_cols)
    low_bits = bits_of(n_dp)
    w_spread = spread_parts([(0, w_out_part)], low_bits[-1:])

    seg_all = jnp.concatenate([prev_seg, segments], axis=0)
    low_key = jnp.sum((seg_all[None, :] < segments[:, None]).astype(jnp.int32), axis=1)
    low_key = jnp.where(dp_idx == 0, jnp.maximum(low_key, WINDOW), low_key)
    spot = jnp.arange(block_len, dtype=jnp.int32)
    low_key = jnp.maximum(low_key, spot + 1)
    low_key = low_key - jnp.where(spot >= block_len // 2, block_len // 2, 0)
    low_col, low_row = low_key[:, None], low_key[None, :]

    came = (gx.f, gx.b)
    mine, low_col, low_row = together(tuple(dp_cols(w) for w in own_w), low_col, low_row)
    first = after(mine[0], *came)
    gate_got = [to_group(first, s) for s in range(1, groups)]
    bufs = list(bufs)
    bufs[0] = after(bufs[0], low_col, low_row, first, w_out_part)
    bufs = qkv(far, bufs)
    query, key_value, x_all = bufs
    tail_kv = after(key_value[block_len - WINDOW :])
    prev = shifted(tail_kv, "dp", 1)
    gy = Gather(after(cotangent, *came), square)
    gy.step()

    late = ((key_value, 0), (key_value, 1))
    heads_late = attend(1, query, late, low_col, None)
    heads_late, prev, gy.f, gy.b = together(heads_late, prev, gy.f, gy.b)
    early = ((prev, 0), (key_value, 0))
    heads_low = attend(0, query, early, low_col, heads_late)
    heads_low = heads_low.reshape(n_tensor, rows, head_cols)
    w_first = w_spread[-1][1]
    heads_low, w_first, *gate_got = together(heads_low, w_first, *gate_got)
    w_spread[-1] = (w_spread[-1][0], w_first)

    heads_got = lax.all_to_all(heads_low, "tensor", split_axis=0, concat_axis=0, tiled=True)
    w_spread = spread_parts(w_spread, low_bits[:-1], heads_low)
    w_places = jnp.stack([dp_idx ^ x for x, _ in w_spread]).astype(jnp.int32)
    heads_got, *w_out_parts = together(heads_got, *[w for _, w in w_spread])
    second = after(mine[1], heads_got)
    up_got = [to_group(second, s) for s in range(1, groups)]
    gate_all_got = [all_dp(after(g, heads_low)) for g in gate_got]
    gy.step(heads_got)
    y_chunks = gy.chunks
    attn_branch, mid, h_low, my_heads = out_project(
        heads_got, w_places, w_out_parts, tokens, ffn_gain
    )

    gh = Gather(h_low, square)
    sets = {0: ([0], 2), 1: ([-1, 1], 0), 2: ([2], 3)}
    ffn_bufs, dhs = [], {}

    def ffn(i, shard, *deps):
        rels, place = sets[i]
        hs = [c for r in rels for c in gh.chunks[r]]
        ys = [c for r in rels for c in y_chunks[r]]
        srcs = own_w if shard == 0 else got[shard - 1]
        hs[0] = after(hs[0], *deps)
        return ffn_set(
            hs, ys, srcs, units, shard, groups, GROUP * rows, place, dhs.get(i), ffn_bufs
        )

    gh.step()
    ffn_bufs, dhs[0] = ffn(0, 0)
    third = after(mine[2], h_low, *up_got)
    down_got = [to_group(third, s) for s in range(1, groups)]
    came = (*gh.chunks[1], *gh.chunks[-1], *gate_all_got)
    up_all_got = [all_dp(after(g, dhs[0], *came)) for g in up_got]
    gh.step(dhs[0])
    ffn_bufs, dhs[1] = ffn(1, 0)
    came = (*gh.chunks[2], *y_chunks[2], *up_all_got)
    down_all_got = [all_dp(after(d, dhs[1], *came)) for d in down_got]
    got = list(zip(gate_all_got, up_all_got, down_all_got))
    ffn_bufs, dhs[2] = ffn(2, 0)
    for s in range(1, groups):
        ffn_bufs, dhs[2] = ffn(2, s)
    sh = Scatter(dhs[2].astype(BF16), square)
    for s in range(1, groups):
        ffn_bufs, dhs[1] = ffn(1, s, *sh.sent)
    sh.step(dhs[1], False)
    for s in range(1, groups):
        ffn_bufs, dhs[0] = ffn(0, s, *sh.sent)
    h_all, y_all, hid_all, gate_all, up_all = ffn_bufs

    def send_back(red, *deps):
        cut = lambda s: red.value[s * unit_pad : s * unit_pad + units]
        return [to_group(after(cut(s), *deps), groups - s) for s in range(1, groups)]

    red_down = Halves(*tn_cols(hid_all, y_all), 1)
    red_down.send()
    red_gate = Halves(*tn_cols(after(gate_all, red_down.sent), h_all), 1)
    sh.f, sh.b, dhs[0], red_down.got, red_gate.sent = together(
        sh.f, sh.b, dhs[0], red_down.got, red_gate.sent
    )
    grad_mid, grad_mid_low, grad_ffn_gain, my_grad_heads = out_back(
        dhs[0], sh.f, sh.b, mid, cotangent, ffn_gain, w_places, w_out_parts, n_tensor
    )
    grad_heads = lax.all_to_all(
        my_grad_heads, "tensor", split_axis=0, concat_axis=0, tiled=True
    ).reshape(block_len, head_cols)

    red_down.add()
    red_down.send(my_grad_heads)
    red_gate.send(red_down.sent)
    sf_all = down_rows(after(hid_all, red_down.sent), own_w[2], [g[2] for g in got])
    red_up = Halves(*tn_cols(after(up_all, red_down.sent), h_all), 1)
    out_local = tn_whole(my_heads, after(grad_mid_low, red_down.sent))
    grad_heads, red_down.got, red_gate.got, sf_all, red_up.sent, out_local = together(
        grad_heads, red_down.got, red_gate.got, sf_all, red_up.sent, out_local
    )
    red_down.finish()
    down_back = send_back(red_down)
    red_gate.add()
    red_gate.send()
    red_up.send()
    sf = Scatter(sf_all[3 * rows :], square)

    grad_heads = after(grad_heads, red_down.value, *sf.sent, red_gate.sent)
    d_joint, bk, bv = attend_back(0, query, grad_heads, early, low_row, cos, sin, None)
    d_joint, bk, bv, sf.f, sf.b, red_up.got, red_gate.got, *down_back = together(
        d_joint, bk, bv, sf.f, sf.b, red_up.got, red_gate.got, *down_back
    )
    red_gate.finish()
    gate_back = send_back(red_gate)
    back = after(jnp.concatenate([bk[:WINDOW], bv[:WINDOW]], axis=1).astype(BF16))
    got_back = shifted(back, "dp", -1)
    sf.step(after(sf_all, back), False)
    red_up.add()
    red_up.send(back)
    d_joint, ak, av = attend_back(
        1, query, after(grad_heads, back, *sf.sent, red_up.sent, red_gate.value),
        late, low_row, cos, sin, d_joint,
    )
    d_joint, ak, av, got_back, sf.f, sf.b, red_up.got, *gate_back = together(
        d_joint, ak, av, got_back, sf.f, sf.b, red_up.got, *gate_back
    )
    out_dp = lax.psum_scatter(after(out_local, ak), "dp", scatter_dimension=1, tiled=True)
    d_joint = finish_keys(0, ak, av, (bk, 1, 0), (bv, 1, 0), cos, sin, d_joint)
    d_joint = finish_keys(1, ak, av, (got_back, 0, 0), (got_back, 0, 1), cos, sin, d_joint)

    def terms(rels, kind, *deps):
        rels = [r % n_tensor for r in rels]
        return grad_x_terms(after(ring_owners, *deps), rels, d_joint, w_joint, rows, kind)

    red_up.finish(ak)
    up_back = send_back(red_up)
    sx = Scatter(after(terms([far], BF16), red_up.value), ring)
    near = terms([far - 1, 1 - far], F32, red_up.value)
    down_own = shard_sum(after(red_down.value, red_up.value), down_back, units)
    down_dp = all_dp(down_own)
    gate_own = shard_sum(after(red_gate.value, down_own), gate_back, units)
    gate_dp = all_dp(gate_own)
    joint = tn_rows(after(x_all, *sx.sent), d_joint, w_joint)
    grad_attn_gain = joint[2][:, 0] / attn_gain
    ffn_branch = after(sf_all[2 * rows : 3 * rows], *sx.sent).astype(F32)
    ffn_branch = ffn_branch + sf.f.astype(F32) + sf.b.astype(F32)
    result = mid + ffn_branch
    slots = 2 * n_dp + 1
    own_seg = lax.dynamic_slice_in_dim(segments, t_idx * rows, rows)
    one_hot = (own_seg[:, None] == jnp.arange(slots, dtype=jnp.int32)[None, :]).astype(F32)
    per_row = jnp.stack(
        [
            jnp.sum(result * result, axis=1),
            jnp.sum(attn_branch * attn_branch, axis=1),
            jnp.sum(ffn_branch * ffn_branch, axis=1),
            jnp.ones((rows,), F32),
        ],
        axis=1,
    )
    table = jnp.dot(per_row.T, one_hot, precision=lax.Precision.HIGHEST, preferred_element_type=F32)
    packed = jnp.concatenate([grad_attn_gain, grad_ffn_gain[0], table.reshape(-1)])
    packed = jnp.pad(packed, (0, -packed.shape[0] % 1024)).reshape(-1, 128)
    sx.f, sx.b, near, down_own, gate_own, joint, packed, out_dp, *up_back = together(
        sx.f, sx.b, near, down_own, gate_own, tuple(joint), packed, out_dp, *up_back
    )
    red_joint = Halves(*joint[:2], 0)
    red_joint.send()
    far_out = lax.dynamic_slice_in_dim(out_dp, ring_owners[far] * head_cols, head_cols)
    so = Scatter(far_out, ring)
    todo = hops()
    hop = swap(after(packed, red_joint.got), *todo[0])
    sx.step(near, True)
    up_own = shard_sum(after(red_up.value, *sx.sent), up_back, units)
    up_dp = all_dp(up_own)
    near = terms([far - 2, 2 - far], F32, up_own)
    picked = pick_rows(after(ring_pairs, near), out_dp)
    sx.f, sx.b, near, red_joint.got, up_own, picked, hop, so.f, so.b = together(
        sx.f, sx.b, near, red_joint.got, up_own, picked, hop, so.f, so.b
    )
    packed = packed + hop
    so.step(picked, True, at=0)
    red_joint.add()
    red_joint.send()
    sx.step(near, True, red_joint.sent)
    near = terms([far - 3, 3 - far], F32, *sx.sent)
    grad_w_down = widen_cols(after(down_dp, near))
    sx.f, sx.b, near, red_joint.got, grad_w_down, so.f, so.b = together(
        sx.f, sx.b, near, red_joint.got, grad_w_down, so.f, so.b
    )
    so.step(picked, True, at=1)
    sx.step(near, True)
    for k in range(far - 4, 0, -1):
        sx.step(terms([k, -k], F32, *sx.sent), True)
    red_joint.finish()
    joint_parts = spread_parts([(0, red_joint.value)], low_bits[-1:])
    grad_w_gate = widen_cols(after(gate_dp, red_joint.value)).T
    own = terms([0], F32, grad_w_gate)
    sx.f, sx.b, own, so.f, so.b, joint_first = together(
        sx.f, sx.b, own, so.f, so.b, joint_parts[-1][1]
    )
    joint_parts[-1] = (joint_parts[-1][0], joint_first)
    joint_parts = spread_parts(joint_parts, low_bits[:-1][::-1])
    joint_places = jnp.stack([place_of(dp_idx ^ x, n_dp) for x, _ in joint_parts])
    for i in range(2, far - 1):
        so.step(picked, True, at=i)
    for axis, bit in todo[1:]:
        packed = packed + swap(after(packed, sx.f, sx.b), axis, bit)
    out_own = picked[-head_cols:].astype(F32) + so.f.astype(F32) + so.b.astype(F32)
    out_all = all_dp(out_own.astype(BF16))
    input_grad = input_grad_of(own, sx.f, sx.b, grad_mid, tokens, attn_gain)
    grad_w_out = jnp.concatenate(list(out_all), axis=1).astype(F32)
    grad_w_key, grad_w_value, grad_w_query = widen_pieces(
        joint_places.astype(jnp.int32), [v for _, v in joint_parts], [head_cols] * 3
    )
    grad_w_up = widen_cols(up_dp).T

    packed = packed.reshape(-1)
    sums = packed[2 * feats : 2 * feats + 4 * slots].reshape(4, slots)
    doc_rms = jnp.sqrt(sums[:3] / (jnp.maximum(sums[3:], 1.0) * feats))

    return (
        result.astype(BF16),
        input_grad,
        packed[:feats],
        packed[feats : 2 * feats],
        grad_w_query,
        grad_w_key,
        grad_w_value,
        grad_w_out,
        grad_w_gate,
        grad_w_up,
        grad_w_down,
        doc_rms,
    )


def solution(mesh):
    both = P(("dp", "tensor"), None)
    col, row = P(None, "tensor"), P("tensor", None)
    return jax.shard_map(
        shards,
        mesh=mesh,
        in_specs=(both, P("dp"), P(), P(), col, col, col, row, col, col, row, both),
        out_specs=(both, both, P(), P(), col, col, col, row, col, col, row, P()),
        check_vma=False,
    )
```
